32 devices in a mesh: dp: 16 (over z, y, x), section: 2 (over core).
Axes of the slice: x: 2, y: 2, z: 4, core: 2. Of those that a mesh axis runs over, the one named last changes fastest.
Arguments:
- images: float32 [64, 256, 48], P('dp'), may hold values from -1 to 1
- noise_draw: float32 [64, 256, 48], P('dp'), may hold values from -6 to 6
- labels: int32 [64], P('dp'), may hold values from 0 to 999
- class_drop: int32 [64], P('dp'), may hold values 0 or 1
- w_qkv: float32 [2, 768, 2304], P('section', 'dp'), may hold values from -0.21875 to 0.21875
- w_attn: float32 [2, 768, 768], P('section', 'dp'), may hold values from -0.625 to 0.625
- w_up: float32 [2, 768, 3072], P('section', 'dp'), may hold values from -0.21875 to 0.21875
- w_down: float32 [2, 3072, 768], P('section', 'dp'), may hold values from -0.109375 to 0.109375
- w_in: float32 [2, 48, 768], P('section', None, 'dp'), may hold values from -0.875 to 0.875
- w_head: float32 [2, 768, 96], P('section', 'dp'), may hold values from -0.109375 to 0.109375
- w_embed: float32 [2, 1256, 768], P('section', None, 'dp'), may hold values from -3 to 3
- w_norms: float32 [2, 6, 768], P('section', None, 'dp'), may hold values from -1.2 to 1.8
- moment_qkv: float32 [2, 768, 2304], P('section', 'dp'), may hold values from -1.4901161e-07 to 1.4901161e-07
- moment_attn: float32 [2, 768, 768], P('section', 'dp'), may hold values from -1.4901161e-07 to 1.4901161e-07
- moment_up: float32 [2, 768, 3072], P('section', 'dp'), may hold values from -1.4901161e-07 to 1.4901161e-07
- moment_down: float32 [2, 3072, 768], P('section', 'dp'), may hold values from -1.4901161e-07 to 1.4901161e-07
- moment_in: float32 [2, 48, 768], P('section', None, 'dp'), may hold values from -1.4901161e-07 to 1.4901161e-07
- moment_head: float32 [2, 768, 96], P('section', 'dp'), may hold values from -1.4901161e-07 to 1.4901161e-07
- moment_embed: float32 [2, 1256, 768], P('section', None, 'dp'), may hold values from -1e-06 to 1e-06
- moment_norms: float32 [2, 6, 768], P('section', None, 'dp'), may hold values from -1.4901161e-07 to 1.4901161e-07
- square_qkv: float32 [2, 768, 2304], P('section', 'dp'), may hold values from 3.2e-15 to 1.3e-14
- square_attn: float32 [2, 768, 768], P('section', 'dp'), may hold values from 3.2e-15 to 1.3e-14
- square_up: float32 [2, 768, 3072], P('section', 'dp'), may hold values from 3.2e-15 to 1.3e-14
- square_down: float32 [2, 3072, 768], P('section', 'dp'), may hold values from 3.2e-15 to 1.3e-14
- square_in: float32 [2, 48, 768], P('section', None, 'dp'), may hold values from 3.2e-15 to 1.3e-14
- square_head: float32 [2, 768, 96], P('section', 'dp'), may hold values from 3.2e-15 to 1.3e-14
- square_embed: float32 [2, 1256, 768], P('section', None, 'dp'), may hold values from 0 to 1e-13
- square_norms: float32 [2, 6, 768], P('section', None, 'dp'), may hold values from 3.2e-15 to 1.3e-14
Outputs:
- new_moment_qkv: float32 [2, 768, 2304], P('section', 'dp')
- new_moment_attn: float32 [2, 768, 768], P('section', 'dp')
- new_moment_up: float32 [2, 768, 3072], P('section', 'dp')
- new_moment_down: float32 [2, 3072, 768], P('section', 'dp')
- new_moment_in: float32 [2, 48, 768], P('section', None, 'dp')
- new_moment_head: float32 [2, 768, 96], P('section', 'dp')
- new_moment_embed: float32 [2, 1256, 768], P('section', None, 'dp')
- new_moment_norms: float32 [2, 6, 768], P('section', None, 'dp')
- new_square_qkv: float32 [2, 768, 2304], P('section', 'dp')
- new_square_attn: float32 [2, 768, 768], P('section', 'dp')
- new_square_up: float32 [2, 768, 3072], P('section', 'dp')
- new_square_down: float32 [2, 3072, 768], P('section', 'dp')
- new_square_in: float32 [2, 48, 768], P('section', None, 'dp')
- new_square_head: float32 [2, 768, 96], P('section', 'dp')
- new_square_embed: float32 [2, 1256, 768], P('section', None, 'dp')
- new_square_norms: float32 [2, 6, 768], P('section', None, 'dp')
- new_qkv: float32 [2, 768, 2304], P('section', 'dp')
- new_attn: float32 [2, 768, 768], P('section', 'dp')
- new_up: float32 [2, 768, 3072], P('section', 'dp')
- new_down: float32 [2, 3072, 768], P('section', 'dp')
- new_in: float32 [2, 48, 768], P('section', None, 'dp')
- new_head: float32 [2, 768, 96], P('section', 'dp')
- new_embed: float32 [2, 1256, 768], P('section', None, 'dp')
- new_norms: float32 [2, 6, 768], P('section', None, 'dp')
- loss_sum: float32 [], replicated
- grad_norm: float32 [], replicated
- activity: float32 [2, 3], replicated
The draws below stay inside these ranges and needn't reach their ends.
All inputs are finite; a program needn't handle non-finite values. No bound on the sum of `class_drop` on one device may be relied on, other than what follows from the above.
Results may differ from the reference program's by a relative error of at most 0.011.
Values may be sent and summed in bfloat16 or wider, within the bound.
No kernel may reach another device: no remote copies, remote signals or barrier semaphores. Data moves between devices by JAX's collectives and lax.ppermute only.
A program may use at most 256 MiB of HBM per device.

```python
import math
import jax
import jax.numpy as jnp
from jax import lax

D = 768
H = 12
HD = 64
FF = 3072
PD = 48
CLS = 1000
P_SIZE = 256
IMG_DEV = 4
STEP = 10
IMAGES = 64
NPAR = 16315392
N_DP = 16


def draw_images(key, part):
    key = jax.random.fold_in(key, 11)
    position = jnp.arange(IMAGES, dtype=jnp.float32) / max(IMAGES - 1, 1)
    base = jnp.clip(0.5 * jax.random.normal(key, (IMAGES, P_SIZE, PD), jnp.float32), -1.0, 1.0)
    scale = 0.34 + 0.66 * position
    return base * scale[:, None, None]


def draw_noise_draw(key, part):
    key = jax.random.fold_in(key, 31)
    return jnp.clip(jax.random.normal(key, (IMAGES, P_SIZE, PD), jnp.float32), -5.0, 5.0)


def draw_w_norms(key, part):
    key = jax.random.fold_in(key, 23)
    gain_key, bias_key = jax.random.split(key)
    ramp = 0.5 + jnp.arange(D, dtype=jnp.float32) / max(D - 1, 1)
    gains = ramp * jax.random.uniform(gain_key, (2, 3, D), jnp.float32, 0.8, 1.2)
    biases = jnp.clip(0.2 * jax.random.normal(bias_key, (2, 3, D), jnp.float32), -1.0, 1.0)
    return jnp.stack([gains, biases], axis=2).reshape(2, 6, D)


def table_rows():
    typical = 0.001 / math.sqrt(NPAR) / 12.0
    rows = jnp.arange(P_SIZE + CLS)
    return jnp.where(rows < P_SIZE, typical, 0.1 * typical).astype(jnp.float32)


def draw_moment_embed(key, part):
    key = jax.random.fold_in(key, 41)
    values = jnp.clip(jax.random.normal(key, (2, P_SIZE + CLS, D), jnp.float32), -4.0, 4.0)
    return values * (table_rows() / 9.0)[None, :, None]


def draw_square_embed(key, part):
    key = jax.random.fold_in(key, 43)
    factors = jnp.exp(jax.random.uniform(key, (2, P_SIZE + CLS, D), jnp.float32, 0.0, math.log(4.0)))
    sizes = table_rows()
    return factors * (0.0526 * sizes * sizes)[None, :, None]


def touch_ends(entries, own_key, low, largest):
    dims = entries.shape
    index_at = [jax.random.randint(jax.random.fold_in(own_key, axis), (), 0, dims[axis]) for axis in range(len(dims))]
    entries = entries.at[tuple(index_at)].set(low)
    longest = dims.index(max(dims))
    index_at[longest] = (index_at[longest] + 1) % dims[longest]
    return entries.at[tuple(index_at)].set(largest)


def block_levels(own_key, shape, shards, smallest, high):
    def one(dim, shards_of):
        draws = jax.random.uniform(jax.random.fold_in(jax.random.fold_in(own_key, 6), dim), (shards_of,), jnp.float32, smallest / len(shards), high / len(shards))
        return jnp.repeat(jnp.exp(draws), shape[dim] // shards_of).reshape((-1,) + (1,) * (len(shape) - dim - 1))

    factor_of = one(*shards[0])
    for cut in shards[1:]:
        factor_of = factor_of * one(*cut)
    return factor_of


def normal_values(rng, extent, width, most, cuts=(), held_as=jnp.bfloat16):
    array = jax.random.normal(rng, extent, jnp.float32) * width
    if len(cuts) > 0:
        array = block_levels(rng, extent, cuts, -0.22, 0.18) * array
    return jnp.clip(array, min=-most, max=most).astype(held_as)


def setup_inputs(seed: int = 0) -> dict:
    splits = jax.random.split(jax.random.key(seed), 29)
    return {
        "images": draw_images(jax.random.fold_in(splits[28], 71), 0),
        "noise_draw": draw_noise_draw(jax.random.fold_in(splits[28], 71), 0),
        "labels": touch_ends(jax.random.randint(splits[2], (IMAGES,), 0, CLS), jax.random.fold_in(splits[2], 1), 0, CLS - 1).astype(jnp.int32),
        "class_drop": touch_ends((jax.random.randint(splits[3], (IMAGES,), 0, 10) < 1).astype(jnp.int32), jax.random.fold_in(splits[3], 1), 0, 1),
        "w_qkv": normal_values(splits[4], (2, D, 3 * D), D ** -0.5, 0.21875, ((0, 2), (1, 16)), jnp.float32),
        "w_attn": normal_values(splits[5], (2, D, D), (D // 8) ** -0.5, 0.625, ((0, 2), (1, 16)), jnp.float32),
        "w_up": normal_values(splits[6], (2, D, FF), D ** -0.5, 0.21875, ((0, 2), (1, 16)), jnp.float32),
        "w_down": normal_values(splits[7], (2, FF, D), FF ** -0.5, 0.109375, ((0, 2), (1, 16)), jnp.float32),
        "w_in": normal_values(splits[8], (2, PD, D), PD ** -0.5, 0.875, ((0, 2), (2, 16)), jnp.float32),
        "w_head": normal_values(splits[9], (2, D, 2 * PD), (4 * D) ** -0.5, 0.109375, ((0, 2), (1, 16)), jnp.float32),
        "w_embed": normal_values(splits[10], (2, P_SIZE + CLS, D), 0.5, 3.0, ((0, 2), (2, 16)), jnp.float32),
        "w_norms": draw_w_norms(jax.random.fold_in(splits[28], 71), 0),
        "moment_qkv": normal_values(splits[12], (2, D, 3 * D), 0.0000000275, 1.4901161193847656e-07, ((0, 2), (1, 16)), jnp.float32),
        "moment_attn": normal_values(splits[13], (2, D, D), 0.0000000275, 1.4901161193847656e-07, ((0, 2), (1, 16)), jnp.float32),
        "moment_up": normal_values(splits[14], (2, D, FF), 0.0000000275, 1.4901161193847656e-07, ((0, 2), (1, 16)), jnp.float32),
        "moment_down": normal_values(splits[15], (2, FF, D), 0.0000000275, 1.4901161193847656e-07, ((0, 2), (1, 16)), jnp.float32),
        "moment_in": normal_values(splits[16], (2, PD, D), 0.0000000275, 1.4901161193847656e-07, ((0, 2), (2, 16)), jnp.float32),
        "moment_head": normal_values(splits[17], (2, D, 2 * PD), 0.0000000275, 1.4901161193847656e-07, ((0, 2), (1, 16)), jnp.float32),
        "moment_embed": draw_moment_embed(jax.random.fold_in(splits[28], 71), 0),
        "moment_norms": normal_values(splits[19], (2, 6, D), 0.0000000275, 1.4901161193847656e-07, ((0, 2), (2, 16)), jnp.float32),
        "square_qkv": jnp.clip(jnp.exp(math.log(1.29999999412783e-14) - 1.4017985 * jax.random.uniform(splits[20], (2, D, 3 * D), jnp.float32) ** block_levels(splits[20], (2, D, 3 * D), ((0, 2), (1, 16)), -0.2, 0.2)), 3.2000000539596273e-15, 1.29999999412783e-14),
        "square_attn": jnp.clip(jnp.exp(math.log(1.29999999412783e-14) - 1.4017985 * jax.random.uniform(splits[21], (2, D, D), jnp.float32) ** block_levels(splits[21], (2, D, D), ((0, 2), (1, 16)), -0.2, 0.2)), 3.2000000539596273e-15, 1.29999999412783e-14),
        "square_up": jnp.clip(jnp.exp(math.log(1.29999999412783e-14) - 1.4017985 * jax.random.uniform(splits[22], (2, D, FF), jnp.float32) ** block_levels(splits[22], (2, D, FF), ((0, 2), (1, 16)), -0.2, 0.2)), 3.2000000539596273e-15, 1.29999999412783e-14),
        "square_down": jnp.clip(jnp.exp(math.log(1.29999999412783e-14) - 1.4017985 * jax.random.uniform(splits[23], (2, FF, D), jnp.float32) ** block_levels(splits[23], (2, FF, D), ((0, 2), (1, 16)), -0.2, 0.2)), 3.2000000539596273e-15, 1.29999999412783e-14),
        "square_in": jnp.clip(jnp.exp(math.log(1.29999999412783e-14) - 1.4017985 * jax.random.uniform(splits[24], (2, PD, D), jnp.float32) ** block_levels(splits[24], (2, PD, D), ((0, 2), (2, 16)), -0.2, 0.2)), 3.2000000539596273e-15, 1.29999999412783e-14),
        "square_head": jnp.clip(jnp.exp(math.log(1.29999999412783e-14) - 1.4017985 * jax.random.uniform(splits[25], (2, D, 2 * PD), jnp.float32) ** block_levels(splits[25], (2, D, 2 * PD), ((0, 2), (1, 16)), -0.2, 0.2)), 3.2000000539596273e-15, 1.29999999412783e-14),
        "square_embed": draw_square_embed(jax.random.fold_in(splits[28], 71), 0),
        "square_norms": jnp.clip(jnp.exp(math.log(1.29999999412783e-14) - 1.4017985 * jax.random.uniform(splits[27], (2, 6, D), jnp.float32) ** block_levels(splits[27], (2, 6, D), ((0, 2), (2, 16)), -0.2, 0.2)), 3.2000000539596273e-15, 1.29999999412783e-14),
    }


@jax.custom_vjp
def low(v):
    return lax.optimization_barrier(v.astype(jnp.bfloat16)).astype(jnp.float32)

@jax.custom_vjp
def low_back(v):
    return v

def low_keep(v):
    return (low(v), None)

def low_pass(kept, grad):
    return (grad,)

def back_keep(v):
    return (v, None)

def back_low(kept, grad):
    return (low(grad),)
low.defvjp(low_keep, low_pass)
low_back.defvjp(back_keep, back_low)
EPS_NORM = 1e-05
NOISE_SCALE = 0.05
CLIP_NORM = 0.001
BETA_ONE = 0.9
BETA_TWO = 0.95
LEARN_RATES = (0.01, 0.06, 0.01, 0.01, 0.08, 0.01, 0.25, 0.4)
WEIGHT_DECAY = 0.1
EPS_ADAM = 1e-10

def product(left_side, right_side):
    return jnp.matmul(left_side, right_side, precision=lax.Precision.HIGHEST)

def layer_norm(values, gain, offset):
    center = values - lax.optimization_barrier(jnp.mean(values, axis=-1, keepdims=True))
    spread = lax.optimization_barrier(jnp.mean(center * center, axis=-1, keepdims=True))
    return center * lax.rsqrt(spread + EPS_NORM) * gain + offset

def flow_block(params, inputs, labels, keep):
    w_qkv, w_attn, w_up, w_down, w_in, w_head, w_embed, w_norms = params
    count_images = inputs.shape[0]
    hidden = low_back(product(low(inputs), low(w_in)))
    classes = jnp.take(w_embed[P_SIZE:], labels, axis=0) * keep[:, None]
    hidden = hidden + w_embed[:P_SIZE][None] + classes[:, None, :]
    normed = layer_norm(hidden, w_norms[0], w_norms[1])
    joint = low(low_back(product(low(normed), low(w_qkv))))
    joint = joint.reshape(count_images, P_SIZE, 3, H, HD).transpose(2, 0, 3, 1, 4)
    queries, key_rows, value_rows = (joint[0], joint[1], joint[2])
    scores = low_back(product(queries, jnp.swapaxes(key_rows, -1, -2))) * HD ** (-0.5)
    causal = jnp.arange(P_SIZE)[:, None] >= jnp.arange(P_SIZE)[None, :]
    scores = jnp.where(causal, scores, -1e+30)
    scores = scores - lax.optimization_barrier(jnp.max(scores, axis=-1, keepdims=True))
    exps = jnp.exp(scores)
    probs = exps / lax.optimization_barrier(jnp.sum(exps, axis=-1, keepdims=True))
    attended = low(low_back(product(low(probs), value_rows)))
    attended = attended.transpose(0, 2, 1, 3).reshape(count_images, P_SIZE, H * HD)
    branch_attn = low_back(product(attended, low(w_attn)))
    hidden = hidden + branch_attn
    normed = layer_norm(hidden, w_norms[2], w_norms[3])
    up_out = low_back(product(low(normed), low(w_up)))
    branch_mlp = low_back(product(low(jax.nn.gelu(up_out, approximate=False)), low(w_down)))
    hidden = hidden + branch_mlp
    normed = layer_norm(hidden, w_norms[4], w_norms[5])
    head_out = low_back(product(low(normed), low(w_head)))
    padding = jnp.zeros((count_images, 1, PD), jnp.float32)
    shift = jnp.concatenate([padding, head_out[:, :-1, :PD]], axis=1)
    log_scale = jnp.concatenate([padding, head_out[:, :-1, PD:]], axis=1)
    latent = (inputs - shift) * jnp.exp(-log_scale)
    statistics = jnp.stack([jnp.sum(hidden * hidden), jnp.sum(branch_attn * branch_attn), jnp.sum(branch_mlp * branch_mlp)])
    return (latent, jnp.sum(log_scale), statistics)

def reference(images, noise_draw, labels, class_drop, w_qkv, w_attn, w_up, w_down, w_in, w_head, w_embed, w_norms, moment_qkv, moment_attn, moment_up, moment_down, moment_in, moment_head, moment_embed, moment_norms, square_qkv, square_attn, square_up, square_down, square_in, square_head, square_embed, square_norms):
    weights = (w_qkv, w_attn, w_up, w_down, w_in, w_head, w_embed, w_norms)
    moments = (moment_qkv, moment_attn, moment_up, moment_down, moment_in, moment_head, moment_embed, moment_norms)
    squares = (square_qkv, square_attn, square_up, square_down, square_in, square_head, square_embed, square_norms)
    inputs_all = images + NOISE_SCALE * noise_draw
    keep_all = (1 - class_drop).astype(jnp.float32)
    coefficient = 1.0 / (IMAGES * P_SIZE * PD * math.log(2.0))
    grouped = (inputs_all.reshape(N_DP, IMG_DEV, P_SIZE, PD), labels.reshape(N_DP, IMG_DEV), keep_all.reshape(N_DP, IMG_DEV))

    def total(params):

        def group_loss(carry, item):
            group_inputs, group_labels, group_keep = item
            latent_one, det_one, stats_one = flow_block(tuple((param[0] for param in params)), group_inputs, group_labels, group_keep)
            latent_two, det_two, stats_two = flow_block(tuple((param[1] for param in params)), latent_one[:, ::-1], group_labels, group_keep)
            summed = 0.5 * jnp.sum(latent_two * latent_two) + det_one + det_two
            return (carry + summed, jnp.stack([stats_one, stats_two]))
        loss_total, statistics = lax.scan(jax.checkpoint(group_loss), jnp.zeros((), jnp.float32), grouped)
        return (loss_total * coefficient, (loss_total, lax.optimization_barrier(jnp.sum(statistics, axis=0))))
    scaled, backward, aux_values = jax.vjp(total, weights, has_aux=True)
    loss_sum, statistics = aux_values
    gradients, = backward(jnp.ones_like(scaled))
    square_total = sum((jnp.sum(gradient * gradient) for gradient in gradients))
    grad_norm = jnp.sqrt(square_total)
    factor = jnp.minimum(1.0, CLIP_NORM / grad_norm)
    new_moments, new_squares, new_weights = ([], [], [])
    for weight, moment, square, gradient, rate in zip(weights, moments, squares, gradients, LEARN_RATES):
        clipped = gradient * factor
        moment_next = BETA_ONE * moment + (1 - BETA_ONE) * clipped
        square_next = BETA_TWO * square + (1 - BETA_TWO) * clipped * clipped
        update = moment_next / (1 - BETA_ONE ** STEP) / (jnp.sqrt(square_next / (1 - BETA_TWO ** STEP)) + EPS_ADAM)
        new_moments.append(moment_next)
        new_squares.append(square_next)
        new_weights.append(weight - rate * (update + WEIGHT_DECAY * weight))
    activity = jnp.sqrt(statistics / (IMAGES * P_SIZE * D))
    return (new_moments[0], new_moments[1], new_moments[2], new_moments[3], new_moments[4], new_moments[5], new_moments[6], new_moments[7], new_squares[0], new_squares[1], new_squares[2], new_squares[3], new_squares[4], new_squares[5], new_squares[6], new_squares[7], new_weights[0], new_weights[1], new_weights[2], new_weights[3], new_weights[4], new_weights[5], new_weights[6], new_weights[7], loss_sum, grad_norm, activity)
```

```python
import math

import jax
import jax.numpy as jnp
from jax import lax
from jax.experimental import pallas as pl
from jax.experimental.pallas import tpu as pltpu
from jax.sharding import PartitionSpec as P

D = 768
H = 12
HD = 64
FF = 3072
PD = 48
CLS = 1000
P_SIZE = 256
STEP = 10
QKV = 3 * D

EPS_NORM = 1e-05
NOISE_SCALE = 0.05
CLIP_NORM = 0.001
BETA_ONE = 0.9
BETA_TWO = 0.95
LEARN_RATES = (0.01, 0.06, 0.01, 0.01, 0.08, 0.01, 0.25, 0.4)
WEIGHT_DECAY = 0.1
EPS_ADAM = 1e-10

BF = jnp.bfloat16
F32 = jnp.float32

S_HEAD = 2 * P_SIZE
S_NORM = S_HEAD + 2 * PD
S_IN = S_HEAD + 128
S_WIDTH = 768
FIRST_WIDTH = S_WIDTH + QKV + D
PAIR = 2 * HD
PAIRS = H // 2
TILE = 512
VMEM_BYTES = 56 << 20


def swap_pairs(count, bit):
    return [(source, source ^ (1 << bit)) for source in range(count)]


def exchange(value, axis, bit=0):
    return lax.ppermute(value, axis, swap_pairs(lax.axis_size(axis), bit))


def dp_bits():
    return lax.axis_size("dp").bit_length() - 1


def parity_of(bit):
    return (lax.axis_index("dp") >> bit) & 1


GATHER_ORDERS = ({"first": (0, 1, 2, 3), "up": (1, 2, 3, 0), "down": (2, 0, 1, 3)},)
SCATTER_ORDERS = (
    {"down": (0, 2, 1, 3), "up": (1, 2, 0, 3), "first": (0, 1, 2, 3), "last": (1, 2, 0, 3)},
    {"first": (2, 0, 3, 1)},
)


BY_COLLECTIVE = ((), ("down", "up"))
SPLIT = (0, "first")


def order_from(table, block, name):
    count = dp_bits()
    if count == 4:
        return table[block][name]
    first = {"first": 0, "up": 1, "down": 2, "last": 1}[name]
    return tuple((first + step) % count for step in range(count))


class Sequencer:
    def __init__(self):
        self.flights = []
        self.asked = []
        self.token = jnp.zeros((), F32)

    def tie(self, tree):
        leaves, kind = jax.tree.flatten(tree)
        tied = lax.optimization_barrier([self.token] + leaves)
        self.token = tied[0]
        return jax.tree.unflatten(kind, tied[1:])

    def launch(self, steps):
        flight = {"steps": steps, "done": False}
        self.asked.append((flight, next(steps)))
        return flight

    def turn(self):
        requests = []
        for flight, got in zip(self.flights, self.tie([flight["got"] for flight in self.flights])):
            try:
                requests.append((flight, flight["steps"].send(got)))
            except StopIteration as stop:
                flight["done"] = True
                flight["result"] = stop.value
        requests += self.asked
        values = self.tie([value for _, (value, _, _) in requests])
        self.flights, self.asked = [], []
        for value, (flight, (_, axis, bit)) in zip(values, requests):
            flight["got"] = exchange(value, axis, bit)
            self.flights.append(flight)

    def wait(self, *flights):
        while not all(flight["done"] for flight in flights):
            self.turn()
        return flights[0]["result"] if len(flights) == 1 else [f["result"] for f in flights]

    def compute(self, function, *values):
        return self.tie(function(*self.tie(values)))


def gather_steps(part, order):
    have = []
    held = part
    for bit in reversed(order):
        other = yield (held, "dp", bit)
        place = sum(1 for b in have if b > bit)
        swap = parity_of(bit) == 1
        held = jnp.stack([jnp.where(swap, other, held), jnp.where(swap, held, other)], axis=place)
        have.append(bit)
    return held.reshape((-1,) + part.shape[1:])


def weight_steps(part, order):
    mine = yield from gather_steps(part, order)
    other = yield (mine, "section", 0)
    return mine, other


def pair_steps(mine):
    other = yield (mine, "section", 0)
    return mine, other


def part_of(value, axis_index):
    starts = [axis_index.get(axis, 0) for axis in range(value.ndim)]
    sizes = [1 if axis in axis_index else extent for axis, extent in enumerate(value.shape)]
    sliced = lax.dynamic_slice(value, starts, sizes)
    return sliced.reshape([extent for axis, extent in enumerate(sizes) if axis not in axis_index])


def scatter_steps(mine, given, order):
    other = yield (given, "section", 0)
    result = yield from scatter_both((mine, other), order)
    return result


def scatter_both(both, order):
    count = dp_bits()
    rows = both[0].shape[0] >> count
    held = [value.reshape((2,) * count + (rows,) + value.shape[1:]) for value in both]
    left = sorted(range(count), reverse=True)
    chosen = [{} for _ in held]

    def piece(axis, index):
        parts = []
        for value, fixed in zip(held, chosen):
            free = [place for place in range(value.ndim) if place not in fixed]
            parts.append(part_of(value, {**fixed, free[axis]: index}).astype(F32))
        return sum(parts[1:], parts[0])

    for bit in order:
        axis = left.index(bit)
        parity = parity_of(bit)
        other = yield (piece(axis, 1 - parity).astype(BF), "dp", bit)
        for value, fixed in zip(held, chosen):
            free = [place for place in range(value.ndim) if place not in fixed]
            fixed[free[axis]] = parity
        if len(held) > 1:
            kept = sum(part_of(value, fixed).astype(F32) for value, fixed in zip(held, chosen))
            held, chosen = [kept.astype(BF)], [{}]
        held.append(other)
        chosen.append({})
        left.remove(bit)
    return sum(part_of(value, fixed).astype(F32) for value, fixed in zip(held, chosen))


def one_step(value, axis, bit=0):
    got = yield (value, axis, bit)
    return got


def one_pair(mine):
    other = yield (mine, "section", 0)
    return mine, other


def sum_pair(mine, given):
    other = yield (given, "section", 0)
    return mine, other


def down_columns(rows, width):
    count = rows.shape[0] // width
    return rows.reshape(count, width, D).transpose(1, 0, 2).reshape(width, count * D)


def down_rows(columns, width):
    count = columns.shape[1] // D
    return columns.reshape(-1, width, count, D).transpose(0, 2, 1, 3).reshape(-1, D)


def label_steps(labels):
    gathered = yield from gather_steps(labels[None], tuple(range(dp_bits())))
    return gathered.reshape(-1)


def class_steps(own, is_first, order):
    other = yield (own, "section", 0)
    both = jnp.concatenate([jnp.where(is_first, own, other), jnp.where(is_first, other, own)], axis=1)
    whole = yield from gather_steps(both, order)
    return whole


def sum_steps(values):
    other = yield (values, "section", 0)
    values = values + other
    for bit in range(dp_bits()):
        other = yield (values, "dp", bit)
        values = values + other
    return values


def dot(left, right):
    return lax.dot_general(left, right, (((1,), (0,)), ((), ())), preferred_element_type=F32)


def dot_nt(left, right):
    return lax.dot_general(left, right, (((1,), (1,)), ((), ())), preferred_element_type=F32)


def dot_tn(left, right):
    return lax.dot_general(left, right, (((0,), (0,)), ((), ())), preferred_element_type=F32)


def two_terms(value):
    high = lax.optimization_barrier(value.astype(BF))
    return high, (value - high.astype(F32)).astype(BF)


def three_terms(value):
    high = lax.optimization_barrier(value.astype(BF))
    return (high,) + two_terms(value - high.astype(F32))


def whole_spec(*shape):
    return pl.BlockSpec(shape, lambda *_: (0,) * len(shape))


def row_spec(width):
    return pl.BlockSpec((P_SIZE, width), lambda j: (j, 0))


def first_spec(index):
    return pl.BlockSpec((D, D), lambda *_: (0, index))


HEAD_SPEC = pl.BlockSpec((D, 128), lambda *_: (0, S_HEAD // 128))
IN_SPEC = pl.BlockSpec((D, 128), lambda *_: (0, S_IN // 128))


def shape_of(rows, columns, kind=F32):
    return jax.ShapeDtypeStruct((rows, columns), kind)


def call(kernel, name, flops, **fields):
    return pl.pallas_call(
        kernel,
        name=name,
        cost_estimate=pl.CostEstimate(flops=flops, bytes_accessed=flops // 256, transcendentals=0),
        compiler_params=pltpu.CompilerParams(vmem_limit_bytes=VMEM_BYTES),
        **fields,
    )


def iotas(rows, columns):
    return (
        lax.broadcasted_iota(jnp.int32, (rows, columns), 0),
        lax.broadcasted_iota(jnp.int32, (rows, columns), 1),
    )


def where_ones(condition):
    return jnp.where(condition, 1.0, 0.0).astype(BF)


def norm_parts(values):
    center = values - jnp.mean(values, axis=-1, keepdims=True)
    scale = lax.rsqrt(jnp.mean(center * center, axis=-1, keepdims=True) + EPS_NORM)
    return center, scale


def norm_rows(values, norms, which):
    center, scale = norm_parts(values)
    return (center * scale * norms[2 * which : 2 * which + 1] + norms[2 * which + 1 : 2 * which + 2]).astype(BF)


def norm_back_rows(values, norms, which, cotangent):
    center, scale = norm_parts(values)
    unit = center * scale
    inner = cotangent * norms[2 * which : 2 * which + 1]
    first = jnp.mean(inner, axis=-1, keepdims=True)
    second = jnp.mean(inner * unit, axis=-1, keepdims=True)
    gain_grad = jnp.sum(cotangent * unit, axis=0, keepdims=True)
    offset_grad = jnp.sum(cotangent, axis=0, keepdims=True)
    return scale * (inner - first - unit * second), gain_grad, offset_grad


def add_sums(sums_ref, *rows):
    @pl.when(pl.program_id(0) == 0)
    def _():
        sums_ref[...] = jnp.zeros_like(sums_ref)

    for index, row in enumerate(rows):
        sums_ref[index : index + 1, :] += row


def begin_kernel(x_ref, class_ref, small_ref, q_ref, k_ref, v_ref, hidden_ref, normed_ref, joint_ref, norms_ref):
    row, column = iotas(P_SIZE, P_SIZE)
    same = where_ones(row == column)
    hidden = dot_nt(same, small_ref[:, :P_SIZE]) + dot_nt(same, small_ref[:, P_SIZE:S_HEAD])
    hidden = hidden + dot_nt(x_ref[...].astype(BF), small_ref[:, S_IN : S_IN + PD])
    hidden = hidden + class_ref[pl.ds(pl.program_id(0), 1), :]
    row, column = iotas(8, 128)
    place = column - 2 * PD
    term = where_ones((row < 6) & ((place == row) | (place == row + 6) | (place == row + 12)))
    norms = dot_nt(term, small_ref[:, S_HEAD : S_HEAD + 128])
    hidden_ref[...] = hidden
    norms_ref[...] = norms
    normed = norm_rows(hidden, norms, 0)
    normed_ref[...] = normed
    for part, weight_ref in enumerate((q_ref, k_ref, v_ref)):
        joint_ref[:, part * D : (part + 1) * D] = dot(normed, weight_ref[...]).astype(BF)


def begin(inputs, classes, first):
    rows = inputs.shape[0]
    return call(
        begin_kernel,
        "embed_norm_project",
        2 * rows * D * 4 * D,
        grid=(rows // P_SIZE,),
        in_specs=[row_spec(PD), whole_spec(*classes.shape)] + [first_spec(part) for part in range(4)],
        out_specs=[row_spec(D), row_spec(D), row_spec(QKV), whole_spec(8, D)],
        out_shape=[shape_of(rows, D), shape_of(rows, D, BF), shape_of(rows, QKV, BF), shape_of(8, D)],
    )(inputs, classes, first, first, first, first)


def attention_end_kernel(attended_ref, weight_ref, hidden_ref, norms_ref, middle_ref, normed_ref, sums_ref):
    branch = dot(attended_ref[...], weight_ref[...])
    middle = hidden_ref[...] + branch
    middle_ref[...] = middle
    normed_ref[...] = norm_rows(middle, norms_ref[...], 1)
    add_sums(sums_ref, jnp.sum(branch * branch, axis=0, keepdims=True))


def attention_end(attended, first, hidden, norms):
    rows = attended.shape[0]
    return call(
        attention_end_kernel,
        "attention_end",
        2 * rows * D * D,
        grid=(rows // P_SIZE,),
        in_specs=[row_spec(D), first_spec(4), row_spec(D), whole_spec(8, D)],
        out_specs=[row_spec(D), row_spec(D), whole_spec(8, D)],
        out_shape=[shape_of(rows, D), shape_of(rows, D, BF), shape_of(8, D)],
    )(attended, first, hidden, norms)


def half_steps(columns):
    count = columns // TILE
    return 2 * count, lambda j: jnp.minimum(j, count - 1), lambda j: jnp.maximum(j - count, 0), count


def up_kernel(count, x_ref, one_ref, two_ref, active_one, active_two, slope_one, slope_two):
    def half(weight_ref, active_ref, slope_ref):
        u = dot(x_ref[...], weight_ref[...])
        t = pl.reciprocal(1.0 + (0.3275911 / math.sqrt(2.0)) * jnp.abs(u), approx=True)
        bell = jnp.exp(-0.5 * u * u)
        poly = t * (0.127414796 + t * (-0.142248368 + t * (0.7107068705 + t * (-0.7265760135 + t * 0.5307027145))))
        tail = poly * bell
        share = jnp.where(u >= 0, 1.0 - tail, tail)
        active_ref[...] = (u * share).astype(BF)
        slope_ref[...] = (share + u * bell * (1.0 / math.sqrt(2.0 * math.pi))).astype(BF)

    @pl.when(pl.program_id(0) < count)
    def _():
        half(one_ref, active_one, slope_one)

    @pl.when(pl.program_id(0) >= count)
    def _():
        half(two_ref, active_two, slope_two)


def up_halves(normed, one, two):
    rows, columns = normed.shape[0], one.shape[1]
    steps, at_one, at_two, count = half_steps(columns)
    tiles = [lambda j: (0, at_one(j)), lambda j: (0, at_two(j))]
    return call(
        lambda *refs: up_kernel(count, *refs),
        "up_gelu",
        4 * rows * D * columns,
        grid=(steps,),
        in_specs=[whole_spec(rows, D)] + [pl.BlockSpec((D, TILE), tile) for tile in tiles],
        out_specs=[pl.BlockSpec((rows, TILE), tile) for tile in tiles * 2],
        out_shape=[shape_of(rows, columns, BF)] * 4,
    )(normed, one, two)


def end_kernel(
    active_one, active_two, down_one, down_two, middle_ref, norms_ref, head_ref, x_ref,
    final_ref, normed_ref, shrink_ref, latent_ref, sums_ref,
):
    branch = dot(active_one[...], down_one[...]) + dot(active_two[...], down_two[...])
    final = middle_ref[...] + branch
    final_ref[...] = final
    normed = norm_rows(final, norms_ref[...], 2)
    normed_ref[...] = normed
    head_out = dot(normed, head_ref[...])
    row, _ = iotas(P_SIZE, 128)
    moved = jnp.where(row == 0, 0.0, pltpu.roll(head_out, 1, 0))
    log_scale = moved[:, PD : 2 * PD]
    shrink = jnp.exp(-log_scale)
    shrink_ref[...] = shrink
    latent_ref[...] = (x_ref[...] - moved[:, :PD]) * shrink
    _, lane = iotas(1, D)
    add_sums(
        sums_ref,
        jnp.sum(final * final, axis=0, keepdims=True),
        jnp.sum(branch * branch, axis=0, keepdims=True),
        jnp.where(lane == 0, jnp.sum(log_scale), 0.0),
    )


def end(actives, downs, middle, norms, first, inputs):
    rows, columns = actives[0].shape
    return call(
        end_kernel,
        "down_norm_head",
        4 * rows * D * columns,
        grid=(rows // P_SIZE,),
        in_specs=[row_spec(columns)] * 2
        + [whole_spec(columns, D)] * 2
        + [row_spec(D), whole_spec(8, D), HEAD_SPEC, row_spec(PD)],
        out_specs=[row_spec(D), row_spec(D), row_spec(PD), row_spec(PD), whole_spec(8, D)],
        out_shape=[
            shape_of(rows, D), shape_of(rows, D, BF), shape_of(rows, PD), shape_of(rows, PD), shape_of(8, D)
        ],
    )(*actives, *downs, middle, norms, first, inputs)


def head_back_kernel(
    coefficient, latent_grad_ref, shrink_ref, latent_ref, final_ref, norms_ref, head_ref, normed_ref,
    through_ref, flow_ref, low_ref, weight_ref, sums_ref,
):
    latent_grad = latent_grad_ref[...]
    through = latent_grad * shrink_ref[...]
    through_ref[...] = through
    scale_grad = coefficient - latent_grad * latent_ref[...]
    row, column = iotas(PD, 128)
    placed = dot((-through).astype(BF), where_ones(row == column))
    placed = placed + dot(scale_grad.astype(BF), where_ones(row + PD == column))
    row, _ = iotas(P_SIZE, 128)
    head_grad = jnp.where(row == P_SIZE - 1, 0.0, pltpu.roll(placed, P_SIZE - 1, 0)).astype(BF)
    flow, gain_grad, offset_grad = norm_back_rows(
        final_ref[...], norms_ref[...], 2, dot_nt(head_grad, head_ref[...])
    )
    flow_ref[...] = flow
    low_ref[...] = flow.astype(BF)

    @pl.when(pl.program_id(0) == 0)
    def _():
        weight_ref[...] = jnp.zeros_like(weight_ref)

    weight_ref[...] += dot_tn(normed_ref[...], head_grad)
    add_sums(sums_ref, gain_grad, offset_grad)


def head_back(coefficient, latent_grad, shrink, latent, final, norms, first, normed):
    rows = final.shape[0]
    return call(
        lambda *refs: head_back_kernel(coefficient, *refs),
        "head_back",
        4 * rows * D * 128,
        grid=(rows // P_SIZE,),
        in_specs=[row_spec(PD)] * 3 + [row_spec(D), whole_spec(8, D), HEAD_SPEC, row_spec(D)],
        out_specs=[row_spec(PD), row_spec(D), row_spec(D), whole_spec(D, 128), whole_spec(8, D)],
        out_shape=[
            shape_of(rows, PD), shape_of(rows, D), shape_of(rows, D, BF), shape_of(D, 128), shape_of(8, D)
        ],
    )(latent_grad, shrink, latent, final, norms, first, normed)


def down_grad_kernel(count, one_ref, two_ref, low_ref, out_one, out_two):
    @pl.when(pl.program_id(0) < count)
    def _():
        out_one[...] = dot_tn(one_ref[...], low_ref[...]).astype(BF)

    @pl.when(pl.program_id(0) >= count)
    def _():
        out_two[...] = dot_tn(two_ref[...], low_ref[...]).astype(BF)


def down_grads(one, two, low):
    rows, columns = one.shape
    steps, at_one, at_two, count = half_steps(columns)
    return call(
        lambda *refs: down_grad_kernel(count, *refs),
        "down_weight_grad",
        4 * rows * D * columns,
        grid=(steps,),
        in_specs=[
            pl.BlockSpec((rows, TILE), lambda j: (0, at_one(j))),
            pl.BlockSpec((rows, TILE), lambda j: (0, at_two(j))),
            whole_spec(rows, D),
        ],
        out_specs=[
            pl.BlockSpec((TILE, D), lambda j: (at_one(j), 0)),
            pl.BlockSpec((TILE, D), lambda j: (at_two(j), 0)),
        ],
        out_shape=[shape_of(columns, D, BF)] * 2,
    )(one, two, low)


def up_back_kernel(count, low_ref, normed_ref, *refs):
    def half(weight_ref, slope_ref, grad_ref, out_ref):
        grad = (dot_nt(low_ref[...], weight_ref[...]) * slope_ref[...].astype(F32)).astype(BF)
        grad_ref[...] = grad
        out_ref[...] = dot_tn(normed_ref[...], grad).astype(BF)

    @pl.when(pl.program_id(0) < count)
    def _():
        half(*refs[0::2])

    @pl.when(pl.program_id(0) >= count)
    def _():
        half(*refs[1::2])


def up_back(low, normed, downs, slopes):
    rows, columns = slopes[0].shape
    steps, at_one, at_two, count = half_steps(columns)
    by_column = [lambda j: (0, at_one(j)), lambda j: (0, at_two(j))]
    by_row = [lambda j: (at_one(j), 0), lambda j: (at_two(j), 0)]
    tiles = [pl.BlockSpec((rows, TILE), tile) for tile in by_column]
    return call(
        lambda *refs: up_back_kernel(count, *refs),
        "up_back",
        8 * rows * D * columns,
        grid=(steps,),
        in_specs=[whole_spec(rows, D)] * 2 + [pl.BlockSpec((TILE, D), tile) for tile in by_row] + tiles,
        out_specs=tiles + [pl.BlockSpec((D, TILE), tile) for tile in by_column],
        out_shape=[shape_of(rows, columns, BF)] * 2 + [shape_of(D, columns, BF)] * 2,
    )(low, normed, *downs, *slopes)


def middle_back_kernel(
    one_ref, two_ref, up_one, up_two, middle_ref, norms_ref, above_ref, weight_ref,
    wide_ref, low_ref, attended_ref, sums_ref,
):
    back = dot_nt(one_ref[...], up_one[...]) + dot_nt(two_ref[...], up_two[...])
    flow, gain_grad, offset_grad = norm_back_rows(middle_ref[...], norms_ref[...], 1, back)
    total = above_ref[...] + flow
    wide_ref[...] = total
    low = total.astype(BF)
    low_ref[...] = low
    attended_ref[...] = dot_nt(low, weight_ref[...]).astype(BF)
    add_sums(sums_ref, gain_grad, offset_grad)


def middle_back(grads, ups, middle, norms, above, first):
    rows, columns = grads[0].shape
    return call(
        middle_back_kernel,
        "middle_back",
        4 * rows * D * columns,
        grid=(rows // P_SIZE,),
        in_specs=[row_spec(columns)] * 2
        + [whole_spec(D, columns)] * 2
        + [row_spec(D), whole_spec(8, D), row_spec(D), first_spec(4)],
        out_specs=[row_spec(D), row_spec(D), row_spec(D), whole_spec(8, D)],
        out_shape=[shape_of(rows, D), shape_of(rows, D, BF), shape_of(rows, D, BF), shape_of(8, D)],
    )(*grads, *ups, middle, norms, above, first)


def input_back_kernel(
    joint_ref, q_ref, k_ref, v_ref, hidden_ref, norms_ref, above_ref, in_ref, through_ref, low_ref, out_ref, sums_ref
):
    back = sum(
        dot_nt(joint_ref[:, part * D : (part + 1) * D], weight_ref[...])
        for part, weight_ref in enumerate((q_ref, k_ref, v_ref))
    )
    flow, gain_grad, offset_grad = norm_back_rows(hidden_ref[...], norms_ref[...], 0, back)
    low = (above_ref[...] + flow).astype(BF)
    low_ref[...] = low
    out_ref[...] = through_ref[...] + dot(low, in_ref[...])[:, :PD]
    add_sums(sums_ref, gain_grad, offset_grad)


def input_back(joint_grad, first, hidden, norms, above, through):
    rows = hidden.shape[0]
    return call(
        input_back_kernel,
        "input_back",
        2 * rows * D * QKV,
        grid=(rows // P_SIZE,),
        in_specs=[row_spec(QKV)]
        + [first_spec(part) for part in range(1, 4)]
        + [row_spec(D), whole_spec(8, D), row_spec(D), IN_SPEC, row_spec(PD)],
        out_specs=[row_spec(D), row_spec(PD), whole_spec(8, D)],
        out_shape=[shape_of(rows, D, BF), shape_of(rows, PD), shape_of(8, D)],
    )(joint_grad, first, first, first, hidden, norms, above, first, through)


COLUMNS = 256
SOURCE_AT = (QKV + D) // COLUMNS


def first_grad_kernel(
    steps, section_ref, normed_ref, attended_ref, low_ref, joint_ref, middle_ref, source_ref, head_ref,
    sums_one, sums_two, sums_three, mine_ref, given_ref,
):
    step = pl.program_id(0)
    to_mine = (step >= steps // 2) == (section_ref[0] == 1)

    def put(value):
        @pl.when(to_mine)
        def _():
            mine_ref[...] = value

        @pl.when(jnp.logical_not(to_mine))
        def _():
            given_ref[...] = value

    @pl.when(step < QKV // COLUMNS)
    def _():
        put(dot_tn(normed_ref[...], joint_ref[...]).astype(BF))

    @pl.when((step >= QKV // COLUMNS) & (step < SOURCE_AT))
    def _():
        put(dot_tn(attended_ref[...], middle_ref[...]).astype(BF))

    @pl.when((step >= SOURCE_AT) & (step < steps - 1))
    def _():
        put(dot_tn(low_ref[...], source_ref[...]).astype(BF))

    @pl.when(step == steps - 1)
    def _():
        row, column = iotas(8, 128)
        rest = head_ref[...]
        for which, sums_ref in enumerate((sums_one, sums_two, sums_three)):
            place = where_ones((row < 2) & (column == row + 2 * PD + 2 * which))
            rest = rest + dot_tn(sums_ref[...].astype(BF), place)
        source = dot_tn(low_ref[...], source_ref[:, :128])
        put(jnp.concatenate([source, rest], axis=1).astype(BF))


def first_grads(section, normed, attended, low, joint_grad, low_middle, sources, head, sums):
    rows = normed.shape[0]
    steps = SOURCE_AT + sources.shape[1] // COLUMNS
    half = steps // 2

    def tile(offset, count):
        return pl.BlockSpec((rows, COLUMNS), lambda j, s: (0, jnp.clip(j - offset, 0, count - 1)))

    whole = pl.BlockSpec((rows, D), lambda j, s: (0, 0))
    small = pl.BlockSpec((8, D), lambda j, s: (0, 0))
    return call(
        lambda *refs: first_grad_kernel(steps, *refs),
        "first_weight_grad",
        2 * rows * D * (QKV + D + sources.shape[1]),
        grid_spec=pltpu.PrefetchScalarGridSpec(
            num_scalar_prefetch=1,
            grid=(steps,),
            in_specs=[
                whole,
                whole,
                whole,
                tile(0, QKV // COLUMNS),
                tile(QKV // COLUMNS, D // COLUMNS),
                tile(SOURCE_AT, sources.shape[1] // COLUMNS),
                pl.BlockSpec((D, 128), lambda j, s: (0, 0)),
                small,
                small,
                small,
            ],
            out_specs=[
                pl.BlockSpec((D, COLUMNS), lambda j, s: (0, jnp.clip(j - half * s[0], 0, half - 1))),
                pl.BlockSpec((D, COLUMNS), lambda j, s: (0, jnp.clip(j - half * (1 - s[0]), 0, half - 1))),
            ],
        ),
        out_shape=[shape_of(D, half * COLUMNS, BF)] * 2,
    )(section[None].astype(jnp.int32), normed, attended, low, joint_grad, low_middle, sources, head, *sums)


def head_mask(which, axis, scale=1.0):
    shape = (1, PAIR) if axis == 1 else (PAIR, 1)
    place = lax.broadcasted_iota(jnp.int32, shape, axis)
    return jnp.where((place >= HD * which) & (place < HD * (which + 1)), scale, 0.0).astype(BF)


def attend_kernel(q_ref, k_ref, v_ref, out_ref, probs_ref):
    queries, key_rows = q_ref[...], k_ref[...]
    values_t = v_ref[...].T
    key_at = lax.broadcasted_iota(jnp.int32, (P_SIZE, P_SIZE), 0)
    query_at = lax.broadcasted_iota(jnp.int32, (P_SIZE, P_SIZE), 1)
    causal = key_at <= query_at
    total = jnp.zeros((PAIR, P_SIZE), F32)
    for which in range(2):
        scores = dot_nt(key_rows, queries * head_mask(which, 1, HD ** (-0.5)))
        scores = jnp.where(causal, scores, -1e30)
        exps = jnp.exp(scores - jnp.max(scores, axis=0, keepdims=True))
        probs = (exps * (1.0 / jnp.sum(exps, axis=0, keepdims=True))).astype(BF)
        probs_ref[0, which] = probs
        total = total + dot(values_t * head_mask(which, 0), probs)
    out_ref[...] = total.T.astype(BF)


def attend(joint):
    count = joint.shape[0] // P_SIZE
    part = [pl.BlockSpec((P_SIZE, PAIR), lambda n, p, s=s: (n, s * PAIRS + p)) for s in range(3)]
    return pl.pallas_call(
        attend_kernel,
        grid=(count, PAIRS),
        in_specs=part,
        out_specs=[
            pl.BlockSpec((P_SIZE, PAIR), lambda n, p: (n, p)),
            pl.BlockSpec((1, 2, P_SIZE, P_SIZE), lambda n, p: (n, p, 0, 0)),
        ],
        out_shape=[
            jax.ShapeDtypeStruct((joint.shape[0], D), BF),
            jax.ShapeDtypeStruct((count, H, P_SIZE, P_SIZE), BF),
        ],
        cost_estimate=pl.CostEstimate(
            flops=8 * count * H * P_SIZE * P_SIZE * HD,
            bytes_accessed=2 * count * H * P_SIZE * P_SIZE + 8 * joint.shape[0] * D,
            transcendentals=count * H * P_SIZE * P_SIZE,
        ),
        compiler_params=pltpu.CompilerParams(vmem_limit_bytes=VMEM_BYTES),
        name="attention",
    )(joint, joint, joint)


def attend_back_kernel(q_ref, k_ref, v_ref, probs_ref, grad_ref, out_ref):
    pair = pl.program_id(1)
    queries, value_rows, grad = q_ref[...], v_ref[...], grad_ref[...]
    keys_t = k_ref[...].T
    query_grad = jnp.zeros((PAIR, P_SIZE), F32)
    key_grad = jnp.zeros((P_SIZE, PAIR), F32)
    value_grad = jnp.zeros((P_SIZE, PAIR), F32)
    for which in range(2):
        mask = head_mask(which, 1)
        probs = probs_ref[0, which]
        own_grad = grad * mask
        value_grad = value_grad + dot(probs, own_grad)
        prob_grad = dot_nt(value_rows, own_grad)
        wide = probs.astype(F32)
        total = jnp.sum(wide * prob_grad, axis=0, keepdims=True)
        score_grad = (wide * (prob_grad - total) * HD ** (-0.5)).astype(BF)
        key_grad = key_grad + dot(score_grad, queries * mask)
        query_grad = query_grad + dot(keys_t * head_mask(which, 0), score_grad)
    for part, value in enumerate((query_grad.T, key_grad, value_grad)):
        out_ref[:, pl.ds(pl.multiple_of(part * D + pair * PAIR, PAIR), PAIR)] = value.astype(BF)


def attend_back(joint, probs, grad):
    count = joint.shape[0] // P_SIZE
    part = [pl.BlockSpec((P_SIZE, PAIR), lambda n, p, s=s: (n, s * PAIRS + p)) for s in range(3)]
    return pl.pallas_call(
        attend_back_kernel,
        grid=(count, PAIRS),
        in_specs=part
        + [
            pl.BlockSpec((1, 2, P_SIZE, P_SIZE), lambda n, p: (n, p, 0, 0)),
            pl.BlockSpec((P_SIZE, PAIR), lambda n, p: (n, p)),
        ],
        out_specs=pl.BlockSpec((P_SIZE, QKV), lambda n, p: (n, 0)),
        out_shape=jax.ShapeDtypeStruct(joint.shape, BF),
        cost_estimate=pl.CostEstimate(
            flops=16 * count * H * P_SIZE * P_SIZE * HD,
            bytes_accessed=2 * count * H * P_SIZE * P_SIZE + 14 * joint.shape[0] * D,
            transcendentals=0,
        ),
        compiler_params=pltpu.CompilerParams(vmem_limit_bytes=VMEM_BYTES),
        name="attention_back",
    )(joint, joint, joint, probs, grad)


def place_halves(is_first, mine, other):
    return jnp.concatenate(
        [jnp.where(is_first, mine, other), jnp.where(is_first, other, mine)], axis=1
    )


def block_forward(seq, is_first, flights, classes, inputs, picks, between=lambda: None):
    count = inputs.shape[0] // P_SIZE
    first = seq.compute(place_halves, is_first, *seq.wait(flights["first"]))
    own = dot_nt(jnp.concatenate([picks, picks], axis=1), classes)
    hidden, normed_one, joint, norms = seq.compute(begin, inputs, own, first)
    attended, probs = seq.compute(attend, joint)
    middle, normed_two, sums_two = seq.compute(attention_end, attended, first, hidden, norms)
    ups = seq.wait(flights["up"])
    *actives, slope_one, slope_two = seq.compute(up_halves, normed_two, *ups)
    between()
    seq.turn()
    downs = seq.wait(flights["down"])
    final, normed_three, shrink, latent, sums = seq.compute(end, actives, downs, middle, norms, first, inputs)
    saved = dict(
        first=first, ups=ups, downs=downs, inputs=inputs, hidden=hidden, normed_one=normed_one, joint=joint,
        norms=norms, attended=attended, probs=probs, middle=middle, normed_two=normed_two, actives=actives,
        slopes=(slope_one, slope_two), final=final, normed_three=normed_three, shrink=shrink, latent=latent,
    )
    squares = jnp.stack([jnp.sum(sums[0]), jnp.sum(sums_two[0]), jnp.sum(sums[1]), jnp.sum(sums[2])])
    return saved, squares


def part_scattered(pieces, block, scattered):
    scattered = scattered.astype(F32)
    place = 0
    for name in BY_COLLECTIVE[block]:
        shape = pieces[name]["result"][0].shape
        height = shape[0] // lax.axis_size("dp")
        columns = []
        for _ in range(0, shape[1], D):
            columns.append(scattered[place : place + height])
            place += height
        pieces[name] = {"done": True, "result": jnp.concatenate(columns, axis=1)}


def block_backward(seq, section, block, saved, picks, latent_grad, coefficient, pieces):
    count = latent_grad.shape[0] // P_SIZE
    first, norms = saved["first"], saved["norms"]

    def launch(name, mine, given):
        if name in BY_COLLECTIVE[block] or (block, name) == SPLIT:
            pieces[name] = seq.launch(sum_pair(mine, given))
            return
        order = order_from(SCATTER_ORDERS, block, name)
        pieces[name] = seq.launch(scatter_steps(mine, given, order))

    def scatter_summed():
        rows = []
        for name in BY_COLLECTIVE[block]:
            mine, other = (value.reshape(lax.axis_size("dp"), -1, *value.shape[1:]) for value in pieces[name]["result"])
            total = (mine.astype(F32) + other.astype(F32)).astype(BF)
            rows += [total[:, :, start : start + D] for start in range(0, total.shape[2], D)]
        whole = jnp.concatenate(rows, axis=1)
        return lax.psum_scatter(seq.tie(whole), "dp", scatter_dimension=0, tiled=False)

    through, flow, low_final, head_grad, sums_three = seq.compute(
        lambda grad: head_back(
            coefficient, grad, saved["shrink"], saved["latent"], saved["final"], norms, first, saved["normed_three"]
        ),
        latent_grad,
    )
    launch("down", *seq.compute(down_grads, *saved["actives"], low_final))
    if block == 0:
        seq.turn()
    grad_one, grad_two, *up_grads = seq.compute(
        lambda low: up_back(low, saved["normed_two"], saved["downs"], saved["slopes"]), low_final
    )
    launch("up", *up_grads)
    if block == 1:
        seq.turn()
    wide_middle, low_middle, attended_grad, sums_two = seq.compute(
        lambda one, two: middle_back((one, two), saved["ups"], saved["middle"], norms, flow, first), grad_one, grad_two
    )
    if block == 0:
        seq.turn()
    joint_grad = seq.compute(attend_back, saved["joint"], saved["probs"], attended_grad)
    if block == 1:
        seq.turn()
        pieces["scattered"] = scatter_summed()
    low_hidden, input_grad, sums_one = seq.compute(
        lambda grad: input_back(grad, first, saved["hidden"], norms, wide_middle, through), joint_grad
    )
    places = jnp.tile(jnp.eye(P_SIZE, dtype=BF), (count, 1))
    sources = jnp.concatenate(
        [places, saved["inputs"].astype(BF), jnp.repeat(picks, P_SIZE, axis=0)], axis=1
    )
    sources = jnp.pad(sources, ((0, 0), (0, 128 + -(sources.shape[1] + 128) % 512)))
    launch(
        "first",
        *seq.compute(
            lambda low: first_grads(
                section, saved["normed_one"], saved["attended"], low, joint_grad, low_middle, sources, head_grad,
                (sums_one, sums_two, sums_three),
            ),
            low_hidden,
        ),
    )
    return input_grad


def body(*arguments):
    images, noise_draw, labels, class_drop = arguments[:4]
    weights, moments, squares = arguments[4:12], arguments[12:20], arguments[20:28]
    w_qkv, w_attn, w_up, w_down, w_in, w_head, w_embed, w_norms = (w[0] for w in weights)
    count_dp = lax.axis_size("dp")
    section = lax.axis_index("section")
    is_first = section == 0
    dp_index = lax.axis_index("dp")
    per_chip = images.shape[0]
    per_core = per_chip // 2
    total_images = per_chip * count_dp
    width = w_qkv.shape[0]
    ff_width = w_down.shape[0]
    coefficient = 1.0 / (total_images * P_SIZE * PD * math.log(2.0))
    seq = Sequencer()

    position = jnp.concatenate(two_terms(w_embed[:P_SIZE]), axis=0)
    small = jnp.concatenate(
        [
            position.T,
            w_head.astype(BF),
            jnp.pad(jnp.concatenate(three_terms(w_norms), axis=0), ((0, S_IN - S_NORM - 18), (0, 0))).T,
            jnp.pad(w_in.astype(BF), ((0, S_WIDTH - S_IN - PD), (0, 0))).T,
        ],
        axis=1,
    )
    first = jnp.concatenate([small, w_qkv.astype(BF), w_attn.astype(BF)], axis=1)
    up_units = w_up.astype(BF).reshape(width, count_dp, 2, ff_width // 2)
    own_halves = dict(
        first=(first[:, : FIRST_WIDTH // 2], first[:, FIRST_WIDTH // 2 :]),
        up=tuple(up_units[:, :, half].reshape(width, FF // 2) for half in range(2)),
        down=(w_down[: ff_width // 2].astype(BF), w_down[ff_width // 2 :].astype(BF)),
    )
    label_flight = seq.launch(label_steps(labels))
    starts = [seq.launch(one_step(jnp.where(is_first, right, left), "section")) for left, right in own_halves.values()]
    seq.turn()
    seq.turn()
    parts = ({}, {})
    for (name, (left, right)), start in zip(own_halves.items(), starts):
        taken = start["result"]
        parts[0][name] = jnp.where(is_first, left, taken)
        parts[1][name] = jnp.where(is_first, taken, right)
    flat = jnp.concatenate([parts[1]["first"], parts[1]["up"], down_columns(parts[1]["down"], width)], axis=1)
    gathered = lax.all_gather(seq.tie(flat), "dp", axis=0, tiled=True)
    flights = {
        name: seq.launch(weight_steps(parts[0][name], order_from(GATHER_ORDERS, 0, name))) for name in own_halves
    }
    all_labels = seq.wait(label_flight)
    named = (jnp.arange(CLS)[:, None] == all_labels[None, :]).astype(BF)
    own_classes = [dot_tn(term, named).astype(BF) for term in two_terms(w_embed[P_SIZE:])]
    class_flight = seq.launch(
        class_steps(jnp.concatenate(own_classes, axis=1), is_first, tuple(range(dp_bits())))
    )
    classes = seq.wait(class_flight)
    classes_of = (classes[:, : 2 * total_images], classes[:, 2 * total_images :])

    start = section * per_core
    own_images = lax.dynamic_slice_in_dim(images, start, per_core, 0)
    own_noise = lax.dynamic_slice_in_dim(noise_draw, start, per_core, 0)
    keep = (1 - lax.dynamic_slice_in_dim(class_drop, start, per_core, 0)).astype(F32)
    inputs = (own_images + NOISE_SCALE * own_noise).reshape(per_core * P_SIZE, PD)

    def reverse(rows):
        return rows.reshape(per_core, P_SIZE, PD)[:, ::-1].reshape(per_core * P_SIZE, PD)

    image_ids = dp_index * per_chip + start + jnp.arange(per_core)
    picks = jnp.where(jnp.arange(total_images)[None, :] == image_ids[:, None], keep[:, None], 0.0).astype(BF)
    later = {}

    def split_gathered():
        whole = seq.tie(gathered)
        edge = FIRST_WIDTH // 2
        later["first"] = seq.launch(one_pair(whole[:, :edge]))
        later["up"] = seq.launch(one_pair(whole[:, edge : edge + FF // 2]))
        later["down"] = seq.launch(one_pair(down_rows(whole[:, edge + FF // 2 :], width)))

    saved_zero, sums_zero = block_forward(
        seq, is_first, flights, classes_of[0], inputs, picks, split_gathered
    )
    flights = later
    saved_one, sums_one = block_forward(
        seq, is_first, flights, classes_of[1], reverse(saved_zero["latent"]), picks
    )
    latent_one = saved_one["latent"]
    loss_local = 0.5 * jnp.sum(latent_one * latent_one) + sums_zero[3] + sums_one[3]

    pieces = ({}, {})
    grad_one = block_backward(
        seq, section, 1, saved_one, picks, coefficient * latent_one, coefficient, pieces[1]
    )
    block_backward(seq, section, 0, saved_zero, picks, reverse(grad_one), coefficient, pieces[0])

    while not pieces[0]["first"]["done"]:
        seq.turn()
    both = pieces[0]["first"]["result"]
    half = both[0].shape[1] // 2
    last = [
        seq.launch(
            scatter_both(
                [value[:, part * half : (part + 1) * half] for value in both],
                order_from(SCATTER_ORDERS, 0, ("first", "last")[part]),
            )
        )
        for part in range(2)
    ]
    pieces[0]["first"] = {"done": True, "result": jnp.concatenate(seq.wait(*last), axis=1)}
    part_scattered(pieces[1], 1, seq.tie(pieces[1]["scattered"]))

    own = {}
    for name in ("down", "up", "first"):
        one, zero = seq.wait(pieces[1][name], pieces[0][name])
        kept = jnp.where(is_first, zero, one)
        own[name] = (kept, seq.launch(one_step(jnp.where(is_first, one, zero), "section")))
    for name, (kept, flight) in own.items():
        other = seq.wait(flight)
        own[name] = (jnp.where(is_first, kept, other), jnp.where(is_first, other, kept))
    first = jnp.concatenate(own["first"], axis=1)
    small = first[:, QKV + D :]
    rest = small.shape[1] - 128
    class_at = P_SIZE + PD
    class_rows = lax.dot_general(
        named.astype(F32),
        small[:, class_at : class_at + total_images],
        (((1,), (1,)), ((), ())),
        precision=lax.Precision.HIGHEST,
        preferred_element_type=F32,
    )
    up_grad = jnp.stack([half.reshape(width, count_dp, ff_width // 2) for half in own["up"]], axis=2)
    shards = (
        first[:, :QKV],
        first[:, QKV : QKV + D],
        up_grad.reshape(width, FF),
        jnp.concatenate(own["down"], axis=0),
        small[:, P_SIZE : P_SIZE + PD].T,
        small[:, rest : rest + 2 * PD],
        jnp.concatenate([small[:, :P_SIZE].T, class_rows], axis=0),
        small[:, rest + 2 * PD : rest + 2 * PD + 6].T,
    )
    square_local = sum(jnp.sum(shard * shard) for shard in shards)
    totals = jnp.concatenate([sums_zero[:3], sums_one[:3], jnp.stack([loss_local, square_local])])[None]
    totals = seq.wait(seq.launch(sum_steps(totals)))[0]
    loss_sum = totals[6] + seq.token
    grad_norm = jnp.sqrt(totals[7])
    activity = jnp.sqrt(totals[:6].reshape(2, 3) / (total_images * P_SIZE * D))
    factor = jnp.minimum(1.0, CLIP_NORM / grad_norm)
    new_moments, new_squares, new_weights = ([], [], [])
    for weight, moment, square, shard, rate in zip(weights, moments, squares, shards, LEARN_RATES):
        clipped = shard[None] * factor
        moment_next = BETA_ONE * moment + (1 - BETA_ONE) * clipped
        square_next = BETA_TWO * square + (1 - BETA_TWO) * clipped * clipped
        update = (
            moment_next
            / (1 - BETA_ONE**STEP)
            / (jnp.sqrt(square_next / (1 - BETA_TWO**STEP)) + EPS_ADAM)
        )
        new_moments.append(moment_next)
        new_squares.append(square_next)
        new_weights.append(weight - rate * (update + WEIGHT_DECAY * weight))
    return (*new_moments, *new_squares, *new_weights, loss_sum, grad_norm, activity)


def solution(mesh):
    by_row = P("section", "dp", None)
    by_column = P("section", None, "dp")
    weight_specs = (by_row, by_row, by_row, by_row, by_column, by_row, by_column, by_column)
    return jax.shard_map(
        body,
        mesh=mesh,
        in_specs=(P("dp", None, None), P("dp", None, None), P("dp"), P("dp")) + weight_specs * 3,
        out_specs=weight_specs * 3 + (P(), P(), P()),
        check_vma=False,
    )
```

```python
import math

import jax
import jax.numpy as jnp
from jax import lax
from jax.experimental import pallas as pl
from jax.experimental.pallas import tpu as pltpu
from jax.sharding import PartitionSpec as P

D = 768
H = 12
HD = 64
FF = 3072
PD = 48
CLS = 1000
P_SIZE = 256
STEP = 10
QKV = 3 * D

EPS_NORM = 1e-05
NOISE_SCALE = 0.05
CLIP_NORM = 0.001
BETA_ONE = 0.9
BETA_TWO = 0.95
LEARN_RATES = (0.01, 0.06, 0.01, 0.01, 0.08, 0.01, 0.25, 0.4)
WEIGHT_DECAY = 0.1
EPS_ADAM = 1e-10

BF = jnp.bfloat16
F32 = jnp.float32

S_HEAD = 2 * P_SIZE
S_NORM = S_HEAD + 2 * PD
S_IN = S_HEAD + 128
S_WIDTH = 768
FIRST_WIDTH = S_WIDTH + QKV + D
PAIR = 2 * HD
PAIRS = H // 2
TILE = D
FF_HALF = FF // 2
VMEM_BYTES = 30 << 20


def swap_pairs(count, bit):
    mask = bit[0] if isinstance(bit, tuple) else 1 << bit
    return [(source, source ^ mask) for source in range(count)]


def exchange(value, axis, bit=0):
    return lax.ppermute(value, axis, swap_pairs(lax.axis_size(axis), bit))


def dp_bits():
    return lax.axis_size("dp").bit_length() - 1


def parity_of(bit):
    return (lax.axis_index("dp") >> bit) & 1


GATHER_ORDERS = ({"first": (0, 1, 2, 3), "up": (1, 2, 3, 0), "down": (2, 0, 1, 3)},)
SCATTER_ORDERS = (
    {"down": (2, 0, 1, 3), "up": (1, 2, 0, 3), "first": (0, 1, 2, 3), "last": (1, 2, 0, 3)},
    {"down": (0, 2, 1, 3), "up": (1, 0, 2, 3), "first": (0, 1, 2, 3)},
)


SPLIT = (0, "first")


def order_from(table, block, name):
    count = dp_bits()
    if count == 4:
        return table[block][name]
    first = {"first": 0, "up": 1, "down": 2, "last": 1}[name]
    return tuple((first + step) % count for step in range(count))


class Sequencer:
    def __init__(self):
        self.flights = []
        self.asked = []
        self.token = jnp.zeros((), F32)

    def tie(self, tree):
        leaves, kind = jax.tree.flatten(tree)
        tied = lax.optimization_barrier([self.token] + leaves)
        self.token = tied[0]
        return jax.tree.unflatten(kind, tied[1:])

    def launch(self, steps):
        flight = {"steps": steps, "done": False}
        self.asked.append((flight, next(steps)))
        return flight

    def turn(self):
        requests = []
        for flight, got in zip(self.flights, self.tie([flight["got"] for flight in self.flights])):
            try:
                requests.append((flight, flight["steps"].send(got)))
            except StopIteration as stop:
                flight["done"] = True
                flight["result"] = stop.value
        requests += self.asked
        values = self.tie([value for _, (value, _, _) in requests])
        self.flights, self.asked = [], []
        for value, (flight, (_, axis, bit)) in zip(values, requests):
            flight["got"] = exchange(value, axis, bit)
            self.flights.append(flight)

    def wait(self, *flights):
        while not all(flight["done"] for flight in flights):
            self.turn()
        return flights[0]["result"] if len(flights) == 1 else [f["result"] for f in flights]

    def compute(self, function, *values):
        return self.tie(function(*self.tie(values)))


def gather_steps(part, order):
    have = []
    held = part
    for bit in reversed(order):
        other = yield (held, "dp", bit)
        place = sum(1 for b in have if b > bit)
        swap = parity_of(bit) == 1
        held = jnp.stack([jnp.where(swap, other, held), jnp.where(swap, held, other)], axis=place)
        have.append(bit)
    return held.reshape((-1,) + part.shape[1:])


def weight_steps(part, order):
    mine = yield from gather_steps(part, order)
    other = yield (mine, "section", 0)
    return mine, other


def pair_steps(mine):
    other = yield (mine, "section", 0)
    return mine, other


def part_of(value, axis_index):
    starts = [axis_index.get(axis, 0) for axis in range(value.ndim)]
    sizes = [1 if axis in axis_index else extent for axis, extent in enumerate(value.shape)]
    sliced = lax.dynamic_slice(value, starts, sizes)
    return sliced.reshape([extent for axis, extent in enumerate(sizes) if axis not in axis_index])


def scatter_steps(mine, given, order):
    other = yield (given, "section", 0)
    result = yield from scatter_both((mine, other), order)
    return result


def scatter_both(both, order):
    count = dp_bits()
    rows = both[0].shape[0] >> count
    held = [value.reshape((2,) * count + (rows,) + value.shape[1:]) for value in both]
    left = sorted(range(count), reverse=True)
    chosen = [{} for _ in held]

    def piece(axis, index):
        parts = []
        for value, fixed in zip(held, chosen):
            free = [place for place in range(value.ndim) if place not in fixed]
            parts.append(part_of(value, {**fixed, free[axis]: index}).astype(F32))
        return sum(parts[1:], parts[0])

    for bit in order:
        axis = left.index(bit)
        parity = parity_of(bit)
        other = yield (piece(axis, 1 - parity).astype(BF), "dp", bit)
        for value, fixed in zip(held, chosen):
            free = [place for place in range(value.ndim) if place not in fixed]
            fixed[free[axis]] = parity
        if len(held) > 1:
            kept = sum(part_of(value, fixed).astype(F32) for value, fixed in zip(held, chosen))
            held, chosen = [kept.astype(BF)], [{}]
        held.append(other)
        chosen.append({})
        left.remove(bit)
    return sum(part_of(value, fixed).astype(F32) for value, fixed in zip(held, chosen))


def one_step(value, axis, bit=0):
    got = yield (value, axis, bit)
    return got


def sum_pair(mine, given):
    other = yield (given, "section", 0)
    return mine, other


def label_steps(nearby):
    high = dp_bits() - 2
    own = lax.axis_index("dp") >> high
    rows = [sum(jnp.where((own ^ step) == at, value, 0) for step, value in enumerate(nearby)) for at in range(4)]
    held = jnp.stack(rows)
    for bit in range(high - 1, -1, -1):
        other = yield (held, "dp", bit)
        swap = parity_of(bit) == 1
        place = high - bit
        held = jnp.stack([jnp.where(swap, other, held), jnp.where(swap, held, other)], axis=place)
    return held.reshape(-1)


def class_steps(own, is_first, order):
    other = yield (own, "section", 0)
    both = jnp.concatenate([jnp.where(is_first, own, other), jnp.where(is_first, other, own)], axis=1)
    whole = yield from gather_steps(both, order)
    return whole


def class_rows_of(named, columns):
    return lax.dot_general(
        named.astype(F32), columns, (((1,), (1,)), ((), ())),
        precision=lax.Precision.HIGHEST, preferred_element_type=F32,
    )


def sum_steps(values):
    other = yield (values, "section", 0)
    values = values + other
    for bit in range(dp_bits()):
        other = yield (values, "dp", bit)
        values = values + other
    return values


def dot(left, right):
    return lax.dot_general(left, right, (((1,), (0,)), ((), ())), preferred_element_type=F32)


def dot_nt(left, right):
    return lax.dot_general(left, right, (((1,), (1,)), ((), ())), preferred_element_type=F32)


def dot_tn(left, right):
    return lax.dot_general(left, right, (((0,), (0,)), ((), ())), preferred_element_type=F32)


def two_terms(value):
    high = lax.optimization_barrier(value.astype(BF))
    return high, (value - high.astype(F32)).astype(BF)


def three_terms(value):
    high = lax.optimization_barrier(value.astype(BF))
    return (high,) + two_terms(value - high.astype(F32))


def whole_spec(*shape):
    return pl.BlockSpec(shape, lambda *_: (0,) * len(shape))


def row_spec(width):
    return pl.BlockSpec((P_SIZE, width), lambda j: (j, 0))


def first_spec(index):
    return pl.BlockSpec((D, D), lambda *_: (0, index))


HEAD_SPEC = pl.BlockSpec((D, 128), lambda *_: (0, S_HEAD // 128))
IN_SPEC = pl.BlockSpec((D, 128), lambda *_: (0, S_IN // 128))


def half_spec(part):
    return pl.BlockSpec((D, FF_HALF), lambda *_: (0, part[1] // STEPS))


def shape_of(rows, columns, kind=F32):
    return jax.ShapeDtypeStruct((rows, columns), kind)


def call(kernel, name, flops, **fields):
    return pl.pallas_call(
        kernel,
        name=name,
        cost_estimate=pl.CostEstimate(flops=flops, bytes_accessed=flops // 256, transcendentals=0),
        compiler_params=pltpu.CompilerParams(vmem_limit_bytes=VMEM_BYTES),
        **fields,
    )


def iotas(rows, columns):
    return (
        lax.broadcasted_iota(jnp.int32, (rows, columns), 0),
        lax.broadcasted_iota(jnp.int32, (rows, columns), 1),
    )


def where_ones(condition):
    return jnp.where(condition, 1.0, 0.0).astype(BF)


def norm_parts(values):
    center = values - jnp.mean(values, axis=-1, keepdims=True)
    scale = lax.rsqrt(jnp.mean(center * center, axis=-1, keepdims=True) + EPS_NORM)
    return center, scale


def norm_rows(values, norms, which):
    center, scale = norm_parts(values)
    return (center * scale * norms[2 * which : 2 * which + 1] + norms[2 * which + 1 : 2 * which + 2]).astype(BF)


def norm_back_rows(values, norms, which, cotangent):
    center, scale = norm_parts(values)
    unit = center * scale
    inner = cotangent * norms[2 * which : 2 * which + 1]
    first = jnp.mean(inner, axis=-1, keepdims=True)
    second = jnp.mean(inner * unit, axis=-1, keepdims=True)
    gain_grad = jnp.sum(cotangent * unit, axis=0, keepdims=True)
    offset_grad = jnp.sum(cotangent, axis=0, keepdims=True)
    return scale * (inner - first - unit * second), gain_grad, offset_grad


def add_sums(sums_ref, *rows):
    @pl.when(pl.program_id(0) == 0)
    def _():
        sums_ref[...] = jnp.zeros_like(sums_ref)

    for index, row in enumerate(rows):
        sums_ref[index : index + 1, :] += row


def reversed_rows(values):
    row, column = iotas(P_SIZE, P_SIZE)
    turn = where_ones(row + column == P_SIZE - 1)
    high = values.astype(BF)
    rest = values - high.astype(F32)
    middle = rest.astype(BF)
    low = (rest - middle.astype(F32)).astype(BF)
    return dot(turn, high) + dot(turn, middle) + dot(turn, low)


def begin_kernel(x_ref, class_ref, small_ref, q_ref, k_ref, v_ref, hidden_ref, normed_ref, joint_ref, norms_ref):
    row, column = iotas(P_SIZE, P_SIZE)
    same = where_ones(row == column)
    hidden = dot_nt(same, small_ref[:, :P_SIZE]) + dot_nt(same, small_ref[:, P_SIZE:S_HEAD])
    hidden = hidden + dot_nt(x_ref[...].astype(BF), small_ref[:, S_IN : S_IN + PD])
    hidden = hidden + class_ref[pl.ds(pl.program_id(0), 1), :]
    row, column = iotas(8, 128)
    place = column - 2 * PD
    term = where_ones((row < 6) & ((place == row) | (place == row + 6) | (place == row + 12)))
    norms = dot_nt(term, small_ref[:, S_HEAD : S_HEAD + 128])
    hidden_ref[...] = hidden
    norms_ref[...] = norms
    normed = norm_rows(hidden, norms, 0)
    normed_ref[...] = normed
    for part, weight_ref in enumerate((q_ref, k_ref, v_ref)):
        joint_ref[:, part * D : (part + 1) * D] = dot(normed, weight_ref[...]).astype(BF)


def begin(inputs, classes, first):
    rows = inputs.shape[0]
    return call(
        begin_kernel,
        "embed_norm_project",
        2 * rows * D * 4 * D,
        grid=(rows // P_SIZE,),
        in_specs=[row_spec(PD), whole_spec(*classes.shape)] + [first_spec(part) for part in range(4)],
        out_specs=[row_spec(D), row_spec(D), row_spec(QKV), whole_spec(8, D)],
        out_shape=[shape_of(rows, D), shape_of(rows, D, BF), shape_of(rows, QKV, BF), shape_of(8, D)],
    )(inputs, classes, first, first, first, first)


def attention_end_kernel(attended_ref, weight_ref, hidden_ref, norms_ref, middle_ref, normed_ref, sums_ref):
    branch = dot(attended_ref[...], weight_ref[...])
    middle = hidden_ref[...] + branch
    middle_ref[...] = middle
    normed_ref[...] = norm_rows(middle, norms_ref[...], 1)
    add_sums(sums_ref, jnp.sum(branch * branch, axis=0, keepdims=True))


def attention_end(attended, first, hidden, norms):
    rows = attended.shape[0]
    return call(
        attention_end_kernel,
        "attention_end",
        2 * rows * D * D,
        grid=(rows // P_SIZE,),
        in_specs=[row_spec(D), first_spec(4), row_spec(D), whole_spec(8, D)],
        out_specs=[row_spec(D), row_spec(D), whole_spec(8, D)],
        out_shape=[shape_of(rows, D), shape_of(rows, D, BF), shape_of(8, D)],
    )(attended, first, hidden, norms)


STEPS = FF_HALF // TILE


def at_one(j):
    return jnp.minimum(j, STEPS - 1)


def at_two(j):
    return jnp.maximum(j - STEPS, 0)


def tile_specs(rows, starts=(0, 0)):
    return [
        pl.BlockSpec((rows, TILE), lambda j: (0, starts[0] + at_one(j))),
        pl.BlockSpec((rows, TILE), lambda j: (0, starts[1] + at_two(j))),
    ]


def up_kernel(x_ref, one_ref, two_ref, active_one, active_two, slope_one, slope_two):
    def half(weight_ref, active_ref, slope_ref):
        u = dot(x_ref[...], weight_ref[...])
        t = pl.reciprocal(1.0 + (0.3275911 / math.sqrt(2.0)) * jnp.abs(u), approx=True)
        bell = jnp.exp(-0.5 * u * u)
        poly = t * (0.127414796 + t * (-0.142248368 + t * (0.7107068705 + t * (-0.7265760135 + t * 0.5307027145))))
        tail = poly * bell
        share = jnp.where(u >= 0, 1.0 - tail, tail)
        active_ref[...] = (u * share).astype(BF)
        slope_ref[...] = (share + u * bell * (1.0 / math.sqrt(2.0 * math.pi))).astype(BF)

    @pl.when(pl.program_id(0) < STEPS)
    def _():
        half(one_ref, active_one, slope_one)

    @pl.when(pl.program_id(0) >= STEPS)
    def _():
        half(two_ref, active_two, slope_two)


def up_halves(normed, one, two):
    rows = normed.shape[0]
    return call(
        up_kernel,
        "up_gelu",
        4 * rows * D * FF_HALF,
        grid=(2 * STEPS,),
        in_specs=[whole_spec(rows, D)] + tile_specs(D, (one[1], two[1])),
        out_specs=tile_specs(rows) * 2,
        out_shape=[shape_of(rows, FF_HALF, BF)] * 4,
    )(normed, one[0], two[0])


def end_kernel(
    active_one, active_two, down_one, down_two, middle_ref, norms_ref, head_ref, x_ref,
    final_ref, normed_ref, shrink_ref, latent_ref, turned_ref, sums_ref,
):
    branch = sum(
        dot(active_ref[:, part * D : (part + 1) * D], down_ref[:, part * D : (part + 1) * D])
        for active_ref, down_ref in ((active_one, down_one), (active_two, down_two))
        for part in range(STEPS)
    )
    final = middle_ref[...] + branch
    final_ref[...] = final
    normed = norm_rows(final, norms_ref[...], 2)
    normed_ref[...] = normed
    head_out = dot(normed, head_ref[...])
    row, _ = iotas(P_SIZE, 128)
    moved = jnp.where(row == 0, 0.0, pltpu.roll(head_out, 1, 0))
    log_scale = moved[:, PD : 2 * PD]
    shrink = jnp.exp(-log_scale)
    shrink_ref[...] = shrink
    latent = (x_ref[...] - moved[:, :PD]) * shrink
    latent_ref[...] = latent
    turned_ref[...] = reversed_rows(latent)
    _, lane = iotas(1, D)
    add_sums(
        sums_ref,
        jnp.sum(final * final, axis=0, keepdims=True),
        jnp.sum(branch * branch, axis=0, keepdims=True),
        jnp.where(lane == 0, jnp.sum(log_scale), 0.0) + jnp.where(lane == 1, 0.5 * jnp.sum(latent * latent), 0.0),
    )


def end(actives, downs, middle, norms, first, inputs):
    rows = middle.shape[0]
    return call(
        end_kernel,
        "down_norm_head",
        4 * rows * D * FF_HALF,
        grid=(rows // P_SIZE,),
        in_specs=[row_spec(FF_HALF)] * 2
        + [half_spec(down) for down in downs]
        + [row_spec(D), whole_spec(8, D), HEAD_SPEC, row_spec(PD)],
        out_specs=[row_spec(D), row_spec(D)] + [row_spec(PD)] * 3 + [whole_spec(8, D)],
        out_shape=[shape_of(rows, D), shape_of(rows, D, BF)] + [shape_of(rows, PD)] * 3 + [shape_of(8, D)],
    )(*actives, *(down for down, _ in downs), middle, norms, first, inputs)


def head_back_kernel(
    coefficient, last, latent_grad_ref, shrink_ref, latent_ref, final_ref, norms_ref, head_ref, normed_ref,
    through_ref, flow_ref, low_ref, weight_ref, sums_ref,
):
    latent_grad = coefficient * latent_ref[...] if last else latent_grad_ref[...]
    through = latent_grad * shrink_ref[...]
    through_ref[...] = through
    scale_grad = coefficient - latent_grad * latent_ref[...]
    row, column = iotas(PD, 128)
    placed = dot((-through).astype(BF), where_ones(row == column))
    placed = placed + dot(scale_grad.astype(BF), where_ones(row + PD == column))
    row, _ = iotas(P_SIZE, 128)
    head_grad = jnp.where(row == P_SIZE - 1, 0.0, pltpu.roll(placed, P_SIZE - 1, 0)).astype(BF)
    flow, gain_grad, offset_grad = norm_back_rows(
        final_ref[...], norms_ref[...], 2, dot_nt(head_grad, head_ref[...])
    )
    flow_ref[...] = flow
    low_ref[...] = flow.astype(BF)

    @pl.when(pl.program_id(0) == 0)
    def _():
        weight_ref[...] = jnp.zeros_like(weight_ref)

    weight_ref[...] += dot_tn(normed_ref[...], head_grad)
    add_sums(sums_ref, gain_grad, offset_grad)


def head_back(coefficient, last, latent_grad, shrink, latent, final, norms, first, normed):
    rows = final.shape[0]
    return call(
        lambda *refs: head_back_kernel(coefficient, last, *refs),
        "head_back",
        4 * rows * D * 128,
        grid=(rows // P_SIZE,),
        in_specs=[row_spec(PD)] * 3 + [row_spec(D), whole_spec(8, D), HEAD_SPEC, row_spec(D)],
        out_specs=[row_spec(PD), row_spec(D), row_spec(D), whole_spec(D, 128), whole_spec(8, D)],
        out_shape=[
            shape_of(rows, PD), shape_of(rows, D), shape_of(rows, D, BF), shape_of(D, 128), shape_of(8, D)
        ],
    )(latent_grad, shrink, latent, final, norms, first, normed)


def down_grad_kernel(one_ref, two_ref, low_ref, out_one, out_two):
    @pl.when(pl.program_id(0) < STEPS)
    def _():
        out_one[...] = dot_tn(one_ref[...], low_ref[...]).astype(BF)

    @pl.when(pl.program_id(0) >= STEPS)
    def _():
        out_two[...] = dot_tn(two_ref[...], low_ref[...]).astype(BF)


def down_grads(one, two, low):
    rows = low.shape[0]
    return call(
        down_grad_kernel,
        "down_weight_grad",
        4 * rows * D * FF_HALF,
        grid=(2 * STEPS,),
        in_specs=tile_specs(rows) + [whole_spec(rows, D)],
        out_specs=tile_specs(D),
        out_shape=[shape_of(D, FF_HALF, BF)] * 2,
    )(one, two, low)


def up_back_kernel(low_ref, normed_ref, *refs):
    *refs, turned_ref = refs

    @pl.when(pl.program_id(0) == 0)
    def _():
        turned_ref[...] = normed_ref[...].T

    def half(weight_ref, slope_ref, grad_ref, out_ref):
        grad = (dot_nt(low_ref[...], weight_ref[...]) * slope_ref[...].astype(F32)).astype(BF)
        grad_ref[...] = grad
        out_ref[...] = dot(turned_ref[...], grad).astype(BF)

    @pl.when(pl.program_id(0) < STEPS)
    def _():
        half(*refs[0::2])

    @pl.when(pl.program_id(0) >= STEPS)
    def _():
        half(*refs[1::2])


def up_back(low, normed, downs, slopes):
    rows = low.shape[0]
    return call(
        up_back_kernel,
        "up_back",
        8 * rows * D * FF_HALF,
        grid=(2 * STEPS,),
        in_specs=[whole_spec(rows, D)] * 2 + tile_specs(D, [start for _, start in downs]) + tile_specs(rows),
        out_specs=tile_specs(rows) + tile_specs(D),
        out_shape=[shape_of(rows, FF_HALF, BF)] * 2 + [shape_of(D, FF_HALF, BF)] * 2,
        scratch_shapes=[pltpu.VMEM((D, rows), BF)],
    )(low, normed, *(down for down, _ in downs), *slopes)


def middle_back_kernel(
    one_ref, two_ref, up_one, up_two, middle_ref, norms_ref, above_ref, weight_ref,
    wide_ref, low_ref, attended_ref, sums_ref,
):
    back = dot_nt(one_ref[...], up_one[...]) + dot_nt(two_ref[...], up_two[...])
    flow, gain_grad, offset_grad = norm_back_rows(middle_ref[...], norms_ref[...], 1, back)
    total = above_ref[...] + flow
    wide_ref[...] = total
    low = total.astype(BF)
    low_ref[...] = low
    attended_ref[...] = dot_nt(low, weight_ref[...]).astype(BF)
    add_sums(sums_ref, gain_grad, offset_grad)


def middle_back(grads, ups, middle, norms, above, first):
    rows = middle.shape[0]
    return call(
        middle_back_kernel,
        "middle_back",
        4 * rows * D * FF_HALF,
        grid=(rows // P_SIZE,),
        in_specs=[row_spec(FF_HALF)] * 2
        + [half_spec(up) for up in ups]
        + [row_spec(D), whole_spec(8, D), row_spec(D), first_spec(4)],
        out_specs=[row_spec(D), row_spec(D), row_spec(D), whole_spec(8, D)],
        out_shape=[shape_of(rows, D), shape_of(rows, D, BF), shape_of(rows, D, BF), shape_of(8, D)],
    )(*grads, *(up for up, _ in ups), middle, norms, above, first)


def input_back_kernel(
    joint_ref, q_ref, k_ref, v_ref, hidden_ref, norms_ref, above_ref, in_ref, through_ref, low_ref, out_ref, sums_ref
):
    back = sum(
        dot_nt(joint_ref[:, part * D : (part + 1) * D], weight_ref[...])
        for part, weight_ref in enumerate((q_ref, k_ref, v_ref))
    )
    flow, gain_grad, offset_grad = norm_back_rows(hidden_ref[...], norms_ref[...], 0, back)
    low = (above_ref[...] + flow).astype(BF)
    low_ref[...] = low
    out_ref[...] = reversed_rows(through_ref[...] + dot(low, in_ref[...])[:, :PD])
    add_sums(sums_ref, gain_grad, offset_grad)


def input_back(joint_grad, first, hidden, norms, above, through):
    rows = hidden.shape[0]
    return call(
        input_back_kernel,
        "input_back",
        2 * rows * D * QKV,
        grid=(rows // P_SIZE,),
        in_specs=[row_spec(QKV)]
        + [first_spec(part) for part in range(1, 4)]
        + [row_spec(D), whole_spec(8, D), row_spec(D), IN_SPEC, row_spec(PD)],
        out_specs=[row_spec(D), row_spec(PD), whole_spec(8, D)],
        out_shape=[shape_of(rows, D, BF), shape_of(rows, PD), shape_of(8, D)],
    )(joint_grad, first, first, first, hidden, norms, above, first, through)


COLUMNS = 256
SOURCE_AT = (QKV + D) // COLUMNS


def first_grad_kernel(
    steps, section_ref, normed_ref, attended_ref, low_ref, joint_ref, middle_ref, source_ref, head_ref,
    sums_one, sums_two, sums_three, mine_ref, given_ref, turned_ref,
):
    step = pl.program_id(0)
    for at, left_ref in ((0, normed_ref), (QKV // COLUMNS, attended_ref), (SOURCE_AT, low_ref)):

        @pl.when(step == at)
        def _(left_ref=left_ref):
            turned_ref[...] = left_ref[...].T

    to_mine = (step >= steps // 2) == (section_ref[0] == 1)

    def put(value):
        @pl.when(to_mine)
        def _():
            mine_ref[...] = value

        @pl.when(jnp.logical_not(to_mine))
        def _():
            given_ref[...] = value

    @pl.when(step < QKV // COLUMNS)
    def _():
        put(dot(turned_ref[...], joint_ref[...]).astype(BF))

    @pl.when((step >= QKV // COLUMNS) & (step < SOURCE_AT))
    def _():
        put(dot(turned_ref[...], middle_ref[...]).astype(BF))

    @pl.when((step >= SOURCE_AT) & (step < steps - 1))
    def _():
        put(dot(turned_ref[...], source_ref[...]).astype(BF))

    @pl.when(step == steps - 1)
    def _():
        row, column = iotas(8, 128)
        rest = head_ref[...]
        for which, sums_ref in enumerate((sums_one, sums_two, sums_three)):
            place = where_ones((row < 2) & (column == row + 2 * PD + 2 * which))
            rest = rest + dot_tn(sums_ref[...].astype(BF), place)
        source = dot(turned_ref[...], source_ref[:, :128])
        put(jnp.concatenate([source, rest], axis=1).astype(BF))


def first_grads(section, normed, attended, low, joint_grad, low_middle, sources, head, sums):
    rows = normed.shape[0]
    steps = SOURCE_AT + sources.shape[1] // COLUMNS
    half = steps // 2

    def tile(offset, count):
        return pl.BlockSpec((rows, COLUMNS), lambda j, s: (0, jnp.clip(j - offset, 0, count - 1)))

    whole = pl.BlockSpec((rows, D), lambda j, s: (0, 0))
    small = pl.BlockSpec((8, D), lambda j, s: (0, 0))
    return call(
        lambda *refs: first_grad_kernel(steps, *refs),
        "first_weight_grad",
        2 * rows * D * (QKV + D + sources.shape[1]),
        grid_spec=pltpu.PrefetchScalarGridSpec(
            num_scalar_prefetch=1,
            grid=(steps,),
            in_specs=[
                whole,
                whole,
                whole,
                tile(0, QKV // COLUMNS),
                tile(QKV // COLUMNS, D // COLUMNS),
                tile(SOURCE_AT, sources.shape[1] // COLUMNS),
                pl.BlockSpec((D, 128), lambda j, s: (0, 0)),
                small,
                small,
                small,
            ],
            out_specs=[
                pl.BlockSpec((D, COLUMNS), lambda j, s: (0, jnp.clip(j - half * s[0], 0, half - 1))),
                pl.BlockSpec((D, COLUMNS), lambda j, s: (0, jnp.clip(j - half * (1 - s[0]), 0, half - 1))),
            ],
            scratch_shapes=[pltpu.VMEM((D, rows), BF)],
        ),
        out_shape=[shape_of(D, half * COLUMNS, BF)] * 2,
    )(section[None].astype(jnp.int32), normed, attended, low, joint_grad, low_middle, sources, head, *sums)


def head_mask(which, axis, scale=1.0):
    shape = (1, PAIR) if axis == 1 else (PAIR, 1)
    place = lax.broadcasted_iota(jnp.int32, shape, axis)
    return jnp.where((place >= HD * which) & (place < HD * (which + 1)), scale, 0.0).astype(BF)


def attend_kernel(q_ref, k_ref, v_ref, out_ref, probs_ref):
    queries, key_rows = q_ref[...], k_ref[...]
    values_t = v_ref[...].T
    key_at = lax.broadcasted_iota(jnp.int32, (P_SIZE, P_SIZE), 0)
    query_at = lax.broadcasted_iota(jnp.int32, (P_SIZE, P_SIZE), 1)
    causal = key_at <= query_at
    total = jnp.zeros((PAIR, P_SIZE), F32)
    for which in range(2):
        scores = dot_nt(key_rows, queries * head_mask(which, 1, HD ** (-0.5)))
        scores = jnp.where(causal, scores, -1e30)
        exps = jnp.exp(scores - jnp.max(scores, axis=0, keepdims=True))
        probs = (exps * (1.0 / jnp.sum(exps, axis=0, keepdims=True))).astype(BF)
        probs_ref[0, which] = probs
        total = total + dot(values_t * head_mask(which, 0), probs)
    out_ref[...] = total.T.astype(BF)


def attend(joint):
    count = joint.shape[0] // P_SIZE
    part = [pl.BlockSpec((P_SIZE, PAIR), lambda n, p, s=s: (n, s * PAIRS + p)) for s in range(3)]
    return pl.pallas_call(
        attend_kernel,
        grid=(count, PAIRS),
        in_specs=part,
        out_specs=[
            pl.BlockSpec((P_SIZE, PAIR), lambda n, p: (n, p)),
            pl.BlockSpec((1, 2, P_SIZE, P_SIZE), lambda n, p: (n, p, 0, 0)),
        ],
        out_shape=[
            jax.ShapeDtypeStruct((joint.shape[0], D), BF),
            jax.ShapeDtypeStruct((count, H, P_SIZE, P_SIZE), BF),
        ],
        cost_estimate=pl.CostEstimate(
            flops=8 * count * H * P_SIZE * P_SIZE * HD,
            bytes_accessed=2 * count * H * P_SIZE * P_SIZE + 8 * joint.shape[0] * D,
            transcendentals=count * H * P_SIZE * P_SIZE,
        ),
        compiler_params=pltpu.CompilerParams(vmem_limit_bytes=VMEM_BYTES),
        name="attention",
    )(joint, joint, joint)


def attend_back_kernel(q_ref, k_ref, v_ref, probs_ref, grad_ref, out_ref):
    pair = pl.program_id(1)
    queries, value_rows, grad = q_ref[...], v_ref[...], grad_ref[...]
    keys_t = k_ref[...].T
    query_grad = jnp.zeros((PAIR, P_SIZE), F32)
    key_grad = jnp.zeros((P_SIZE, PAIR), F32)
    value_grad = jnp.zeros((P_SIZE, PAIR), F32)
    for which in range(2):
        mask = head_mask(which, 1)
        probs = probs_ref[0, which]
        own_grad = grad * mask
        value_grad = value_grad + dot(probs, own_grad)
        prob_grad = dot_nt(value_rows, own_grad)
        wide = probs.astype(F32)
        total = jnp.sum(wide * prob_grad, axis=0, keepdims=True)
        score_grad = (wide * (prob_grad - total) * HD ** (-0.5)).astype(BF)
        key_grad = key_grad + dot(score_grad, queries * mask)
        query_grad = query_grad + dot(keys_t * head_mask(which, 0), score_grad)
    for part, value in enumerate((query_grad.T, key_grad, value_grad)):
        out_ref[:, pl.ds(pl.multiple_of(part * D + pair * PAIR, PAIR), PAIR)] = value.astype(BF)


def attend_back(joint, probs, grad):
    count = joint.shape[0] // P_SIZE
    part = [pl.BlockSpec((P_SIZE, PAIR), lambda n, p, s=s: (n, s * PAIRS + p)) for s in range(3)]
    return pl.pallas_call(
        attend_back_kernel,
        grid=(count, PAIRS),
        in_specs=part
        + [
            pl.BlockSpec((1, 2, P_SIZE, P_SIZE), lambda n, p: (n, p, 0, 0)),
            pl.BlockSpec((P_SIZE, PAIR), lambda n, p: (n, p)),
        ],
        out_specs=pl.BlockSpec((P_SIZE, QKV), lambda n, p: (n, 0)),
        out_shape=jax.ShapeDtypeStruct(joint.shape, BF),
        cost_estimate=pl.CostEstimate(
            flops=16 * count * H * P_SIZE * P_SIZE * HD,
            bytes_accessed=2 * count * H * P_SIZE * P_SIZE + 14 * joint.shape[0] * D,
            transcendentals=0,
        ),
        compiler_params=pltpu.CompilerParams(vmem_limit_bytes=VMEM_BYTES),
        name="attention_back",
    )(joint, joint, joint, probs, grad)


def square_kernel(class_at, section_ref, named_ref, *refs):
    *parts, out_ref = refs
    images = named_ref.shape[1]
    first_core = section_ref[0] == 0
    total = jnp.zeros((1, 1), F32)
    for index, ref in enumerate(parts):
        value = ref[...]
        squares = jnp.sum(jnp.sum(value * value, axis=0, keepdims=True), axis=1, keepdims=True)
        if index % 3 == 2:
            columns = ref[:, class_at : class_at + images]
            high = columns.astype(BF)
            low = (columns - high.astype(F32)).astype(BF)
            rows = dot_nt(named_ref[...], high) + dot_nt(named_ref[...], low)
            joined = jnp.sum(jnp.sum(rows * rows, axis=0, keepdims=True), axis=1, keepdims=True)
            apart = jnp.sum(jnp.sum(columns * columns, axis=0, keepdims=True), axis=1, keepdims=True)
            squares = squares + jnp.where(first_core, 0.0, joined - apart)
        total = total + squares
    out_ref[...] = jnp.broadcast_to(total, out_ref.shape)


def square_sum(section, named, done, small_width):
    parts = [block[name] for block in done for name in ("down", "up", "first")]
    class_at = parts[2].shape[1] - small_width + P_SIZE
    whole = [pl.BlockSpec(value.shape, lambda j: (0, 0)) for value in [named] + parts]
    return call(
        lambda *refs: square_kernel(class_at, *refs),
        "square_sum",
        0,
        grid=(1,),
        in_specs=[pl.BlockSpec(memory_space=pltpu.SMEM)] + whole,
        out_specs=pl.BlockSpec((8, 128), lambda j: (0, 0)),
        out_shape=shape_of(8, 128),
    )(section[None].astype(jnp.int32), named, *parts)[0, 0]


def adam_kernel(factor_ref, *refs):
    count = len(LEARN_RATES)
    factor = factor_ref[0, 0]
    for index, rate in enumerate(LEARN_RATES):
        weight, moment, square, grad = (ref[...] for ref in refs[4 * index : 4 * index + 4])
        moment_ref, square_ref, weight_ref = refs[4 * count + 3 * index : 4 * count + 3 * index + 3]
        clipped = grad * factor
        moment_next = BETA_ONE * moment + (1 - BETA_ONE) * clipped
        square_next = BETA_TWO * square + (1 - BETA_TWO) * clipped * clipped
        size = jnp.sqrt(square_next * (1.0 / (1 - BETA_TWO**STEP))) + EPS_ADAM
        update = moment_next * (1.0 / (1 - BETA_ONE**STEP)) / size
        moment_ref[...] = moment_next
        square_ref[...] = square_next
        weight_ref[...] = weight - rate * (update + WEIGHT_DECAY * weight)


def adam(factor, states):
    return call(
        adam_kernel,
        "adam",
        0,
        grid=(1,),
        in_specs=[pl.BlockSpec(memory_space=pltpu.SMEM)] + [whole_spec(*value.shape) for state in states for value in state],
        out_specs=[whole_spec(*state[0].shape) for state in states for _ in range(3)],
        out_shape=[shape_of(*state[0].shape) for state in states for _ in range(3)],
    )(factor.reshape(1, 1), *(value for state in states for value in state))


def place_halves(is_first, mine, other):
    return jnp.concatenate(
        [jnp.where(is_first, mine, other), jnp.where(is_first, other, mine)], axis=1
    )


def block_forward(seq, first, mlp_weights, classes, inputs, picks, between=lambda: None):
    own = dot_nt(jnp.concatenate([picks, picks], axis=1), classes)
    hidden, normed_one, joint, norms = seq.compute(begin, inputs, own, first)
    attended, probs = seq.compute(attend, joint)
    middle, normed_two, sums_two = seq.compute(attention_end, attended, first, hidden, norms)
    ups, downs = mlp_weights()
    *actives, slope_one, slope_two = seq.compute(lambda normed: up_halves(normed, *ups), normed_two)
    between()
    final, normed_three, shrink, latent, turned, sums = seq.compute(
        lambda actives, middle: end(actives, downs, middle, norms, first, inputs), actives, middle
    )
    saved = dict(
        first=first, ups=ups, downs=downs, inputs=inputs, hidden=hidden, normed_one=normed_one, joint=joint,
        norms=norms, attended=attended, probs=probs, middle=middle, normed_two=normed_two, actives=actives,
        slopes=(slope_one, slope_two), final=final, normed_three=normed_three, shrink=shrink, latent=latent,
        turned=turned,
    )
    squares = seq.compute(
        lambda one, two: jnp.concatenate(
            [jnp.sum(jnp.concatenate([one[:1], two[:1], one[1:2]], axis=0), axis=1), one[2, :2]]
        ),
        sums,
        sums_two,
    )
    return saved, squares


def block_backward(seq, section, block, saved, picks, latent_grad, coefficient, pieces):
    count = latent_grad.shape[0] // P_SIZE
    first, norms = saved["first"], saved["norms"]

    def launch(name, mine, given):
        if (block, name) == SPLIT:
            pieces[name] = seq.launch(sum_pair(mine, given))
            return
        order = order_from(SCATTER_ORDERS, block, name)
        pieces[name] = seq.launch(scatter_steps(mine, given, order))

    through, flow, low_final, head_grad, sums_three = seq.compute(
        lambda grad: head_back(
            coefficient, block == 1, grad, saved["shrink"], saved["latent"], saved["final"], norms, first, saved["normed_three"]
        ),
        latent_grad,
    )
    launch("down", *seq.compute(down_grads, *saved["actives"], low_final))
    if block == 0:
        seq.turn()
    grad_one, grad_two, *up_grads = seq.compute(
        lambda low: up_back(low, saved["normed_two"], saved["downs"], saved["slopes"]), low_final
    )
    launch("up", *up_grads)
    if block == 1:
        seq.turn()
    wide_middle, low_middle, attended_grad, sums_two = seq.compute(
        lambda one, two: middle_back((one, two), saved["ups"], saved["middle"], norms, flow, first), grad_one, grad_two
    )
    if block == 0:
        seq.turn()
    joint_grad = seq.compute(attend_back, saved["joint"], saved["probs"], attended_grad)
    if block == 1:
        seq.turn()
    low_hidden, input_grad, sums_one = seq.compute(
        lambda grad: input_back(grad, first, saved["hidden"], norms, wide_middle, through), joint_grad
    )
    if block == 0:
        seq.turn()
    places = jnp.tile(jnp.eye(P_SIZE, dtype=BF), (count, 1))
    sources = jnp.concatenate(
        [places, jnp.repeat(picks, P_SIZE, axis=0), saved["inputs"].astype(BF)], axis=1
    )
    sources = jnp.pad(sources, ((0, 0), (0, 128 + -(sources.shape[1] + 128) % 512)))
    launch(
        "first",
        *seq.compute(
            lambda low: first_grads(
                section, saved["normed_one"], saved["attended"], low, joint_grad, low_middle, sources, head_grad,
                (sums_one, sums_two, sums_three),
            ),
            low_hidden,
        ),
    )
    return input_grad


def body(*arguments):
    images, noise_draw, labels, class_drop = arguments[:4]
    weights, moments, squares = arguments[4:12], arguments[12:20], arguments[20:28]
    w_qkv, w_attn, w_up, w_down, w_in, w_head, w_embed, w_norms = (w[0] for w in weights)
    count_dp = lax.axis_size("dp")
    section = lax.axis_index("section")
    is_first = section == 0
    dp_index = lax.axis_index("dp")
    per_chip = images.shape[0]
    per_core = per_chip // 2
    total_images = per_chip * count_dp
    width = w_qkv.shape[0]
    ff_width = w_down.shape[0]
    coefficient = 1.0 / (total_images * P_SIZE * PD * math.log(2.0))
    seq = Sequencer()

    position = jnp.concatenate(two_terms(w_embed[:P_SIZE]), axis=0)
    small = jnp.concatenate(
        [
            position.T,
            w_head.astype(BF),
            jnp.pad(jnp.concatenate(three_terms(w_norms), axis=0), ((0, S_IN - S_NORM - 18), (0, 0))).T,
            jnp.pad(w_in.astype(BF), ((0, S_WIDTH - S_IN - PD), (0, 0))).T,
        ],
        axis=1,
    )
    first = jnp.concatenate([small, w_qkv.astype(BF), w_attn.astype(BF)], axis=1)
    up_units = w_up.astype(BF).reshape(width, count_dp, 2, 2, width).transpose(2, 0, 3, 1, 4).reshape(2, width, FF_HALF)
    down_units = w_down.astype(BF).reshape(2, 2, width, D).transpose(0, 2, 1, 3).reshape(2, width, FF_HALF)
    own_halves = dict(
        up=(up_units[0], up_units[1]),
        down=(down_units[0], down_units[1]),
        first=(first[:, : FIRST_WIDTH // 2], first[:, FIRST_WIDTH // 2 :]),
    )
    nearby = [seq.launch(one_step(labels, "dp", (step << (dp_bits() - 2), ))) for step in range(1, 4)]
    seq.turn()
    seq.turn()
    label_flight = seq.launch(label_steps([labels] + [flight["result"] for flight in nearby]))
    seq.turn()
    starts = [seq.launch(one_step(jnp.where(is_first, right, left), "section")) for left, right in own_halves.values()]
    seq.turn()
    seq.turn()
    parts = ({}, {})
    for (name, (left, right)), start in zip(own_halves.items(), starts):
        taken = start["result"]
        parts[0][name] = jnp.where(is_first, left, taken)
        parts[1][name] = jnp.where(is_first, taken, right)
    flat = jnp.concatenate([parts[1][name] for name in own_halves], axis=1)
    gathered = lax.all_gather(seq.tie(flat), "dp", axis=0, tiled=True)
    flights = {
        name: seq.launch(steps(parts[0][name], order_from(GATHER_ORDERS, 0, name)))
        for name, steps in (("first", weight_steps), ("up", gather_steps), ("down", gather_steps))
    }
    seq.turn()
    all_labels = seq.wait(label_flight)
    named = (jnp.arange(CLS)[:, None] == all_labels[None, :]).astype(BF)
    own_classes = [dot_tn(term, named).astype(BF) for term in two_terms(w_embed[P_SIZE:])]
    class_flight = seq.launch(
        class_steps(jnp.concatenate(own_classes, axis=1), is_first, tuple(range(dp_bits())))
    )
    mine_of = {name: seq.wait(flights[name]) for name in ("up", "down")}
    first_halves = seq.wait(flights["first"])
    later = {name: seq.launch(one_step(mine, "section")) for name, mine in mine_of.items()}
    classes = seq.wait(class_flight)
    seq.turn()
    first = seq.compute(place_halves, is_first, *first_halves)
    classes_of = (classes[:, : 2 * total_images], classes[:, 2 * total_images :])

    start = section * per_core
    own_images = lax.dynamic_slice_in_dim(images, start, per_core, 0)
    own_noise = lax.dynamic_slice_in_dim(noise_draw, start, per_core, 0)
    keep = (1 - lax.dynamic_slice_in_dim(class_drop, start, per_core, 0)).astype(F32)
    inputs = (own_images + NOISE_SCALE * own_noise).reshape(per_core * P_SIZE, PD)

    image_ids = dp_index * per_chip + start + jnp.arange(per_core)
    picks = jnp.where(jnp.arange(total_images)[None, :] == image_ids[:, None], keep[:, None], 0.0).astype(BF)
    swapped = []

    def swap_gathered():
        mine = seq.tie(gathered)
        swapped.append((mine, seq.launch(one_step(mine, "section"))))
        seq.turn()

    def mlp_zero():
        return [[(half, 0) for half in (mine_of[name], seq.wait(later[name]))] for name in ("up", "down")]

    saved_zero, sums_zero = block_forward(seq, first, mlp_zero, classes_of[0], inputs, picks, swap_gathered)
    mine, flight = swapped[0]
    both = (mine, seq.wait(flight))
    first = seq.compute(lambda one, two: place_halves(is_first, one[:, FF:], two[:, FF:]), *both)
    saved_one, sums_one = block_forward(
        seq, first, lambda: [[(half, start) for half in both] for start in (0, STEPS)], classes_of[1], saved_zero["turned"], picks
    )
    loss_local = sums_one[4] + sums_zero[3] + sums_one[3]
    totals = seq.tie(jnp.concatenate([sums_zero[:3], sums_one[:3], loss_local[None], jnp.zeros((1,), F32)]))

    pieces = ({}, {})
    grad_one = block_backward(
        seq, section, 1, saved_one, picks, saved_one["latent"], coefficient, pieces[1]
    )
    seq.turn()
    block_backward(seq, section, 0, saved_zero, picks, grad_one, coefficient, pieces[0])

    small_width = 128 + P_SIZE + PD + total_images
    small_width += -small_width % 512
    while not pieces[0]["first"]["done"]:
        seq.turn()
    both = pieces[0]["first"]["result"]
    half = both[0].shape[1] // 2
    last = [
        seq.launch(
            scatter_both(
                [value[:, part * half : (part + 1) * half] for value in both],
                order_from(SCATTER_ORDERS, 0, ("first", "last")[part]),
            )
        )
        for part in range(2)
    ]
    pieces[0]["first"] = {"done": True, "result": jnp.concatenate(seq.wait(*last), axis=1)}

    done = [{name: seq.wait(pieces[block][name]) for name in ("down", "up", "first")} for block in range(2)]

    done = seq.tie(done)
    square_local = square_sum(section, named, done, small_width)

    own = {}
    for name in ("down", "up", "first"):
        zero, one = done[0][name], done[1][name]
        own[name] = (jnp.where(is_first, zero, one), seq.launch(one_step(jnp.where(is_first, one, zero), "section")))
    totals_flight = seq.launch(sum_steps(jnp.where(jnp.arange(8) == 7, square_local, totals)[None]))
    for name, (kept, flight) in own.items():
        other = seq.wait(flight)
        own[name] = (jnp.where(is_first, kept, other), jnp.where(is_first, other, kept))
    first = jnp.concatenate(own["first"], axis=1)
    small = first[:, QKV + D :]
    rest = small.shape[1] - 128
    class_rows = class_rows_of(named, small[:, P_SIZE : P_SIZE + total_images])
    up_grad = jnp.stack([half.reshape(width, 2, count_dp, width) for half in own["up"]], axis=1)
    up_grad = up_grad.transpose(0, 3, 1, 2, 4)
    down_grad = jnp.stack([half.reshape(width, 2, D).transpose(1, 0, 2) for half in own["down"]])
    shards = (
        first[:, :QKV],
        first[:, QKV : QKV + D],
        up_grad.reshape(width, FF),
        down_grad.reshape(ff_width, D),
        small[:, P_SIZE + total_images : P_SIZE + total_images + PD].T,
        small[:, rest : rest + 2 * PD],
        jnp.concatenate([small[:, :P_SIZE].T, class_rows], axis=0),
        small[:, rest + 2 * PD : rest + 2 * PD + 6].T,
    )
    totals = seq.wait(totals_flight)[0]
    loss_sum = totals[6] + seq.token
    grad_norm = jnp.sqrt(totals[7])
    activity = jnp.sqrt(totals[:6].reshape(2, 3) / (total_images * P_SIZE * D))
    factor = jnp.minimum(1.0, CLIP_NORM / grad_norm)
    new_moments, new_squares, new_weights = ([], [], [])
    for weight, moment, square, shard, rate in zip(weights, moments, squares, shards, LEARN_RATES):
        clipped = shard[None] * factor
        moment_next = BETA_ONE * moment + (1 - BETA_ONE) * clipped
        square_next = BETA_TWO * square + (1 - BETA_TWO) * clipped * clipped
        update = (
            moment_next
            / (1 - BETA_ONE**STEP)
            / (jnp.sqrt(square_next / (1 - BETA_TWO**STEP)) + EPS_ADAM)
        )
        new_moments.append(moment_next)
        new_squares.append(square_next)
        new_weights.append(weight - rate * (update + WEIGHT_DECAY * weight))
    return (*new_moments, *new_squares, *new_weights, loss_sum, grad_norm, activity)


def solution(mesh):
    by_row = P("section", "dp", None)
    by_column = P("section", None, "dp")
    weight_specs = (by_row, by_row, by_row, by_row, by_column, by_row, by_column, by_column)
    return jax.shard_map(
        body,
        mesh=mesh,
        in_specs=(P("dp", None, None), P("dp", None, None), P("dp"), P("dp")) + weight_specs * 3,
        out_specs=weight_specs * 3 + (P(), P(), P()),
        check_vma=False,
    )
```

```python
import math

import jax
import jax.numpy as jnp
from jax import lax
from jax.experimental import pallas as pl
from jax.experimental.pallas import tpu as pltpu
from jax.sharding import PartitionSpec as P

D = 768
H = 12
HD = 64
FF = 3072
PD = 48
CLS = 1000
P_SIZE = 256
STEP = 10
QKV = 3 * D

EPS_NORM = 1e-05
NOISE_SCALE = 0.05
CLIP_NORM = 0.001
BETA_ONE = 0.9
BETA_TWO = 0.95
LEARN_RATES = (0.01, 0.06, 0.01, 0.01, 0.08, 0.01, 0.25, 0.4)
WEIGHT_DECAY = 0.1
EPS_ADAM = 1e-10

BF = jnp.bfloat16
F32 = jnp.float32

S_HEAD = 2 * P_SIZE
S_NORM = S_HEAD + 2 * PD
S_IN = S_HEAD + 128
S_WIDTH = 768
FIRST_WIDTH = S_WIDTH + QKV + D
PAIR = 2 * HD
PAIRS = H // 2
TILE = D
FF_HALF = FF // 2
VMEM_BYTES = 26 << 20


def swap_pairs(count, bit):
    mask = bit[0] if isinstance(bit, tuple) else 1 << bit
    return [(source, source ^ mask) for source in range(count)]


def exchange(value, axis, bit=0):
    return lax.ppermute(value, axis, swap_pairs(lax.axis_size(axis), bit))


def dp_bits():
    return lax.axis_size("dp").bit_length() - 1


def parity_of(bit):
    return (lax.axis_index("dp") >> bit) & 1


GATHER_ORDERS = ({"first": (0, 1, 2, 3), "up": (1, 2, 3, 0), "down": (2, 0, 1, 3)},)
SCATTER_ORDERS = (
    {"down": (0, 2, 1, 3), "up": (1, 0, 2, 3), "first": (0, 1, 2, 3), "last": (1, 2, 0, 3)},
    {"down": (0, 2, 1, 3), "up": (1, 0, 2, 3), "first": (0, 1, 2, 3)},
)


SPLIT = (0, "first")


def order_from(table, block, name):
    count = dp_bits()
    if count == 4:
        return table[block][name]
    first = {"first": 0, "up": 1, "down": 2, "last": 1}[name]
    return tuple((first + step) % count for step in range(count))


class Sequencer:
    def __init__(self):
        self.flights = []
        self.asked = []
        self.token = jnp.zeros((), F32)

    def tie(self, tree):
        leaves, kind = jax.tree.flatten(tree)
        tied = lax.optimization_barrier([self.token] + leaves)
        self.token = tied[0]
        return jax.tree.unflatten(kind, tied[1:])

    def launch(self, steps):
        flight = {"steps": steps, "done": False}
        self.asked.append((flight, next(steps)))
        return flight

    def turn(self):
        requests = []
        for flight, got in zip(self.flights, self.tie([flight["got"] for flight in self.flights])):
            try:
                requests.append((flight, flight["steps"].send(got)))
            except StopIteration as stop:
                flight["done"] = True
                flight["result"] = stop.value
        requests += self.asked
        values = self.tie([value for _, (value, _, _) in requests])
        self.flights, self.asked = [], []
        for value, (flight, (_, axis, bit)) in zip(values, requests):
            flight["got"] = exchange(value, axis, bit)
            self.flights.append(flight)

    def wait(self, *flights):
        while not all(flight["done"] for flight in flights):
            self.turn()
        return flights[0]["result"] if len(flights) == 1 else [f["result"] for f in flights]

    def compute(self, function, *values):
        return self.tie(function(*self.tie(values)))


def gather_steps(part, order):
    have = []
    held = part
    for bit in reversed(order):
        other = yield (held, "dp", bit)
        place = sum(1 for b in have if b > bit)
        swap = parity_of(bit) == 1
        held = jnp.stack([jnp.where(swap, other, held), jnp.where(swap, held, other)], axis=place)
        have.append(bit)
    return held.reshape((-1,) + part.shape[1:])


def weight_steps(part, order):
    mine = yield from gather_steps(part, order)
    other = yield (mine, "section", 0)
    return mine, other


def pair_steps(mine):
    other = yield (mine, "section", 0)
    return mine, other


def part_of(value, axis_index):
    starts = [axis_index.get(axis, 0) for axis in range(value.ndim)]
    sizes = [1 if axis in axis_index else extent for axis, extent in enumerate(value.shape)]
    sliced = lax.dynamic_slice(value, starts, sizes)
    return sliced.reshape([extent for axis, extent in enumerate(sizes) if axis not in axis_index])


def scatter_steps(mine, given, order):
    other = yield (given, "section", 0)
    result = yield from scatter_both((mine, other), order)
    return result


def scatter_both(both, order):
    count = dp_bits()
    rows = both[0].shape[0] >> count
    held = [value.reshape((2,) * count + (rows,) + value.shape[1:]) for value in both]
    left = sorted(range(count), reverse=True)
    chosen = [{} for _ in held]

    def piece(axis, index):
        parts = []
        for value, fixed in zip(held, chosen):
            free = [place for place in range(value.ndim) if place not in fixed]
            parts.append(part_of(value, {**fixed, free[axis]: index}).astype(F32))
        return sum(parts[1:], parts[0])

    for bit in order:
        axis = left.index(bit)
        parity = parity_of(bit)
        other = yield (piece(axis, 1 - parity).astype(BF), "dp", bit)
        for value, fixed in zip(held, chosen):
            free = [place for place in range(value.ndim) if place not in fixed]
            fixed[free[axis]] = parity
        if len(held) > 1:
            kept = sum(part_of(value, fixed).astype(F32) for value, fixed in zip(held, chosen))
            held, chosen = [kept.astype(BF)], [{}]
        held.append(other)
        chosen.append({})
        left.remove(bit)
    return sum(part_of(value, fixed).astype(F32) for value, fixed in zip(held, chosen))


def one_step(value, axis, bit=0):
    got = yield (value, axis, bit)
    return got


def sum_pair(mine, given):
    other = yield (given, "section", 0)
    return mine, other


def label_steps(nearby):
    high = dp_bits() - 2
    own = lax.axis_index("dp") >> high
    rows = [sum(jnp.where((own ^ step) == at, value, 0) for step, value in enumerate(nearby)) for at in range(4)]
    held = jnp.stack(rows)
    for bit in range(high - 1, -1, -1):
        other = yield (held, "dp", bit)
        swap = parity_of(bit) == 1
        place = high - bit
        held = jnp.stack([jnp.where(swap, other, held), jnp.where(swap, held, other)], axis=place)
    return held.reshape(-1)


def class_steps(own, is_first, order):
    other = yield (own, "section", 0)
    both = jnp.concatenate([jnp.where(is_first, own, other), jnp.where(is_first, other, own)], axis=1)
    whole = yield from gather_steps(both, order)
    return whole


def class_rows_of(named, columns):
    return lax.dot_general(
        named.astype(F32), columns, (((1,), (1,)), ((), ())),
        precision=lax.Precision.HIGHEST, preferred_element_type=F32,
    )


def sum_steps(values):
    other = yield (values, "section", 0)
    values = values + other
    for bit in range(dp_bits()):
        other = yield (values, "dp", bit)
        values = values + other
    return values


def dot(left, right):
    return lax.dot_general(left, right, (((1,), (0,)), ((), ())), preferred_element_type=F32)


def dot_nt(left, right):
    return lax.dot_general(left, right, (((1,), (1,)), ((), ())), preferred_element_type=F32)


def dot_tn(left, right):
    return lax.dot_general(left, right, (((0,), (0,)), ((), ())), preferred_element_type=F32)


def two_terms(value):
    high = lax.optimization_barrier(value.astype(BF))
    return high, (value - high.astype(F32)).astype(BF)


def three_terms(value):
    high = lax.optimization_barrier(value.astype(BF))
    return (high,) + two_terms(value - high.astype(F32))


def whole_spec(*shape):
    return pl.BlockSpec(shape, lambda *_: (0,) * len(shape))


def row_spec(width):
    return pl.BlockSpec((P_SIZE, width), lambda j: (j, 0))


def first_spec(index):
    return pl.BlockSpec((D, D), lambda *_: (0, index))


HEAD_SPEC = pl.BlockSpec((D, 128), lambda *_: (0, S_HEAD // 128))
IN_SPEC = pl.BlockSpec((D, 128), lambda *_: (0, S_IN // 128))


def half_spec(part):
    return pl.BlockSpec((D, FF_HALF), lambda *_: (0, part[1] // STEPS))


def shape_of(rows, columns, kind=F32):
    return jax.ShapeDtypeStruct((rows, columns), kind)


def call(kernel, name, flops, **fields):
    return pl.pallas_call(
        kernel,
        name=name,
        cost_estimate=pl.CostEstimate(flops=0, bytes_accessed=0, transcendentals=0),
        compiler_params=pltpu.CompilerParams(vmem_limit_bytes=VMEM_BYTES),
        **fields,
    )


def iotas(rows, columns):
    return (
        lax.broadcasted_iota(jnp.int32, (rows, columns), 0),
        lax.broadcasted_iota(jnp.int32, (rows, columns), 1),
    )


def where_ones(condition):
    return jnp.where(condition, 1.0, 0.0).astype(BF)


def norm_parts(values):
    center = values - jnp.mean(values, axis=-1, keepdims=True)
    scale = lax.rsqrt(jnp.mean(center * center, axis=-1, keepdims=True) + EPS_NORM)
    return center, scale


def norm_rows(values, norms, which):
    center, scale = norm_parts(values)
    return (center * scale * norms[2 * which : 2 * which + 1] + norms[2 * which + 1 : 2 * which + 2]).astype(BF)


def norm_back_rows(values, norms, which, cotangent):
    center, scale = norm_parts(values)
    unit = center * scale
    inner = cotangent * norms[2 * which : 2 * which + 1]
    first = jnp.mean(inner, axis=-1, keepdims=True)
    second = jnp.mean(inner * unit, axis=-1, keepdims=True)
    gain_grad = jnp.sum(cotangent * unit, axis=0, keepdims=True)
    offset_grad = jnp.sum(cotangent, axis=0, keepdims=True)
    return scale * (inner - first - unit * second), gain_grad, offset_grad


def add_sums(sums_ref, *rows):
    @pl.when(pl.program_id(0) == 0)
    def _():
        sums_ref[...] = jnp.zeros_like(sums_ref)

    for index, row in enumerate(rows):
        sums_ref[index : index + 1, :] += row


def reversed_rows(values):
    row, column = iotas(P_SIZE, P_SIZE)
    turn = where_ones(row + column == P_SIZE - 1)
    high = values.astype(BF)
    rest = values - high.astype(F32)
    middle = rest.astype(BF)
    low = (rest - middle.astype(F32)).astype(BF)
    return dot(turn, high) + dot(turn, middle) + dot(turn, low)


def begin_kernel(x_ref, class_ref, small_ref, q_ref, k_ref, v_ref, hidden_ref, normed_ref, joint_ref, norms_ref):
    row, column = iotas(P_SIZE, P_SIZE)
    same = where_ones(row == column)
    hidden = dot_nt(same, small_ref[:, :P_SIZE]) + dot_nt(same, small_ref[:, P_SIZE:S_HEAD])
    hidden = hidden + dot_nt(x_ref[...].astype(BF), small_ref[:, S_IN : S_IN + PD])
    hidden = hidden + class_ref[pl.ds(pl.program_id(0), 1), :]
    row, column = iotas(8, 128)
    place = column - 2 * PD
    term = where_ones((row < 6) & ((place == row) | (place == row + 6) | (place == row + 12)))
    norms = dot_nt(term, small_ref[:, S_HEAD : S_HEAD + 128])
    hidden_ref[...] = hidden
    norms_ref[...] = norms
    normed = norm_rows(hidden, norms, 0)
    normed_ref[...] = normed
    for part, weight_ref in enumerate((q_ref, k_ref, v_ref)):
        joint_ref[:, part * D : (part + 1) * D] = dot(normed, weight_ref[...]).astype(BF)


def begin(inputs, classes, first):
    rows = inputs.shape[0]
    return call(
        begin_kernel,
        "embed_norm_project",
        2 * rows * D * 4 * D,
        grid=(rows // P_SIZE,),
        in_specs=[row_spec(PD), whole_spec(*classes.shape)] + [first_spec(part) for part in range(4)],
        out_specs=[row_spec(D), row_spec(D), row_spec(QKV), whole_spec(8, D)],
        out_shape=[shape_of(rows, D), shape_of(rows, D, BF), shape_of(rows, QKV, BF), shape_of(8, D)],
    )(inputs, classes, first, first, first, first)


def attention_end_kernel(attended_ref, weight_ref, hidden_ref, norms_ref, middle_ref, normed_ref, sums_ref):
    branch = dot(attended_ref[...], weight_ref[...])
    middle = hidden_ref[...] + branch
    middle_ref[...] = middle
    normed_ref[...] = norm_rows(middle, norms_ref[...], 1)
    add_sums(sums_ref, jnp.sum(branch * branch, axis=0, keepdims=True))


def attention_end(attended, first, hidden, norms):
    rows = attended.shape[0]
    return call(
        attention_end_kernel,
        "attention_end",
        2 * rows * D * D,
        grid=(rows // P_SIZE,),
        in_specs=[row_spec(D), first_spec(4), row_spec(D), whole_spec(8, D)],
        out_specs=[row_spec(D), row_spec(D), whole_spec(8, D)],
        out_shape=[shape_of(rows, D), shape_of(rows, D, BF), shape_of(8, D)],
    )(attended, first, hidden, norms)


STEPS = FF_HALF // TILE


def at_one(j):
    return jnp.minimum(j, STEPS - 1)


def at_two(j):
    return jnp.maximum(j - STEPS, 0)


def tile_specs(rows, starts=(0, 0)):
    return [
        pl.BlockSpec((rows, TILE), lambda j: (0, starts[0] + at_one(j))),
        pl.BlockSpec((rows, TILE), lambda j: (0, starts[1] + at_two(j))),
    ]


def up_kernel(x_ref, one_ref, two_ref, active_one, active_two, slope_one, slope_two):
    def half(weight_ref, active_ref, slope_ref):
        u = dot(x_ref[...], weight_ref[...])
        t = pl.reciprocal(1.0 + (0.3275911 / math.sqrt(2.0)) * jnp.abs(u), approx=True)
        bell = jnp.exp(-0.5 * u * u)
        poly = t * (0.127414796 + t * (-0.142248368 + t * (0.7107068705 + t * (-0.7265760135 + t * 0.5307027145))))
        tail = poly * bell
        share = jnp.where(u >= 0, 1.0 - tail, tail)
        active_ref[...] = (u * share).astype(BF)
        slope_ref[...] = (share + u * bell * (1.0 / math.sqrt(2.0 * math.pi))).astype(BF)

    @pl.when(pl.program_id(0) < STEPS)
    def _():
        half(one_ref, active_one, slope_one)

    @pl.when(pl.program_id(0) >= STEPS)
    def _():
        half(two_ref, active_two, slope_two)


def up_halves(normed, one, two):
    rows = normed.shape[0]
    return call(
        up_kernel,
        "up_gelu",
        4 * rows * D * FF_HALF,
        grid=(2 * STEPS,),
        in_specs=[whole_spec(rows, D)] + tile_specs(D, (one[1], two[1])),
        out_specs=tile_specs(rows) * 2,
        out_shape=[shape_of(rows, FF_HALF, BF)] * 4,
    )(normed, one[0], two[0])


def end_kernel(
    active_one, active_two, down_one, down_two, middle_ref, norms_ref, head_ref, x_ref,
    final_ref, normed_ref, shrink_ref, latent_ref, turned_ref, sums_ref,
):
    branch = sum(
        dot(active_ref[:, part * D : (part + 1) * D], down_ref[:, part * D : (part + 1) * D])
        for active_ref, down_ref in ((active_one, down_one), (active_two, down_two))
        for part in range(STEPS)
    )
    final = middle_ref[...] + branch
    final_ref[...] = final
    normed = norm_rows(final, norms_ref[...], 2)
    normed_ref[...] = normed
    head_out = dot(normed, head_ref[...])
    row, _ = iotas(P_SIZE, 128)
    moved = jnp.where(row == 0, 0.0, pltpu.roll(head_out, 1, 0))
    log_scale = moved[:, PD : 2 * PD]
    shrink = jnp.exp(-log_scale)
    shrink_ref[...] = shrink
    latent = (x_ref[...] - moved[:, :PD]) * shrink
    latent_ref[...] = latent
    turned_ref[...] = reversed_rows(latent)
    _, lane = iotas(1, D)
    add_sums(
        sums_ref,
        jnp.sum(final * final, axis=0, keepdims=True),
        jnp.sum(branch * branch, axis=0, keepdims=True),
        jnp.where(lane == 0, jnp.sum(log_scale), 0.0) + jnp.where(lane == 1, 0.5 * jnp.sum(latent * latent), 0.0),
    )


def end(actives, downs, middle, norms, first, inputs):
    rows = middle.shape[0]
    return call(
        end_kernel,
        "down_norm_head",
        4 * rows * D * FF_HALF,
        grid=(rows // P_SIZE,),
        in_specs=[row_spec(FF_HALF)] * 2
        + [half_spec(down) for down in downs]
        + [row_spec(D), whole_spec(8, D), HEAD_SPEC, row_spec(PD)],
        out_specs=[row_spec(D), row_spec(D)] + [row_spec(PD)] * 3 + [whole_spec(8, D)],
        out_shape=[shape_of(rows, D), shape_of(rows, D, BF)] + [shape_of(rows, PD)] * 3 + [shape_of(8, D)],
    )(*actives, *(down for down, _ in downs), middle, norms, first, inputs)


def head_back_kernel(
    coefficient, last, latent_grad_ref, shrink_ref, latent_ref, final_ref, norms_ref, head_ref, normed_ref,
    through_ref, flow_ref, low_ref, weight_ref, sums_ref,
):
    latent_grad = coefficient * latent_ref[...] if last else latent_grad_ref[...]
    through = latent_grad * shrink_ref[...]
    through_ref[...] = through
    scale_grad = coefficient - latent_grad * latent_ref[...]
    row, column = iotas(PD, 128)
    placed = dot((-through).astype(BF), where_ones(row == column))
    placed = placed + dot(scale_grad.astype(BF), where_ones(row + PD == column))
    row, _ = iotas(P_SIZE, 128)
    head_grad = jnp.where(row == P_SIZE - 1, 0.0, pltpu.roll(placed, P_SIZE - 1, 0)).astype(BF)
    flow, gain_grad, offset_grad = norm_back_rows(
        final_ref[...], norms_ref[...], 2, dot_nt(head_grad, head_ref[...])
    )
    flow_ref[...] = flow
    low_ref[...] = flow.astype(BF)

    @pl.when(pl.program_id(0) == 0)
    def _():
        weight_ref[...] = jnp.zeros_like(weight_ref)

    weight_ref[...] += dot_tn(normed_ref[...], head_grad)
    add_sums(sums_ref, gain_grad, offset_grad)


def head_back(coefficient, last, latent_grad, shrink, latent, final, norms, first, normed):
    rows = final.shape[0]
    return call(
        lambda *refs: head_back_kernel(coefficient, last, *refs),
        "head_back",
        4 * rows * D * 128,
        grid=(rows // P_SIZE,),
        in_specs=[row_spec(PD)] * 3 + [row_spec(D), whole_spec(8, D), HEAD_SPEC, row_spec(D)],
        out_specs=[row_spec(PD), row_spec(D), row_spec(D), whole_spec(D, 128), whole_spec(8, D)],
        out_shape=[
            shape_of(rows, PD), shape_of(rows, D), shape_of(rows, D, BF), shape_of(D, 128), shape_of(8, D)
        ],
    )(latent_grad, shrink, latent, final, norms, first, normed)


def down_grad_kernel(one_ref, two_ref, low_ref, out_one, out_two):
    @pl.when(pl.program_id(0) < STEPS)
    def _():
        out_one[...] = dot_tn(one_ref[...], low_ref[...]).astype(BF)

    @pl.when(pl.program_id(0) >= STEPS)
    def _():
        out_two[...] = dot_tn(two_ref[...], low_ref[...]).astype(BF)


def down_grads(one, two, low):
    rows = low.shape[0]
    return call(
        down_grad_kernel,
        "down_weight_grad",
        4 * rows * D * FF_HALF,
        grid=(2 * STEPS,),
        in_specs=tile_specs(rows) + [whole_spec(rows, D)],
        out_specs=tile_specs(D),
        out_shape=[shape_of(D, FF_HALF, BF)] * 2,
    )(one, two, low)


def up_back_kernel(low_ref, normed_ref, *refs):
    *refs, turned_ref = refs

    @pl.when(pl.program_id(0) == 0)
    def _():
        turned_ref[...] = normed_ref[...].T

    def half(weight_ref, slope_ref, grad_ref, out_ref):
        grad = (dot_nt(low_ref[...], weight_ref[...]) * slope_ref[...].astype(F32)).astype(BF)
        grad_ref[...] = grad
        out_ref[...] = dot(turned_ref[...], grad).astype(BF)

    @pl.when(pl.program_id(0) < STEPS)
    def _():
        half(*refs[0::2])

    @pl.when(pl.program_id(0) >= STEPS)
    def _():
        half(*refs[1::2])


def up_back(low, normed, downs, slopes):
    rows = low.shape[0]
    return call(
        up_back_kernel,
        "up_back",
        8 * rows * D * FF_HALF,
        grid=(2 * STEPS,),
        in_specs=[whole_spec(rows, D)] * 2 + tile_specs(D, [start for _, start in downs]) + tile_specs(rows),
        out_specs=tile_specs(rows) + tile_specs(D),
        out_shape=[shape_of(rows, FF_HALF, BF)] * 2 + [shape_of(D, FF_HALF, BF)] * 2,
        scratch_shapes=[pltpu.VMEM((D, rows), BF)],
    )(low, normed, *(down for down, _ in downs), *slopes)


def middle_back_kernel(
    one_ref, two_ref, up_one, up_two, middle_ref, norms_ref, above_ref, weight_ref,
    wide_ref, low_ref, attended_ref, sums_ref,
):
    back = dot_nt(one_ref[...], up_one[...]) + dot_nt(two_ref[...], up_two[...])
    flow, gain_grad, offset_grad = norm_back_rows(middle_ref[...], norms_ref[...], 1, back)
    total = above_ref[...] + flow
    wide_ref[...] = total
    low = total.astype(BF)
    low_ref[...] = low
    attended_ref[...] = dot_nt(low, weight_ref[...]).astype(BF)
    add_sums(sums_ref, gain_grad, offset_grad)


def middle_back(grads, ups, middle, norms, above, first):
    rows = middle.shape[0]
    return call(
        middle_back_kernel,
        "middle_back",
        4 * rows * D * FF_HALF,
        grid=(rows // P_SIZE,),
        in_specs=[row_spec(FF_HALF)] * 2
        + [half_spec(up) for up in ups]
        + [row_spec(D), whole_spec(8, D), row_spec(D), first_spec(4)],
        out_specs=[row_spec(D), row_spec(D), row_spec(D), whole_spec(8, D)],
        out_shape=[shape_of(rows, D), shape_of(rows, D, BF), shape_of(rows, D, BF), shape_of(8, D)],
    )(*grads, *(up for up, _ in ups), middle, norms, above, first)


def input_back_kernel(
    joint_ref, q_ref, k_ref, v_ref, hidden_ref, norms_ref, above_ref, in_ref, through_ref, low_ref, out_ref, sums_ref
):
    back = sum(
        dot_nt(joint_ref[:, part * D : (part + 1) * D], weight_ref[...])
        for part, weight_ref in enumerate((q_ref, k_ref, v_ref))
    )
    flow, gain_grad, offset_grad = norm_back_rows(hidden_ref[...], norms_ref[...], 0, back)
    low = (above_ref[...] + flow).astype(BF)
    low_ref[...] = low
    out_ref[...] = reversed_rows(through_ref[...] + dot(low, in_ref[...])[:, :PD])
    add_sums(sums_ref, gain_grad, offset_grad)


def input_back(joint_grad, first, hidden, norms, above, through):
    rows = hidden.shape[0]
    return call(
        input_back_kernel,
        "input_back",
        2 * rows * D * QKV,
        grid=(rows // P_SIZE,),
        in_specs=[row_spec(QKV)]
        + [first_spec(part) for part in range(1, 4)]
        + [row_spec(D), whole_spec(8, D), row_spec(D), IN_SPEC, row_spec(PD)],
        out_specs=[row_spec(D), row_spec(PD), whole_spec(8, D)],
        out_shape=[shape_of(rows, D, BF), shape_of(rows, PD), shape_of(8, D)],
    )(joint_grad, first, first, first, hidden, norms, above, first, through)


COLUMNS = 256
SOURCE_AT = (QKV + D) // COLUMNS


def first_grad_kernel(
    steps, section_ref, normed_ref, attended_ref, low_ref, joint_ref, middle_ref, source_ref, head_ref,
    sums_one, sums_two, sums_three, mine_ref, given_ref, turned_ref,
):
    step = pl.program_id(0)
    for at, left_ref in ((0, normed_ref), (QKV // COLUMNS, attended_ref), (SOURCE_AT, low_ref)):

        @pl.when(step == at)
        def _(left_ref=left_ref):
            turned_ref[...] = left_ref[...].T

    to_mine = (step >= steps // 2) == (section_ref[0] == 1)

    def put(value):
        @pl.when(to_mine)
        def _():
            mine_ref[...] = value

        @pl.when(jnp.logical_not(to_mine))
        def _():
            given_ref[...] = value

    @pl.when(step < QKV // COLUMNS)
    def _():
        put(dot(turned_ref[...], joint_ref[...]).astype(BF))

    @pl.when((step >= QKV // COLUMNS) & (step < SOURCE_AT))
    def _():
        put(dot(turned_ref[...], middle_ref[...]).astype(BF))

    @pl.when((step >= SOURCE_AT) & (step < steps - 1))
    def _():
        put(dot(turned_ref[...], source_ref[...]).astype(BF))

    @pl.when(step == steps - 1)
    def _():
        row, column = iotas(8, 128)
        rest = head_ref[...]
        for which, sums_ref in enumerate((sums_one, sums_two, sums_three)):
            place = where_ones((row < 2) & (column == row + 2 * PD + 2 * which))
            rest = rest + dot_tn(sums_ref[...].astype(BF), place)
        source = dot(turned_ref[...], source_ref[:, :128])
        put(jnp.concatenate([source, rest], axis=1).astype(BF))


def first_grads(section, normed, attended, low, joint_grad, low_middle, sources, head, sums):
    rows = normed.shape[0]
    steps = SOURCE_AT + sources.shape[1] // COLUMNS
    half = steps // 2

    def tile(offset, count):
        return pl.BlockSpec((rows, COLUMNS), lambda j, s: (0, jnp.clip(j - offset, 0, count - 1)))

    whole = pl.BlockSpec((rows, D), lambda j, s: (0, 0))
    small = pl.BlockSpec((8, D), lambda j, s: (0, 0))
    return call(
        lambda *refs: first_grad_kernel(steps, *refs),
        "first_weight_grad",
        2 * rows * D * (QKV + D + sources.shape[1]),
        grid_spec=pltpu.PrefetchScalarGridSpec(
            num_scalar_prefetch=1,
            grid=(steps,),
            in_specs=[
                whole,
                whole,
                whole,
                tile(0, QKV // COLUMNS),
                tile(QKV // COLUMNS, D // COLUMNS),
                tile(SOURCE_AT, sources.shape[1] // COLUMNS),
                pl.BlockSpec((D, 128), lambda j, s: (0, 0)),
                small,
                small,
                small,
            ],
            out_specs=[
                pl.BlockSpec((D, COLUMNS), lambda j, s: (0, jnp.clip(j - half * s[0], 0, half - 1))),
                pl.BlockSpec((D, COLUMNS), lambda j, s: (0, jnp.clip(j - half * (1 - s[0]), 0, half - 1))),
            ],
            scratch_shapes=[pltpu.VMEM((D, rows), BF)],
        ),
        out_shape=[shape_of(D, half * COLUMNS, BF)] * 2,
    )(section[None].astype(jnp.int32), normed, attended, low, joint_grad, low_middle, sources, head, *sums)


def head_mask(which, axis, scale=1.0):
    shape = (1, PAIR) if axis == 1 else (PAIR, 1)
    place = lax.broadcasted_iota(jnp.int32, shape, axis)
    return jnp.where((place >= HD * which) & (place < HD * (which + 1)), scale, 0.0).astype(BF)


def attend_kernel(q_ref, k_ref, v_ref, out_ref, probs_ref):
    queries, key_rows = q_ref[...], k_ref[...]
    values_t = v_ref[...].T
    key_at = lax.broadcasted_iota(jnp.int32, (P_SIZE, P_SIZE), 0)
    query_at = lax.broadcasted_iota(jnp.int32, (P_SIZE, P_SIZE), 1)
    causal = key_at <= query_at
    total = jnp.zeros((PAIR, P_SIZE), F32)
    for which in range(2):
        scores = dot_nt(key_rows, queries * head_mask(which, 1, HD ** (-0.5)))
        scores = jnp.where(causal, scores, -1e30)
        exps = jnp.exp(scores - jnp.max(scores, axis=0, keepdims=True))
        probs = (exps * (1.0 / jnp.sum(exps, axis=0, keepdims=True))).astype(BF)
        probs_ref[0, which] = probs
        total = total + dot(values_t * head_mask(which, 0), probs)
    out_ref[...] = total.T.astype(BF)


def attend(joint):
    count = joint.shape[0] // P_SIZE
    part = [pl.BlockSpec((P_SIZE, PAIR), lambda n, p, s=s: (n, s * PAIRS + p)) for s in range(3)]
    return pl.pallas_call(
        attend_kernel,
        grid=(count, PAIRS),
        in_specs=part,
        out_specs=[
            pl.BlockSpec((P_SIZE, PAIR), lambda n, p: (n, p)),
            pl.BlockSpec((1, 2, P_SIZE, P_SIZE), lambda n, p: (n, p, 0, 0)),
        ],
        out_shape=[
            jax.ShapeDtypeStruct((joint.shape[0], D), BF),
            jax.ShapeDtypeStruct((count, H, P_SIZE, P_SIZE), BF),
        ],
        cost_estimate=pl.CostEstimate(flops=0, bytes_accessed=0, transcendentals=0),
        compiler_params=pltpu.CompilerParams(vmem_limit_bytes=VMEM_BYTES),
        name="attention",
    )(joint, joint, joint)


def attend_back_kernel(q_ref, k_ref, v_ref, probs_ref, grad_ref, out_ref):
    pair = pl.program_id(1)
    queries, value_rows, grad = q_ref[...], v_ref[...], grad_ref[...]
    keys_t = k_ref[...].T
    query_grad = jnp.zeros((PAIR, P_SIZE), F32)
    key_grad = jnp.zeros((P_SIZE, PAIR), F32)
    value_grad = jnp.zeros((P_SIZE, PAIR), F32)
    for which in range(2):
        mask = head_mask(which, 1)
        probs = probs_ref[0, which]
        own_grad = grad * mask
        value_grad = value_grad + dot(probs, own_grad)
        prob_grad = dot_nt(value_rows, own_grad)
        wide = probs.astype(F32)
        total = jnp.sum(wide * prob_grad, axis=0, keepdims=True)
        score_grad = (wide * (prob_grad - total) * HD ** (-0.5)).astype(BF)
        key_grad = key_grad + dot(score_grad, queries * mask)
        query_grad = query_grad + dot(keys_t * head_mask(which, 0), score_grad)
    for part, value in enumerate((query_grad.T, key_grad, value_grad)):
        out_ref[:, pl.ds(pl.multiple_of(part * D + pair * PAIR, PAIR), PAIR)] = value.astype(BF)


def attend_back(joint, probs, grad):
    count = joint.shape[0] // P_SIZE
    part = [pl.BlockSpec((P_SIZE, PAIR), lambda n, p, s=s: (n, s * PAIRS + p)) for s in range(3)]
    return pl.pallas_call(
        attend_back_kernel,
        grid=(count, PAIRS),
        in_specs=part
        + [
            pl.BlockSpec((1, 2, P_SIZE, P_SIZE), lambda n, p: (n, p, 0, 0)),
            pl.BlockSpec((P_SIZE, PAIR), lambda n, p: (n, p)),
        ],
        out_specs=pl.BlockSpec((P_SIZE, QKV), lambda n, p: (n, 0)),
        out_shape=jax.ShapeDtypeStruct(joint.shape, BF),
        cost_estimate=pl.CostEstimate(flops=0, bytes_accessed=0, transcendentals=0),
        compiler_params=pltpu.CompilerParams(vmem_limit_bytes=VMEM_BYTES),
        name="attention_back",
    )(joint, joint, joint, probs, grad)


def square_kernel(class_at, section_ref, named_ref, *refs):
    *parts, out_ref = refs
    images = named_ref.shape[1]
    first_core = section_ref[0] == 0
    total = jnp.zeros((1, 1), F32)
    for index, ref in enumerate(parts):
        value = ref[...]
        squares = jnp.sum(jnp.sum(value * value, axis=0, keepdims=True), axis=1, keepdims=True)
        if index % 3 == 2:
            columns = ref[:, class_at : class_at + images]
            high = columns.astype(BF)
            low = (columns - high.astype(F32)).astype(BF)
            rows = dot_nt(named_ref[...], high) + dot_nt(named_ref[...], low)
            joined = jnp.sum(jnp.sum(rows * rows, axis=0, keepdims=True), axis=1, keepdims=True)
            apart = jnp.sum(jnp.sum(columns * columns, axis=0, keepdims=True), axis=1, keepdims=True)
            squares = squares + jnp.where(first_core, 0.0, joined - apart)
        total = total + squares
    out_ref[...] = jnp.broadcast_to(total, out_ref.shape)


def square_sum(section, named, done, small_width):
    parts = [block[name] for block in done for name in ("down", "up", "first")]
    class_at = parts[2].shape[1] - small_width + P_SIZE
    whole = [pl.BlockSpec(value.shape, lambda j: (0, 0)) for value in [named] + parts]
    return call(
        lambda *refs: square_kernel(class_at, *refs),
        "square_sum",
        0,
        grid=(1,),
        in_specs=[pl.BlockSpec(memory_space=pltpu.SMEM)] + whole,
        out_specs=pl.BlockSpec((8, 128), lambda j: (0, 0)),
        out_shape=shape_of(8, 128),
    )(section[None].astype(jnp.int32), named, *parts)[0, 0]


def adam_kernel(factor_ref, *refs):
    count = len(LEARN_RATES)
    factor = factor_ref[0, 0]
    for index, rate in enumerate(LEARN_RATES):
        weight, moment, square, grad = (ref[...] for ref in refs[4 * index : 4 * index + 4])
        moment_ref, square_ref, weight_ref = refs[4 * count + 3 * index : 4 * count + 3 * index + 3]
        clipped = grad * factor
        moment_next = BETA_ONE * moment + (1 - BETA_ONE) * clipped
        square_next = BETA_TWO * square + (1 - BETA_TWO) * clipped * clipped
        size = jnp.sqrt(square_next * (1.0 / (1 - BETA_TWO**STEP))) + EPS_ADAM
        update = moment_next * (1.0 / (1 - BETA_ONE**STEP)) / size
        moment_ref[...] = moment_next
        square_ref[...] = square_next
        weight_ref[...] = weight - rate * (update + WEIGHT_DECAY * weight)


def adam(factor, states):
    return call(
        adam_kernel,
        "adam",
        0,
        grid=(1,),
        in_specs=[pl.BlockSpec(memory_space=pltpu.SMEM)] + [whole_spec(*value.shape) for state in states for value in state],
        out_specs=[whole_spec(*state[0].shape) for state in states for _ in range(3)],
        out_shape=[shape_of(*state[0].shape) for state in states for _ in range(3)],
    )(factor.reshape(1, 1), *(value for state in states for value in state))


def place_halves(is_first, mine, other):
    return jnp.concatenate(
        [jnp.where(is_first, mine, other), jnp.where(is_first, other, mine)], axis=1
    )


def block_forward(seq, first, mlp_weights, classes, inputs, picks, between=lambda: None):
    own = dot_nt(jnp.concatenate([picks, picks], axis=1), classes)
    hidden, normed_one, joint, norms = seq.compute(begin, inputs, own, first)
    attended, probs = seq.compute(attend, joint)
    middle, normed_two, sums_two = seq.compute(attention_end, attended, first, hidden, norms)
    ups, downs = mlp_weights()
    *actives, slope_one, slope_two = seq.compute(lambda normed: up_halves(normed, *ups), normed_two)
    between()
    final, normed_three, shrink, latent, turned, sums = seq.compute(
        lambda actives, middle: end(actives, downs, middle, norms, first, inputs), actives, middle
    )
    saved = dict(
        first=first, ups=ups, downs=downs, inputs=inputs, hidden=hidden, normed_one=normed_one, joint=joint,
        norms=norms, attended=attended, probs=probs, middle=middle, normed_two=normed_two, actives=actives,
        slopes=(slope_one, slope_two), final=final, normed_three=normed_three, shrink=shrink, latent=latent,
        turned=turned,
    )
    squares = seq.compute(
        lambda one, two: jnp.concatenate(
            [jnp.sum(jnp.concatenate([one[:1], two[:1], one[1:2]], axis=0), axis=1), one[2, :2]]
        ),
        sums,
        sums_two,
    )
    return saved, squares


def block_backward(seq, section, block, saved, picks, latent_grad, coefficient, pieces):
    count = latent_grad.shape[0] // P_SIZE
    first, norms = saved["first"], saved["norms"]

    def launch(name, mine, given):
        if (block, name) == SPLIT:
            pieces[name] = seq.launch(sum_pair(mine, given))
            return
        order = order_from(SCATTER_ORDERS, block, name)
        pieces[name] = seq.launch(scatter_steps(mine, given, order))

    through, flow, low_final, head_grad, sums_three = seq.compute(
        lambda grad: head_back(
            coefficient, block == 1, grad, saved["shrink"], saved["latent"], saved["final"], norms, first, saved["normed_three"]
        ),
        latent_grad,
    )
    launch("down", *seq.compute(down_grads, *saved["actives"], low_final))
    if block == 0:
        seq.turn()
    grad_one, grad_two, *up_grads = seq.compute(
        lambda low: up_back(low, saved["normed_two"], saved["downs"], saved["slopes"]), low_final
    )
    launch("up", *up_grads)
    if block == 1:
        seq.turn()
    wide_middle, low_middle, attended_grad, sums_two = seq.compute(
        lambda one, two: middle_back((one, two), saved["ups"], saved["middle"], norms, flow, first), grad_one, grad_two
    )
    if block == 0:
        seq.turn()
    joint_grad = seq.compute(attend_back, saved["joint"], saved["probs"], attended_grad)
    if block == 1:
        seq.turn()
    low_hidden, input_grad, sums_one = seq.compute(
        lambda grad: input_back(grad, first, saved["hidden"], norms, wide_middle, through), joint_grad
    )
    if block == 0:
        seq.turn()
    places = jnp.tile(jnp.eye(P_SIZE, dtype=BF), (count, 1))
    sources = jnp.concatenate(
        [places, jnp.repeat(picks, P_SIZE, axis=0), saved["inputs"].astype(BF)], axis=1
    )
    sources = jnp.pad(sources, ((0, 0), (0, 128 + -(sources.shape[1] + 128) % 512)))
    launch(
        "first",
        *seq.compute(
            lambda low: first_grads(
                section, saved["normed_one"], saved["attended"], low, joint_grad, low_middle, sources, head_grad,
                (sums_one, sums_two, sums_three),
            ),
            low_hidden,
        ),
    )
    return input_grad


def body(*arguments):
    images, noise_draw, labels, class_drop = arguments[:4]
    weights, moments, squares = arguments[4:12], arguments[12:20], arguments[20:28]
    w_qkv, w_attn, w_up, w_down, w_in, w_head, w_embed, w_norms = (w[0] for w in weights)
    count_dp = lax.axis_size("dp")
    section = lax.axis_index("section")
    is_first = section == 0
    dp_index = lax.axis_index("dp")
    per_chip = images.shape[0]
    per_core = per_chip // 2
    total_images = per_chip * count_dp
    width = w_qkv.shape[0]
    ff_width = w_down.shape[0]
    coefficient = 1.0 / (total_images * P_SIZE * PD * math.log(2.0))
    seq = Sequencer()

    position = jnp.concatenate(two_terms(w_embed[:P_SIZE]), axis=0)
    small = jnp.concatenate(
        [
            position.T,
            w_head.astype(BF),
            jnp.pad(jnp.concatenate(three_terms(w_norms), axis=0), ((0, S_IN - S_NORM - 18), (0, 0))).T,
            jnp.pad(w_in.astype(BF), ((0, S_WIDTH - S_IN - PD), (0, 0))).T,
        ],
        axis=1,
    )
    first = jnp.concatenate([small, w_qkv.astype(BF), w_attn.astype(BF)], axis=1)
    up_units = w_up.astype(BF).reshape(width, count_dp, 2, 2, width).transpose(2, 0, 3, 1, 4).reshape(2, width, FF_HALF)
    down_units = w_down.astype(BF).reshape(2, 2, width, D).transpose(0, 2, 1, 3).reshape(2, width, FF_HALF)
    own_halves = dict(
        up=(up_units[0], up_units[1]),
        down=(down_units[0], down_units[1]),
        first=(first[:, : FIRST_WIDTH // 2], first[:, FIRST_WIDTH // 2 :]),
    )
    nearby = [seq.launch(one_step(labels, "dp", (step << (dp_bits() - 2), ))) for step in range(1, 4)]
    seq.turn()
    seq.turn()
    label_flight = seq.launch(label_steps([labels] + [flight["result"] for flight in nearby]))
    seq.turn()
    starts = [seq.launch(one_step(jnp.where(is_first, right, left), "section")) for left, right in own_halves.values()]
    seq.turn()
    seq.turn()
    parts = ({}, {})
    for (name, (left, right)), start in zip(own_halves.items(), starts):
        taken = start["result"]
        parts[0][name] = jnp.where(is_first, left, taken)
        parts[1][name] = jnp.where(is_first, taken, right)
    flat = jnp.concatenate([parts[1][name] for name in own_halves], axis=1)
    gathered = lax.all_gather(seq.tie(flat), "dp", axis=0, tiled=True)
    flights = {
        name: seq.launch(steps(parts[0][name], order_from(GATHER_ORDERS, 0, name)))
        for name, steps in (("first", weight_steps), ("up", gather_steps), ("down", gather_steps))
    }
    seq.turn()
    all_labels = seq.wait(label_flight)
    named = (jnp.arange(CLS)[:, None] == all_labels[None, :]).astype(BF)
    own_classes = [dot_tn(term, named).astype(BF) for term in two_terms(w_embed[P_SIZE:])]
    class_flight = seq.launch(
        class_steps(jnp.concatenate(own_classes, axis=1), is_first, tuple(range(dp_bits())))
    )
    mine_of = {name: seq.wait(flights[name]) for name in ("up", "down")}
    first_halves = seq.wait(flights["first"])
    later = {name: seq.launch(one_step(mine, "section")) for name, mine in mine_of.items()}
    classes = seq.wait(class_flight)
    first = seq.compute(place_halves, is_first, *first_halves)
    classes_of = (classes[:, : 2 * total_images], classes[:, 2 * total_images :])

    start = section * per_core
    own_images = lax.dynamic_slice_in_dim(images, start, per_core, 0)
    own_noise = lax.dynamic_slice_in_dim(noise_draw, start, per_core, 0)
    keep = (1 - lax.dynamic_slice_in_dim(class_drop, start, per_core, 0)).astype(F32)
    inputs = (own_images + NOISE_SCALE * own_noise).reshape(per_core * P_SIZE, PD)

    image_ids = dp_index * per_chip + start + jnp.arange(per_core)
    picks = jnp.where(jnp.arange(total_images)[None, :] == image_ids[:, None], keep[:, None], 0.0).astype(BF)
    swapped = []

    def swap_gathered():
        mine = seq.tie(gathered)
        swapped.append((mine, seq.launch(one_step(mine, "section"))))
        seq.turn()

    def mlp_zero():
        return [[(half, 0) for half in (mine_of[name], seq.wait(later[name]))] for name in ("up", "down")]

    saved_zero, sums_zero = block_forward(seq, first, mlp_zero, classes_of[0], inputs, picks, swap_gathered)
    mine, flight = swapped[0]
    both = (mine, seq.wait(flight))
    first = seq.compute(lambda one, two: place_halves(is_first, one[:, FF:], two[:, FF:]), *both)
    saved_one, sums_one = block_forward(
        seq, first, lambda: [[(half, start) for half in both] for start in (0, STEPS)], classes_of[1], saved_zero["turned"], picks
    )
    loss_local = sums_one[4] + sums_zero[3] + sums_one[3]
    totals = seq.tie(jnp.concatenate([sums_zero[:3], sums_one[:3], loss_local[None], jnp.zeros((1,), F32)]))

    pieces = ({}, {})
    grad_one = block_backward(
        seq, section, 1, saved_one, picks, saved_one["latent"], coefficient, pieces[1]
    )
    seq.turn()
    block_backward(seq, section, 0, saved_zero, picks, grad_one, coefficient, pieces[0])

    small_width = 128 + P_SIZE + PD + total_images
    small_width += -small_width % 512
    while not pieces[0]["first"]["done"]:
        seq.turn()
    both = pieces[0]["first"]["result"]
    half = both[0].shape[1] // 2
    last = [
        seq.launch(
            scatter_both(
                [value[:, part * half : (part + 1) * half] for value in both],
                order_from(SCATTER_ORDERS, 0, ("first", "last")[part]),
            )
        )
        for part in range(2)
    ]
    pieces[0]["first"] = {"done": True, "result": jnp.concatenate(seq.wait(*last), axis=1)}

    done = [{name: seq.wait(pieces[block][name]) for name in ("down", "up", "first")} for block in range(2)]

    done = seq.tie(done)
    square_local = square_sum(section, named, done, small_width)

    own = {}
    for name in ("down", "up", "first"):
        zero, one = done[0][name], done[1][name]
        own[name] = (jnp.where(is_first, zero, one), seq.launch(one_step(jnp.where(is_first, one, zero), "section")))
    totals_flight = seq.launch(sum_steps(jnp.where(jnp.arange(8) == 7, square_local, totals)[None]))
    for name, (kept, flight) in own.items():
        other = seq.wait(flight)
        own[name] = (jnp.where(is_first, kept, other), jnp.where(is_first, other, kept))
    first = jnp.concatenate(own["first"], axis=1)
    small = first[:, QKV + D :]
    rest = small.shape[1] - 128
    class_rows = class_rows_of(named, small[:, P_SIZE : P_SIZE + total_images])
    up_grad = jnp.stack([half.reshape(width, 2, count_dp, width) for half in own["up"]], axis=1)
    up_grad = up_grad.transpose(0, 3, 1, 2, 4)
    down_grad = jnp.stack([half.reshape(width, 2, D).transpose(1, 0, 2) for half in own["down"]])
    shards = (
        first[:, :QKV],
        first[:, QKV : QKV + D],
        up_grad.reshape(width, FF),
        down_grad.reshape(ff_width, D),
        small[:, P_SIZE + total_images : P_SIZE + total_images + PD].T,
        small[:, rest : rest + 2 * PD],
        jnp.concatenate([small[:, :P_SIZE].T, class_rows], axis=0),
        small[:, rest + 2 * PD : rest + 2 * PD + 6].T,
    )
    totals = seq.wait(totals_flight)[0]
    loss_sum = totals[6] + seq.token
    grad_norm = jnp.sqrt(totals[7])
    activity = jnp.sqrt(totals[:6].reshape(2, 3) / (total_images * P_SIZE * D))
    factor = jnp.minimum(1.0, CLIP_NORM / grad_norm)
    new_moments, new_squares, new_weights = ([], [], [])
    for weight, moment, square, shard, rate in zip(weights, moments, squares, shards, LEARN_RATES):
        clipped = shard[None] * factor
        moment_next = BETA_ONE * moment + (1 - BETA_ONE) * clipped
        square_next = BETA_TWO * square + (1 - BETA_TWO) * clipped * clipped
        update = (
            moment_next
            / (1 - BETA_ONE**STEP)
            / (jnp.sqrt(square_next / (1 - BETA_TWO**STEP)) + EPS_ADAM)
        )
        new_moments.append(moment_next)
        new_squares.append(square_next)
        new_weights.append(weight - rate * (update + WEIGHT_DECAY * weight))
    return (*new_moments, *new_squares, *new_weights, loss_sum, grad_norm, activity)


def solution(mesh):
    by_row = P("section", "dp", None)
    by_column = P("section", None, "dp")
    weight_specs = (by_row, by_row, by_row, by_row, by_column, by_row, by_column, by_column)
    return jax.shard_map(
        body,
        mesh=mesh,
        in_specs=(P("dp", None, None), P("dp", None, None), P("dp"), P("dp")) + weight_specs * 3,
        out_specs=weight_specs * 3 + (P(), P(), P()),
        check_vma=False,
    )
```

```python
import math

import jax
import jax.numpy as jnp
from jax import lax
from jax.experimental import pallas as pl
from jax.experimental.pallas import tpu as pltpu
from jax.sharding import PartitionSpec as P

D = 768
H = 12
HD = 64
FF = 3072
PD = 48
CLS = 1000
P_SIZE = 256
STEP = 10
QKV = 3 * D

EPS_NORM = 1e-05
NOISE_SCALE = 0.05
CLIP_NORM = 0.001
BETA_ONE = 0.9
BETA_TWO = 0.95
LEARN_RATES = (0.01, 0.06, 0.01, 0.01, 0.08, 0.01, 0.25, 0.4)
WEIGHT_DECAY = 0.1
EPS_ADAM = 1e-10

BF = jnp.bfloat16
F32 = jnp.float32

S_HEAD = 2 * P_SIZE
S_NORM = S_HEAD + 2 * PD
S_IN = S_HEAD + 128
S_WIDTH = 768
FIRST_WIDTH = S_WIDTH + QKV + D
PAIR = 2 * HD
PAIRS = H // 2
TILE = D
FF_HALF = FF // 2
VMEM_BYTES = 26 << 20


def swap_pairs(count, bit):
    mask = bit[0] if isinstance(bit, tuple) else 1 << bit
    return [(source, source ^ mask) for source in range(count)]


def exchange(value, axis, bit=0):
    return lax.ppermute(value, axis, swap_pairs(lax.axis_size(axis), bit))


def dp_bits():
    return lax.axis_size("dp").bit_length() - 1


def parity_of(bit):
    return (lax.axis_index("dp") >> bit) & 1


GATHER_ORDERS = ({"first": (0, 1, 2, 3), "up": (1, 2, 3, 0), "down": (2, 0, 1, 3)},)
SCATTER_ORDERS = (
    {"down": (0, 2, 1, 3), "up": (1, 0, 2, 3), "first": (0, 1, 2, 3), "last": (1, 2, 0, 3)},
    {"down": (0, 2, 1, 3), "up": (1, 0, 2, 3), "first": (0, 1, 2, 3)},
)


SPLIT = (0, "first")


def order_from(table, block, name):
    count = dp_bits()
    if count == 4:
        return table[block][name]
    first = {"first": 0, "up": 1, "down": 2, "last": 1}[name]
    return tuple((first + step) % count for step in range(count))


class Sequencer:
    def __init__(self):
        self.flights = []
        self.asked = []
        self.token = jnp.zeros((), F32)

    def tie(self, tree):
        leaves, kind = jax.tree.flatten(tree)
        tied = lax.optimization_barrier([self.token] + leaves)
        self.token = tied[0]
        return jax.tree.unflatten(kind, tied[1:])

    def launch(self, steps):
        flight = {"steps": steps, "done": False}
        self.asked.append((flight, next(steps)))
        return flight

    def turn(self):
        requests = []
        for flight, got in zip(self.flights, self.tie([flight["got"] for flight in self.flights])):
            try:
                requests.append((flight, flight["steps"].send(got)))
            except StopIteration as stop:
                flight["done"] = True
                flight["result"] = stop.value
        requests += self.asked
        values = self.tie([value for _, (value, _, _) in requests])
        self.flights, self.asked = [], []
        for value, (flight, (_, axis, bit)) in zip(values, requests):
            flight["got"] = exchange(value, axis, bit)
            self.flights.append(flight)

    def wait(self, *flights):
        while not all(flight["done"] for flight in flights):
            self.turn()
        return flights[0]["result"] if len(flights) == 1 else [f["result"] for f in flights]

    def compute(self, function, *values):
        return self.tie(function(*self.tie(values)))


def gather_steps(part, order):
    have = []
    held = part
    for bit in reversed(order):
        other = yield (held, "dp", bit)
        place = sum(1 for b in have if b > bit)
        swap = parity_of(bit) == 1
        held = jnp.stack([jnp.where(swap, other, held), jnp.where(swap, held, other)], axis=place)
        have.append(bit)
    return held.reshape((-1,) + part.shape[1:])


def weight_steps(part, order):
    mine = yield from gather_steps(part, order)
    other = yield (mine, "section", 0)
    return mine, other


def pair_steps(mine):
    other = yield (mine, "section", 0)
    return mine, other


def part_of(value, axis_index):
    starts = [axis_index.get(axis, 0) for axis in range(value.ndim)]
    sizes = [1 if axis in axis_index else extent for axis, extent in enumerate(value.shape)]
    sliced = lax.dynamic_slice(value, starts, sizes)
    return sliced.reshape([extent for axis, extent in enumerate(sizes) if axis not in axis_index])


def scatter_steps(mine, given, order):
    other = yield (given, "section", 0)
    result = yield from scatter_both((mine, other), order)
    return result


def scatter_both(both, order):
    count = dp_bits()
    rows = both[0].shape[0] >> count
    held = [value.reshape((2,) * count + (rows,) + value.shape[1:]) for value in both]
    left = sorted(range(count), reverse=True)
    chosen = [{} for _ in held]

    def piece(axis, index):
        parts = []
        for value, fixed in zip(held, chosen):
            free = [place for place in range(value.ndim) if place not in fixed]
            parts.append(part_of(value, {**fixed, free[axis]: index}).astype(F32))
        return sum(parts[1:], parts[0])

    for bit in order:
        axis = left.index(bit)
        parity = parity_of(bit)
        other = yield (piece(axis, 1 - parity).astype(BF), "dp", bit)
        for value, fixed in zip(held, chosen):
            free = [place for place in range(value.ndim) if place not in fixed]
            fixed[free[axis]] = parity
        if len(held) > 1:
            kept = sum(part_of(value, fixed).astype(F32) for value, fixed in zip(held, chosen))
            held, chosen = [kept.astype(BF)], [{}]
        held.append(other)
        chosen.append({})
        left.remove(bit)
    return sum(part_of(value, fixed).astype(F32) for value, fixed in zip(held, chosen))


def one_step(value, axis, bit=0):
    got = yield (value, axis, bit)
    return got


def sum_pair(mine, given):
    other = yield (given, "section", 0)
    return mine, other


def label_steps(nearby):
    high = dp_bits() - 2
    own = lax.axis_index("dp") >> high
    rows = [sum(jnp.where((own ^ step) == at, value, 0) for step, value in enumerate(nearby)) for at in range(4)]
    held = jnp.stack(rows)
    for bit in range(high - 1, -1, -1):
        other = yield (held, "dp", bit)
        swap = parity_of(bit) == 1
        place = high - bit
        held = jnp.stack([jnp.where(swap, other, held), jnp.where(swap, held, other)], axis=place)
    return held.reshape(-1)


def class_steps(own, is_first, order):
    other = yield (own, "section", 0)
    both = jnp.concatenate([jnp.where(is_first, own, other), jnp.where(is_first, other, own)], axis=1)
    whole = yield from gather_steps(both, order)
    return whole


def class_rows_of(named, columns):
    return lax.dot_general(
        named.astype(F32), columns, (((1,), (1,)), ((), ())),
        precision=lax.Precision.HIGHEST, preferred_element_type=F32,
    )


def sum_steps(values):
    other = yield (values, "section", 0)
    values = values + other
    for bit in range(dp_bits()):
        other = yield (values, "dp", bit)
        values = values + other
    return values


def dot(left, right):
    return lax.dot_general(left, right, (((1,), (0,)), ((), ())), preferred_element_type=F32)


def dot_nt(left, right):
    return lax.dot_general(left, right, (((1,), (1,)), ((), ())), preferred_element_type=F32)


def dot_tn(left, right):
    return lax.dot_general(left, right, (((0,), (0,)), ((), ())), preferred_element_type=F32)


def two_terms(value):
    high = lax.optimization_barrier(value.astype(BF))
    return high, (value - high.astype(F32)).astype(BF)


def three_terms(value):
    high = lax.optimization_barrier(value.astype(BF))
    return (high,) + two_terms(value - high.astype(F32))


def whole_spec(*shape):
    return pl.BlockSpec(shape, lambda *_: (0,) * len(shape))


def row_spec(width):
    return pl.BlockSpec((P_SIZE, width), lambda j: (j, 0))


def first_spec(index):
    return pl.BlockSpec((D, D), lambda *_: (0, index))


HEAD_SPEC = pl.BlockSpec((D, 128), lambda *_: (0, S_HEAD // 128))
IN_SPEC = pl.BlockSpec((D, 128), lambda *_: (0, S_IN // 128))


def half_spec(part):
    return pl.BlockSpec((D, FF_HALF), lambda *_: (0, part[1] // STEPS))


def shape_of(rows, columns, kind=F32):
    return jax.ShapeDtypeStruct((rows, columns), kind)


def call(kernel, name, flops, **fields):
    return pl.pallas_call(
        kernel,
        name=name,
        cost_estimate=pl.CostEstimate(flops=0, bytes_accessed=0, transcendentals=0),
        compiler_params=pltpu.CompilerParams(vmem_limit_bytes=VMEM_BYTES),
        **fields,
    )


def iotas(rows, columns):
    return (
        lax.broadcasted_iota(jnp.int32, (rows, columns), 0),
        lax.broadcasted_iota(jnp.int32, (rows, columns), 1),
    )


def where_ones(condition):
    return jnp.where(condition, 1.0, 0.0).astype(BF)


def norm_parts(values):
    center = values - jnp.mean(values, axis=-1, keepdims=True)
    scale = lax.rsqrt(jnp.mean(center * center, axis=-1, keepdims=True) + EPS_NORM)
    return center, scale


def norm_rows(values, norms, which):
    center, scale = norm_parts(values)
    return (center * scale * norms[2 * which : 2 * which + 1] + norms[2 * which + 1 : 2 * which + 2]).astype(BF)


def norm_back_rows(values, norms, which, cotangent):
    center, scale = norm_parts(values)
    unit = center * scale
    inner = cotangent * norms[2 * which : 2 * which + 1]
    first = jnp.mean(inner, axis=-1, keepdims=True)
    second = jnp.mean(inner * unit, axis=-1, keepdims=True)
    gain_grad = jnp.sum(cotangent * unit, axis=0, keepdims=True)
    offset_grad = jnp.sum(cotangent, axis=0, keepdims=True)
    return scale * (inner - first - unit * second), gain_grad, offset_grad


def add_sums(sums_ref, *rows):
    @pl.when(pl.program_id(0) == 0)
    def _():
        sums_ref[...] = jnp.zeros_like(sums_ref)

    for index, row in enumerate(rows):
        sums_ref[index : index + 1, :] += row


def reversed_rows(values):
    row, column = iotas(P_SIZE, P_SIZE)
    turn = where_ones(row + column == P_SIZE - 1)
    high = values.astype(BF)
    rest = values - high.astype(F32)
    middle = rest.astype(BF)
    low = (rest - middle.astype(F32)).astype(BF)
    return dot(turn, high) + dot(turn, middle) + dot(turn, low)


def begin_kernel(x_ref, class_ref, small_ref, q_ref, k_ref, v_ref, hidden_ref, normed_ref, joint_ref, norms_ref):
    row, column = iotas(P_SIZE, P_SIZE)
    same = where_ones(row == column)
    hidden = dot_nt(same, small_ref[:, :P_SIZE]) + dot_nt(same, small_ref[:, P_SIZE:S_HEAD])
    hidden = hidden + dot_nt(x_ref[...].astype(BF), small_ref[:, S_IN : S_IN + PD])
    hidden = hidden + class_ref[pl.ds(pl.program_id(0), 1), :]
    row, column = iotas(8, 128)
    place = column - 2 * PD
    term = where_ones((row < 6) & ((place == row) | (place == row + 6) | (place == row + 12)))
    norms = dot_nt(term, small_ref[:, S_HEAD : S_HEAD + 128])
    hidden_ref[...] = hidden
    norms_ref[...] = norms
    normed = norm_rows(hidden, norms, 0)
    normed_ref[...] = normed
    for part, weight_ref in enumerate((q_ref, k_ref, v_ref)):
        joint_ref[:, part * D : (part + 1) * D] = dot(normed, weight_ref[...]).astype(BF)


def begin(inputs, classes, first):
    rows = inputs.shape[0]
    return call(
        begin_kernel,
        "embed_norm_project",
        2 * rows * D * 4 * D,
        grid=(rows // P_SIZE,),
        in_specs=[row_spec(PD), whole_spec(*classes.shape)] + [first_spec(part) for part in range(4)],
        out_specs=[row_spec(D), row_spec(D), row_spec(QKV), whole_spec(8, D)],
        out_shape=[shape_of(rows, D), shape_of(rows, D, BF), shape_of(rows, QKV, BF), shape_of(8, D)],
    )(inputs, classes, first, first, first, first)


def attention_end_kernel(attended_ref, weight_ref, hidden_ref, norms_ref, middle_ref, normed_ref, sums_ref):
    branch = dot(attended_ref[...], weight_ref[...])
    middle = hidden_ref[...] + branch
    middle_ref[...] = middle
    normed_ref[...] = norm_rows(middle, norms_ref[...], 1)
    add_sums(sums_ref, jnp.sum(branch * branch, axis=0, keepdims=True))


def attention_end(attended, first, hidden, norms):
    rows = attended.shape[0]
    return call(
        attention_end_kernel,
        "attention_end",
        2 * rows * D * D,
        grid=(rows // P_SIZE,),
        in_specs=[row_spec(D), first_spec(4), row_spec(D), whole_spec(8, D)],
        out_specs=[row_spec(D), row_spec(D), whole_spec(8, D)],
        out_shape=[shape_of(rows, D), shape_of(rows, D, BF), shape_of(8, D)],
    )(attended, first, hidden, norms)


STEPS = FF_HALF // TILE


def at_one(j):
    return jnp.minimum(j, STEPS - 1)


def at_two(j):
    return jnp.maximum(j - STEPS, 0)


def tile_specs(rows, starts=(0, 0)):
    return [
        pl.BlockSpec((rows, TILE), lambda j: (0, starts[0] + at_one(j))),
        pl.BlockSpec((rows, TILE), lambda j: (0, starts[1] + at_two(j))),
    ]


def up_kernel(x_ref, one_ref, two_ref, active_one, active_two, slope_one, slope_two):
    def half(weight_ref, active_ref, slope_ref):
        u = dot(x_ref[...], weight_ref[...])
        t = pl.reciprocal(1.0 + (0.3275911 / math.sqrt(2.0)) * jnp.abs(u), approx=True)
        bell = jnp.exp(-0.5 * u * u)
        poly = t * (0.127414796 + t * (-0.142248368 + t * (0.7107068705 + t * (-0.7265760135 + t * 0.5307027145))))
        tail = poly * bell
        share = jnp.where(u >= 0, 1.0 - tail, tail)
        active_ref[...] = (u * share).astype(BF)
        slope_ref[...] = (share + u * bell * (1.0 / math.sqrt(2.0 * math.pi))).astype(BF)

    @pl.when(pl.program_id(0) < STEPS)
    def _():
        half(one_ref, active_one, slope_one)

    @pl.when(pl.program_id(0) >= STEPS)
    def _():
        half(two_ref, active_two, slope_two)


def up_halves(normed, one, two):
    rows = normed.shape[0]
    return call(
        up_kernel,
        "up_gelu",
        4 * rows * D * FF_HALF,
        grid=(2 * STEPS,),
        in_specs=[whole_spec(rows, D)] + tile_specs(D, (one[1], two[1])),
        out_specs=tile_specs(rows) * 2,
        out_shape=[shape_of(rows, FF_HALF, BF)] * 4,
    )(normed, one[0], two[0])


def end_kernel(
    active_one, active_two, down_one, down_two, middle_ref, norms_ref, head_ref, x_ref,
    final_ref, normed_ref, shrink_ref, latent_ref, turned_ref, sums_ref,
):
    branch = sum(
        dot(active_ref[:, part * D : (part + 1) * D], down_ref[:, part * D : (part + 1) * D])
        for active_ref, down_ref in ((active_one, down_one), (active_two, down_two))
        for part in range(STEPS)
    )
    final = middle_ref[...] + branch
    final_ref[...] = final
    normed = norm_rows(final, norms_ref[...], 2)
    normed_ref[...] = normed
    head_out = dot(normed, head_ref[...])
    row, _ = iotas(P_SIZE, 128)
    moved = jnp.where(row == 0, 0.0, pltpu.roll(head_out, 1, 0))
    log_scale = moved[:, PD : 2 * PD]
    shrink = jnp.exp(-log_scale)
    shrink_ref[...] = shrink
    latent = (x_ref[...] - moved[:, :PD]) * shrink
    latent_ref[...] = latent
    turned_ref[...] = reversed_rows(latent)
    _, lane = iotas(1, D)
    add_sums(
        sums_ref,
        jnp.sum(final * final, axis=0, keepdims=True),
        jnp.sum(branch * branch, axis=0, keepdims=True),
        jnp.where(lane == 0, jnp.sum(log_scale), 0.0) + jnp.where(lane == 1, 0.5 * jnp.sum(latent * latent), 0.0),
    )


def end(actives, downs, middle, norms, first, inputs):
    rows = middle.shape[0]
    return call(
        end_kernel,
        "down_norm_head",
        4 * rows * D * FF_HALF,
        grid=(rows // P_SIZE,),
        in_specs=[row_spec(FF_HALF)] * 2
        + [half_spec(down) for down in downs]
        + [row_spec(D), whole_spec(8, D), HEAD_SPEC, row_spec(PD)],
        out_specs=[row_spec(D), row_spec(D)] + [row_spec(PD)] * 3 + [whole_spec(8, D)],
        out_shape=[shape_of(rows, D), shape_of(rows, D, BF)] + [shape_of(rows, PD)] * 3 + [shape_of(8, D)],
    )(*actives, *(down for down, _ in downs), middle, norms, first, inputs)


def head_back_kernel(
    coefficient, last, latent_grad_ref, shrink_ref, latent_ref, final_ref, norms_ref, head_ref, normed_ref,
    through_ref, flow_ref, low_ref, weight_ref, sums_ref,
):
    latent_grad = coefficient * latent_ref[...] if last else latent_grad_ref[...]
    through = latent_grad * shrink_ref[...]
    through_ref[...] = through
    scale_grad = coefficient - latent_grad * latent_ref[...]
    row, column = iotas(PD, 128)
    placed = dot((-through).astype(BF), where_ones(row == column))
    placed = placed + dot(scale_grad.astype(BF), where_ones(row + PD == column))
    row, _ = iotas(P_SIZE, 128)
    head_grad = jnp.where(row == P_SIZE - 1, 0.0, pltpu.roll(placed, P_SIZE - 1, 0)).astype(BF)
    flow, gain_grad, offset_grad = norm_back_rows(
        final_ref[...], norms_ref[...], 2, dot_nt(head_grad, head_ref[...])
    )
    flow_ref[...] = flow
    low_ref[...] = flow.astype(BF)

    @pl.when(pl.program_id(0) == 0)
    def _():
        weight_ref[...] = jnp.zeros_like(weight_ref)

    weight_ref[...] += dot_tn(normed_ref[...], head_grad)
    add_sums(sums_ref, gain_grad, offset_grad)


def head_back(coefficient, last, latent_grad, shrink, latent, final, norms, first, normed):
    rows = final.shape[0]
    return call(
        lambda *refs: head_back_kernel(coefficient, last, *refs),
        "head_back",
        4 * rows * D * 128,
        grid=(rows // P_SIZE,),
        in_specs=[row_spec(PD)] * 3 + [row_spec(D), whole_spec(8, D), HEAD_SPEC, row_spec(D)],
        out_specs=[row_spec(PD), row_spec(D), row_spec(D), whole_spec(D, 128), whole_spec(8, D)],
        out_shape=[
            shape_of(rows, PD), shape_of(rows, D), shape_of(rows, D, BF), shape_of(D, 128), shape_of(8, D)
        ],
    )(latent_grad, shrink, latent, final, norms, first, normed)


def down_grad_kernel(one_ref, two_ref, low_ref, out_one, out_two):
    @pl.when(pl.program_id(0) < STEPS)
    def _():
        out_one[...] = dot_tn(one_ref[...], low_ref[...]).astype(BF)

    @pl.when(pl.program_id(0) >= STEPS)
    def _():
        out_two[...] = dot_tn(two_ref[...], low_ref[...]).astype(BF)


def down_grads(one, two, low):
    rows = low.shape[0]
    return call(
        down_grad_kernel,
        "down_weight_grad",
        4 * rows * D * FF_HALF,
        grid=(2 * STEPS,),
        in_specs=tile_specs(rows) + [whole_spec(rows, D)],
        out_specs=tile_specs(D),
        out_shape=[shape_of(D, FF_HALF, BF)] * 2,
    )(one, two, low)


def up_back_kernel(low_ref, normed_ref, *refs):
    *refs, turned_ref = refs

    @pl.when(pl.program_id(0) == 0)
    def _():
        turned_ref[...] = normed_ref[...].T

    def half(weight_ref, slope_ref, grad_ref, out_ref):
        grad = (dot_nt(low_ref[...], weight_ref[...]) * slope_ref[...].astype(F32)).astype(BF)
        grad_ref[...] = grad
        out_ref[...] = dot(turned_ref[...], grad).astype(BF)

    @pl.when(pl.program_id(0) < STEPS)
    def _():
        half(*refs[0::2])

    @pl.when(pl.program_id(0) >= STEPS)
    def _():
        half(*refs[1::2])


def up_back(low, normed, downs, slopes):
    rows = low.shape[0]
    return call(
        up_back_kernel,
        "up_back",
        8 * rows * D * FF_HALF,
        grid=(2 * STEPS,),
        in_specs=[whole_spec(rows, D)] * 2 + tile_specs(D, [start for _, start in downs]) + tile_specs(rows),
        out_specs=tile_specs(rows) + tile_specs(D),
        out_shape=[shape_of(rows, FF_HALF, BF)] * 2 + [shape_of(D, FF_HALF, BF)] * 2,
        scratch_shapes=[pltpu.VMEM((D, rows), BF)],
    )(low, normed, *(down for down, _ in downs), *slopes)


def middle_back_kernel(
    one_ref, two_ref, up_one, up_two, middle_ref, norms_ref, above_ref, weight_ref,
    wide_ref, low_ref, attended_ref, sums_ref,
):
    back = dot_nt(one_ref[...], up_one[...]) + dot_nt(two_ref[...], up_two[...])
    flow, gain_grad, offset_grad = norm_back_rows(middle_ref[...], norms_ref[...], 1, back)
    total = above_ref[...] + flow
    wide_ref[...] = total
    low = total.astype(BF)
    low_ref[...] = low
    attended_ref[...] = dot_nt(low, weight_ref[...]).astype(BF)
    add_sums(sums_ref, gain_grad, offset_grad)


def middle_back(grads, ups, middle, norms, above, first):
    rows = middle.shape[0]
    return call(
        middle_back_kernel,
        "middle_back",
        4 * rows * D * FF_HALF,
        grid=(rows // P_SIZE,),
        in_specs=[row_spec(FF_HALF)] * 2
        + [half_spec(up) for up in ups]
        + [row_spec(D), whole_spec(8, D), row_spec(D), first_spec(4)],
        out_specs=[row_spec(D), row_spec(D), row_spec(D), whole_spec(8, D)],
        out_shape=[shape_of(rows, D), shape_of(rows, D, BF), shape_of(rows, D, BF), shape_of(8, D)],
    )(*grads, *(up for up, _ in ups), middle, norms, above, first)


def input_back_kernel(
    joint_ref, q_ref, k_ref, v_ref, hidden_ref, norms_ref, above_ref, in_ref, through_ref, low_ref, out_ref, sums_ref
):
    back = sum(
        dot_nt(joint_ref[:, part * D : (part + 1) * D], weight_ref[...])
        for part, weight_ref in enumerate((q_ref, k_ref, v_ref))
    )
    flow, gain_grad, offset_grad = norm_back_rows(hidden_ref[...], norms_ref[...], 0, back)
    low = (above_ref[...] + flow).astype(BF)
    low_ref[...] = low
    out_ref[...] = reversed_rows(through_ref[...] + dot(low, in_ref[...])[:, :PD])
    add_sums(sums_ref, gain_grad, offset_grad)


def input_back(joint_grad, first, hidden, norms, above, through):
    rows = hidden.shape[0]
    return call(
        input_back_kernel,
        "input_back",
        2 * rows * D * QKV,
        grid=(rows // P_SIZE,),
        in_specs=[row_spec(QKV)]
        + [first_spec(part) for part in range(1, 4)]
        + [row_spec(D), whole_spec(8, D), row_spec(D), IN_SPEC, row_spec(PD)],
        out_specs=[row_spec(D), row_spec(PD), whole_spec(8, D)],
        out_shape=[shape_of(rows, D, BF), shape_of(rows, PD), shape_of(8, D)],
    )(joint_grad, first, first, first, hidden, norms, above, first, through)


COLUMNS = 256
SOURCE_AT = (QKV + D) // COLUMNS


def first_grad_kernel(
    steps, section_ref, normed_ref, attended_ref, low_ref, joint_ref, middle_ref, source_ref, head_ref,
    sums_one, sums_two, sums_three, mine_ref, given_ref, turned_ref,
):
    step = pl.program_id(0)
    for at, left_ref in ((0, normed_ref), (QKV // COLUMNS, attended_ref), (SOURCE_AT, low_ref)):

        @pl.when(step == at)
        def _(left_ref=left_ref):
            turned_ref[...] = left_ref[...].T

    to_mine = (step >= steps // 2) == (section_ref[0] == 1)

    def put(value):
        @pl.when(to_mine)
        def _():
            mine_ref[...] = value

        @pl.when(jnp.logical_not(to_mine))
        def _():
            given_ref[...] = value

    @pl.when(step < QKV // COLUMNS)
    def _():
        put(dot(turned_ref[...], joint_ref[...]).astype(BF))

    @pl.when((step >= QKV // COLUMNS) & (step < SOURCE_AT))
    def _():
        put(dot(turned_ref[...], middle_ref[...]).astype(BF))

    @pl.when((step >= SOURCE_AT) & (step < steps - 1))
    def _():
        put(dot(turned_ref[...], source_ref[...]).astype(BF))

    @pl.when(step == steps - 1)
    def _():
        row, column = iotas(8, 128)
        rest = head_ref[...]
        for which, sums_ref in enumerate((sums_one, sums_two, sums_three)):
            place = where_ones((row < 2) & (column == row + 2 * PD + 2 * which))
            rest = rest + dot_tn(sums_ref[...].astype(BF), place)
        source = dot(turned_ref[...], source_ref[:, :128])
        put(jnp.concatenate([source, rest], axis=1).astype(BF))


def first_grads(section, normed, attended, low, joint_grad, low_middle, sources, head, sums):
    rows = normed.shape[0]
    steps = SOURCE_AT + sources.shape[1] // COLUMNS
    half = steps // 2

    def tile(offset, count):
        return pl.BlockSpec((rows, COLUMNS), lambda j, s: (0, jnp.clip(j - offset, 0, count - 1)))

    whole = pl.BlockSpec((rows, D), lambda j, s: (0, 0))
    small = pl.BlockSpec((8, D), lambda j, s: (0, 0))
    return call(
        lambda *refs: first_grad_kernel(steps, *refs),
        "first_weight_grad",
        2 * rows * D * (QKV + D + sources.shape[1]),
        grid_spec=pltpu.PrefetchScalarGridSpec(
            num_scalar_prefetch=1,
            grid=(steps,),
            in_specs=[
                whole,
                whole,
                whole,
                tile(0, QKV // COLUMNS),
                tile(QKV // COLUMNS, D // COLUMNS),
                tile(SOURCE_AT, sources.shape[1] // COLUMNS),
                pl.BlockSpec((D, 128), lambda j, s: (0, 0)),
                small,
                small,
                small,
            ],
            out_specs=[
                pl.BlockSpec((D, COLUMNS), lambda j, s: (0, jnp.clip(j - half * s[0], 0, half - 1))),
                pl.BlockSpec((D, COLUMNS), lambda j, s: (0, jnp.clip(j - half * (1 - s[0]), 0, half - 1))),
            ],
            scratch_shapes=[pltpu.VMEM((D, rows), BF)],
        ),
        out_shape=[shape_of(D, half * COLUMNS, BF)] * 2,
    )(section[None].astype(jnp.int32), normed, attended, low, joint_grad, low_middle, sources, head, *sums)


def head_mask(which, axis, scale=1.0):
    shape = (1, PAIR) if axis == 1 else (PAIR, 1)
    place = lax.broadcasted_iota(jnp.int32, shape, axis)
    return jnp.where((place >= HD * which) & (place < HD * (which + 1)), scale, 0.0).astype(BF)


def attend_kernel(q_ref, k_ref, v_ref, out_ref, probs_ref):
    queries, key_rows = q_ref[...], k_ref[...]
    values_t = v_ref[...].T
    key_at = lax.broadcasted_iota(jnp.int32, (P_SIZE, P_SIZE), 0)
    query_at = lax.broadcasted_iota(jnp.int32, (P_SIZE, P_SIZE), 1)
    causal = key_at <= query_at
    total = jnp.zeros((PAIR, P_SIZE), F32)
    for which in range(2):
        scores = dot_nt(key_rows, queries * head_mask(which, 1, HD ** (-0.5)))
        scores = jnp.where(causal, scores, -1e30)
        exps = jnp.exp(scores - jnp.max(scores, axis=0, keepdims=True))
        probs = (exps * (1.0 / jnp.sum(exps, axis=0, keepdims=True))).astype(BF)
        probs_ref[0, which] = probs
        total = total + dot(values_t * head_mask(which, 0), probs)
    out_ref[...] = total.T.astype(BF)


def attend(joint):
    count = joint.shape[0] // P_SIZE
    part = [pl.BlockSpec((P_SIZE, PAIR), lambda n, p, s=s: (n, s * PAIRS + p)) for s in range(3)]
    return pl.pallas_call(
        attend_kernel,
        grid=(count, PAIRS),
        in_specs=part,
        out_specs=[
            pl.BlockSpec((P_SIZE, PAIR), lambda n, p: (n, p)),
            pl.BlockSpec((1, 2, P_SIZE, P_SIZE), lambda n, p: (n, p, 0, 0)),
        ],
        out_shape=[
            jax.ShapeDtypeStruct((joint.shape[0], D), BF),
            jax.ShapeDtypeStruct((count, H, P_SIZE, P_SIZE), BF),
        ],
        cost_estimate=pl.CostEstimate(flops=0, bytes_accessed=0, transcendentals=0),
        compiler_params=pltpu.CompilerParams(vmem_limit_bytes=VMEM_BYTES),
        name="attention",
    )(joint, joint, joint)


def attend_back_kernel(q_ref, k_ref, v_ref, probs_ref, grad_ref, out_ref):
    pair = pl.program_id(1)
    queries, value_rows, grad = q_ref[...], v_ref[...], grad_ref[...]
    keys_t = k_ref[...].T
    query_grad = jnp.zeros((PAIR, P_SIZE), F32)
    key_grad = jnp.zeros((P_SIZE, PAIR), F32)
    value_grad = jnp.zeros((P_SIZE, PAIR), F32)
    for which in range(2):
        mask = head_mask(which, 1)
        probs = probs_ref[0, which]
        own_grad = grad * mask
        value_grad = value_grad + dot(probs, own_grad)
        prob_grad = dot_nt(value_rows, own_grad)
        wide = probs.astype(F32)
        total = jnp.sum(wide * prob_grad, axis=0, keepdims=True)
        score_grad = (wide * (prob_grad - total) * HD ** (-0.5)).astype(BF)
        key_grad = key_grad + dot(score_grad, queries * mask)
        query_grad = query_grad + dot(keys_t * head_mask(which, 0), score_grad)
    for part, value in enumerate((query_grad.T, key_grad, value_grad)):
        out_ref[:, pl.ds(pl.multiple_of(part * D + pair * PAIR, PAIR), PAIR)] = value.astype(BF)


def attend_back(joint, probs, grad):
    count = joint.shape[0] // P_SIZE
    part = [pl.BlockSpec((P_SIZE, PAIR), lambda n, p, s=s: (n, s * PAIRS + p)) for s in range(3)]
    return pl.pallas_call(
        attend_back_kernel,
        grid=(count, PAIRS),
        in_specs=part
        + [
            pl.BlockSpec((1, 2, P_SIZE, P_SIZE), lambda n, p: (n, p, 0, 0)),
            pl.BlockSpec((P_SIZE, PAIR), lambda n, p: (n, p)),
        ],
        out_specs=pl.BlockSpec((P_SIZE, QKV), lambda n, p: (n, 0)),
        out_shape=jax.ShapeDtypeStruct(joint.shape, BF),
        cost_estimate=pl.CostEstimate(flops=0, bytes_accessed=0, transcendentals=0),
        compiler_params=pltpu.CompilerParams(vmem_limit_bytes=VMEM_BYTES),
        name="attention_back",
    )(joint, joint, joint, probs, grad)


def square_kernel(class_at, section_ref, named_ref, *refs):
    *parts, out_ref = refs
    images = named_ref.shape[1]
    first_core = section_ref[0] == 0
    total = jnp.zeros((1, 1), F32)
    for index, ref in enumerate(parts):
        value = ref[...]
        squares = jnp.sum(jnp.sum(value * value, axis=0, keepdims=True), axis=1, keepdims=True)
        if index % 3 == 2:
            columns = ref[:, class_at : class_at + images]
            high = columns.astype(BF)
            low = (columns - high.astype(F32)).astype(BF)
            rows = dot_nt(named_ref[...], high) + dot_nt(named_ref[...], low)
            joined = jnp.sum(jnp.sum(rows * rows, axis=0, keepdims=True), axis=1, keepdims=True)
            apart = jnp.sum(jnp.sum(columns * columns, axis=0, keepdims=True), axis=1, keepdims=True)
            squares = squares + jnp.where(first_core, 0.0, joined - apart)
        total = total + squares
    out_ref[...] = jnp.broadcast_to(total, out_ref.shape)


def square_sum(section, named, done, small_width):
    parts = [block[name] for block in done for name in ("down", "up", "first")]
    class_at = parts[2].shape[1] - small_width + P_SIZE
    whole = [pl.BlockSpec(value.shape, lambda j: (0, 0)) for value in [named] + parts]
    return call(
        lambda *refs: square_kernel(class_at, *refs),
        "square_sum",
        0,
        grid=(1,),
        in_specs=[pl.BlockSpec(memory_space=pltpu.SMEM)] + whole,
        out_specs=pl.BlockSpec((8, 128), lambda j: (0, 0)),
        out_shape=shape_of(8, 128),
    )(section[None].astype(jnp.int32), named, *parts)[0, 0]


def adam_kernel(factor_ref, *refs):
    count = len(LEARN_RATES)
    factor = factor_ref[0, 0]
    for index, rate in enumerate(LEARN_RATES):
        weight, moment, square, grad = (ref[...] for ref in refs[4 * index : 4 * index + 4])
        moment_ref, square_ref, weight_ref = refs[4 * count + 3 * index : 4 * count + 3 * index + 3]
        clipped = grad * factor
        moment_next = BETA_ONE * moment + (1 - BETA_ONE) * clipped
        square_next = BETA_TWO * square + (1 - BETA_TWO) * clipped * clipped
        size = jnp.sqrt(square_next * (1.0 / (1 - BETA_TWO**STEP))) + EPS_ADAM
        update = moment_next * (1.0 / (1 - BETA_ONE**STEP)) / size
        moment_ref[...] = moment_next
        square_ref[...] = square_next
        weight_ref[...] = weight - rate * (update + WEIGHT_DECAY * weight)


def adam(factor, states):
    return call(
        adam_kernel,
        "adam",
        0,
        grid=(1,),
        in_specs=[pl.BlockSpec(memory_space=pltpu.SMEM)] + [whole_spec(*value.shape) for state in states for value in state],
        out_specs=[whole_spec(*state[0].shape) for state in states for _ in range(3)],
        out_shape=[shape_of(*state[0].shape) for state in states for _ in range(3)],
    )(factor.reshape(1, 1), *(value for state in states for value in state))


def place_halves(is_first, mine, other):
    return jnp.concatenate(
        [jnp.where(is_first, mine, other), jnp.where(is_first, other, mine)], axis=1
    )


def block_forward(seq, first, mlp_weights, classes, inputs, picks, between=lambda: None):
    own = dot_nt(jnp.concatenate([picks, picks], axis=1), classes)
    hidden, normed_one, joint, norms = seq.compute(begin, inputs, own, first)
    attended, probs = seq.compute(attend, joint)
    middle, normed_two, sums_two = seq.compute(attention_end, attended, first, hidden, norms)
    ups, downs = mlp_weights()
    *actives, slope_one, slope_two = seq.compute(lambda normed: up_halves(normed, *ups), normed_two)
    between()
    final, normed_three, shrink, latent, turned, sums = seq.compute(
        lambda actives, middle: end(actives, downs, middle, norms, first, inputs), actives, middle
    )
    saved = dict(
        first=first, ups=ups, downs=downs, inputs=inputs, hidden=hidden, normed_one=normed_one, joint=joint,
        norms=norms, attended=attended, probs=probs, middle=middle, normed_two=normed_two, actives=actives,
        slopes=(slope_one, slope_two), final=final, normed_three=normed_three, shrink=shrink, latent=latent,
        turned=turned,
    )
    squares = seq.compute(
        lambda one, two: jnp.concatenate(
            [jnp.sum(jnp.concatenate([one[:1], two[:1], one[1:2]], axis=0), axis=1), one[2, :2]]
        ),
        sums,
        sums_two,
    )
    return saved, squares


def block_backward(seq, section, block, saved, picks, latent_grad, coefficient, pieces):
    count = latent_grad.shape[0] // P_SIZE
    first, norms = saved["first"], saved["norms"]

    def launch(name, mine, given):
        if (block, name) == SPLIT:
            pieces[name] = seq.launch(sum_pair(mine, given))
            return
        order = order_from(SCATTER_ORDERS, block, name)
        pieces[name] = seq.launch(scatter_steps(mine, given, order))

    through, flow, low_final, head_grad, sums_three = seq.compute(
        lambda grad: head_back(
            coefficient, block == 1, grad, saved["shrink"], saved["latent"], saved["final"], norms, first, saved["normed_three"]
        ),
        latent_grad,
    )
    if block == 0:
        seq.turn()
    launch("down", *seq.compute(down_grads, *saved["actives"], low_final))
    if block == 0:
        seq.turn()
    grad_one, grad_two, *up_grads = seq.compute(
        lambda low: up_back(low, saved["normed_two"], saved["downs"], saved["slopes"]), low_final
    )
    launch("up", *up_grads)
    if block == 1:
        seq.turn()
    wide_middle, low_middle, attended_grad, sums_two = seq.compute(
        lambda one, two: middle_back((one, two), saved["ups"], saved["middle"], norms, flow, first), grad_one, grad_two
    )
    if block == 0:
        seq.turn()
    joint_grad = seq.compute(attend_back, saved["joint"], saved["probs"], attended_grad)
    if block == 1:
        seq.turn()
    low_hidden, input_grad, sums_one = seq.compute(
        lambda grad: input_back(grad, first, saved["hidden"], norms, wide_middle, through), joint_grad
    )
    if block == 0:
        seq.turn()
    places = jnp.tile(jnp.eye(P_SIZE, dtype=BF), (count, 1))
    sources = jnp.concatenate(
        [places, jnp.repeat(picks, P_SIZE, axis=0), saved["inputs"].astype(BF)], axis=1
    )
    sources = jnp.pad(sources, ((0, 0), (0, 128 + -(sources.shape[1] + 128) % 512)))
    launch(
        "first",
        *seq.compute(
            lambda low: first_grads(
                section, saved["normed_one"], saved["attended"], low, joint_grad, low_middle, sources, head_grad,
                (sums_one, sums_two, sums_three),
            ),
            low_hidden,
        ),
    )
    return input_grad


def body(*arguments):
    images, noise_draw, labels, class_drop = arguments[:4]
    weights, moments, squares = arguments[4:12], arguments[12:20], arguments[20:28]
    w_qkv, w_attn, w_up, w_down, w_in, w_head, w_embed, w_norms = (w[0] for w in weights)
    count_dp = lax.axis_size("dp")
    section = lax.axis_index("section")
    is_first = section == 0
    dp_index = lax.axis_index("dp")
    per_chip = images.shape[0]
    per_core = per_chip // 2
    total_images = per_chip * count_dp
    width = w_qkv.shape[0]
    ff_width = w_down.shape[0]
    coefficient = 1.0 / (total_images * P_SIZE * PD * math.log(2.0))
    seq = Sequencer()

    position = jnp.concatenate(two_terms(w_embed[:P_SIZE]), axis=0)
    small = jnp.concatenate(
        [
            position.T,
            w_head.astype(BF),
            jnp.pad(jnp.concatenate(three_terms(w_norms), axis=0), ((0, S_IN - S_NORM - 18), (0, 0))).T,
            jnp.pad(w_in.astype(BF), ((0, S_WIDTH - S_IN - PD), (0, 0))).T,
        ],
        axis=1,
    )
    first = jnp.concatenate([small, w_qkv.astype(BF), w_attn.astype(BF)], axis=1)
    up_units = w_up.astype(BF).reshape(width, count_dp, 2, 2, width).transpose(2, 0, 3, 1, 4).reshape(2, width, FF_HALF)
    down_units = w_down.astype(BF).reshape(2, 2, width, D).transpose(0, 2, 1, 3).reshape(2, width, FF_HALF)
    own_halves = dict(
        up=(up_units[0], up_units[1]),
        down=(down_units[0], down_units[1]),
        first=(first[:, : FIRST_WIDTH // 2], first[:, FIRST_WIDTH // 2 :]),
    )
    nearby = [seq.launch(one_step(labels, "dp", (step << (dp_bits() - 2), ))) for step in range(1, 4)]
    seq.turn()
    seq.turn()
    label_flight = seq.launch(label_steps([labels] + [flight["result"] for flight in nearby]))
    seq.turn()
    starts = [seq.launch(one_step(jnp.where(is_first, right, left), "section")) for left, right in own_halves.values()]
    seq.turn()
    seq.turn()
    parts = ({}, {})
    for (name, (left, right)), start in zip(own_halves.items(), starts):
        taken = start["result"]
        parts[0][name] = jnp.where(is_first, left, taken)
        parts[1][name] = jnp.where(is_first, taken, right)
    flat = jnp.concatenate([parts[1][name] for name in own_halves], axis=1)
    gathered = lax.all_gather(seq.tie(flat), "dp", axis=0, tiled=True)
    flights = {
        name: seq.launch(steps(parts[0][name], order_from(GATHER_ORDERS, 0, name)))
        for name, steps in (("first", weight_steps), ("up", gather_steps), ("down", gather_steps))
    }
    seq.turn()
    all_labels = seq.wait(label_flight)
    named = (jnp.arange(CLS)[:, None] == all_labels[None, :]).astype(BF)
    own_classes = [dot_tn(term, named).astype(BF) for term in two_terms(w_embed[P_SIZE:])]
    class_flight = seq.launch(
        class_steps(jnp.concatenate(own_classes, axis=1), is_first, tuple(range(dp_bits())))
    )
    mine_of = {name: seq.wait(flights[name]) for name in ("up", "down")}
    first_halves = seq.wait(flights["first"])
    later = {name: seq.launch(one_step(mine, "section")) for name, mine in mine_of.items()}
    first = seq.compute(place_halves, is_first, *first_halves)
    classes = seq.wait(class_flight)
    classes_of = (classes[:, : 2 * total_images], classes[:, 2 * total_images :])

    start = section * per_core
    own_images = lax.dynamic_slice_in_dim(images, start, per_core, 0)
    own_noise = lax.dynamic_slice_in_dim(noise_draw, start, per_core, 0)
    keep = (1 - lax.dynamic_slice_in_dim(class_drop, start, per_core, 0)).astype(F32)
    inputs = (own_images + NOISE_SCALE * own_noise).reshape(per_core * P_SIZE, PD)

    image_ids = dp_index * per_chip + start + jnp.arange(per_core)
    picks = jnp.where(jnp.arange(total_images)[None, :] == image_ids[:, None], keep[:, None], 0.0).astype(BF)
    swapped = []

    def swap_gathered():
        mine = seq.tie(gathered)
        swapped.append((mine, seq.launch(one_step(mine, "section"))))
        seq.turn()

    def mlp_zero():
        return [[(half, 0) for half in (mine_of[name], seq.wait(later[name]))] for name in ("up", "down")]

    saved_zero, sums_zero = block_forward(seq, first, mlp_zero, classes_of[0], inputs, picks, swap_gathered)
    mine, flight = swapped[0]
    both = (mine, seq.wait(flight))
    first = seq.compute(lambda one, two: place_halves(is_first, one[:, FF:], two[:, FF:]), *both)
    saved_one, sums_one = block_forward(
        seq, first, lambda: [[(half, start) for half in both] for start in (0, STEPS)], classes_of[1], saved_zero["turned"], picks
    )
    loss_local = sums_one[4] + sums_zero[3] + sums_one[3]
    totals = seq.tie(jnp.concatenate([sums_zero[:3], sums_one[:3], loss_local[None], jnp.zeros((1,), F32)]))

    pieces = ({}, {})
    grad_one = block_backward(
        seq, section, 1, saved_one, picks, saved_one["latent"], coefficient, pieces[1]
    )
    block_backward(seq, section, 0, saved_zero, picks, grad_one, coefficient, pieces[0])

    small_width = 128 + P_SIZE + PD + total_images
    small_width += -small_width % 512
    while not pieces[0]["first"]["done"]:
        seq.turn()
    both = pieces[0]["first"]["result"]
    half = both[0].shape[1] // 2
    last = [
        seq.launch(
            scatter_both(
                [value[:, part * half : (part + 1) * half] for value in both],
                order_from(SCATTER_ORDERS, 0, ("first", "last")[part]),
            )
        )
        for part in range(2)
    ]
    pieces[0]["first"] = {"done": True, "result": jnp.concatenate(seq.wait(*last), axis=1)}

    done = [{name: seq.wait(pieces[block][name]) for name in ("down", "up", "first")} for block in range(2)]

    done = seq.tie(done)
    square_local = square_sum(section, named, done, small_width)

    own = {}
    for name in ("down", "up", "first"):
        zero, one = done[0][name], done[1][name]
        own[name] = (jnp.where(is_first, zero, one), seq.launch(one_step(jnp.where(is_first, one, zero), "section")))
    totals_flight = seq.launch(sum_steps(jnp.where(jnp.arange(8) == 7, square_local, totals)[None]))
    for name, (kept, flight) in own.items():
        other = seq.wait(flight)
        own[name] = (jnp.where(is_first, kept, other), jnp.where(is_first, other, kept))
    first = jnp.concatenate(own["first"], axis=1)
    small = first[:, QKV + D :]
    rest = small.shape[1] - 128
    class_rows = class_rows_of(named, small[:, P_SIZE : P_SIZE + total_images])
    up_grad = jnp.stack([half.reshape(width, 2, count_dp, width) for half in own["up"]], axis=1)
    up_grad = up_grad.transpose(0, 3, 1, 2, 4)
    down_grad = jnp.stack([half.reshape(width, 2, D).transpose(1, 0, 2) for half in own["down"]])
    shards = (
        first[:, :QKV],
        first[:, QKV : QKV + D],
        up_grad.reshape(width, FF),
        down_grad.reshape(ff_width, D),
        small[:, P_SIZE + total_images : P_SIZE + total_images + PD].T,
        small[:, rest : rest + 2 * PD],
        jnp.concatenate([small[:, :P_SIZE].T, class_rows], axis=0),
        small[:, rest + 2 * PD : rest + 2 * PD + 6].T,
    )
    totals = seq.wait(totals_flight)[0]
    loss_sum = totals[6] + seq.token
    grad_norm = jnp.sqrt(totals[7])
    activity = jnp.sqrt(totals[:6].reshape(2, 3) / (total_images * P_SIZE * D))
    factor = jnp.minimum(1.0, CLIP_NORM / grad_norm)
    new_moments, new_squares, new_weights = ([], [], [])
    for weight, moment, square, shard, rate in zip(weights, moments, squares, shards, LEARN_RATES):
        clipped = shard[None] * factor
        moment_next = BETA_ONE * moment + (1 - BETA_ONE) * clipped
        square_next = BETA_TWO * square + (1 - BETA_TWO) * clipped * clipped
        update = (
            moment_next
            / (1 - BETA_ONE**STEP)
            / (jnp.sqrt(square_next / (1 - BETA_TWO**STEP)) + EPS_ADAM)
        )
        new_moments.append(moment_next)
        new_squares.append(square_next)
        new_weights.append(weight - rate * (update + WEIGHT_DECAY * weight))
    return (*new_moments, *new_squares, *new_weights, loss_sum, grad_norm, activity)


def solution(mesh):
    by_row = P("section", "dp", None)
    by_column = P("section", None, "dp")
    weight_specs = (by_row, by_row, by_row, by_row, by_column, by_row, by_column, by_column)
    return jax.shard_map(
        body,
        mesh=mesh,
        in_specs=(P("dp", None, None), P("dp", None, None), P("dp"), P("dp")) + weight_specs * 3,
        out_specs=weight_specs * 3 + (P(), P(), P()),
        check_vma=False,
    )
```
